32 devices in a mesh: dp: 8 (over z, x), fsdp: 4 (over y, core).
Axes of the slice: x: 2, y: 2, z: 4, core: 2. Of those that a mesh axis runs over, the one named last changes fastest.
Arguments:
- inputs: bfloat16 [32768, 768], P(('dp', 'fsdp')), may hold values from -6 to 6
- cotangent: bfloat16 [32768, 768], P(('dp', 'fsdp')), may hold values from -6 to 6
- segment_ids: int32 [32768], P(('dp', 'fsdp')), may hold values from 0 to 7, as said below
- cls_positions: int32 [256], P(('dp', 'fsdp')), may hold values from 0 to 1023, as said below
- doc_flags: int32 [256], replicated, may hold values from 0 to 1, as said below
- positives: int32 [256], P(('dp', 'fsdp')), may hold values from 0 to 255, as said below
- query_weight: bfloat16 [768, 768], P(('dp', 'fsdp')), may hold values from -0.21875 to 0.21875
- query_bias: bfloat16 [768], P(('dp', 'fsdp')), may hold values from -1.5 to 1.5
- key_weight: bfloat16 [768, 768], P(('dp', 'fsdp')), may hold values from -0.21875 to 0.21875
- value_weight: bfloat16 [768, 768], P(('dp', 'fsdp')), may hold values from -0.21875 to 0.21875
- value_bias: bfloat16 [768], P(('dp', 'fsdp')), may hold values from -1.5 to 1.5
- out_weight: bfloat16 [768, 768], P(('dp', 'fsdp')), may hold values from -1.75 to 1.75
- out_bias: bfloat16 [768], P(('dp', 'fsdp')), may hold values from -1.5 to 1.5
- first_gain: bfloat16 [768], P(('dp', 'fsdp')), may hold values from 0.5 to 1.5
- first_shift: bfloat16 [768], P(('dp', 'fsdp')), may hold values from -1.5 to 1.5
- up_weight: bfloat16 [768, 3072], P(('dp', 'fsdp')), may hold values from -0.21875 to 0.21875
- up_bias: bfloat16 [3072], P(('dp', 'fsdp')), may hold values from -1.5 to 1.5
- down_weight: bfloat16 [3072, 768], P(('dp', 'fsdp')), may hold values from -0.109375 to 0.109375
- down_bias: bfloat16 [768], P(('dp', 'fsdp')), may hold values from -1.5 to 1.5
- second_gain: bfloat16 [768], P(('dp', 'fsdp')), may hold values from 0.5 to 1.5
- second_shift: bfloat16 [768], P(('dp', 'fsdp')), may hold values from -1.5 to 1.5
Outputs:
- layer_output: bfloat16 [32768, 768], P(('dp', 'fsdp'))
- embeddings: bfloat16 [256, 768], P(('dp', 'fsdp'))
- scores: float32 [256, 256], P(('dp', 'fsdp'))
- loss: float32 [], replicated
- embedding_grad: float32 [256, 768], P(('dp', 'fsdp'))
- input_grad: float32 [32768, 768], P(('dp', 'fsdp'))
- grad_query_weight: float32 [768, 768], P(('dp', 'fsdp'))
- grad_query_bias: float32 [768], P(('dp', 'fsdp'))
- grad_key_weight: float32 [768, 768], P(('dp', 'fsdp'))
- grad_value_weight: float32 [768, 768], P(('dp', 'fsdp'))
- grad_value_bias: float32 [768], P(('dp', 'fsdp'))
- grad_out_weight: float32 [768, 768], P(('dp', 'fsdp'))
- grad_out_bias: float32 [768], P(('dp', 'fsdp'))
- grad_first_gain: float32 [768], P(('dp', 'fsdp'))
- grad_first_shift: float32 [768], P(('dp', 'fsdp'))
- grad_up_weight: float32 [768, 3072], P(('dp', 'fsdp'))
- grad_up_bias: float32 [3072], P(('dp', 'fsdp'))
- grad_down_weight: float32 [3072, 768], P(('dp', 'fsdp'))
- grad_down_bias: float32 [768], P(('dp', 'fsdp'))
- grad_second_gain: float32 [768], P(('dp', 'fsdp'))
- grad_second_shift: float32 [768], P(('dp', 'fsdp'))
The draws below stay inside these ranges and needn't reach their ends.
Inputs may be any that keep to these rules, and one draw needn't show every extreme that they name: `segment_ids`: each row of 1024 tokens holds 8 documents one after another; a token's number is its document's place in its row, so numbers rise within a row and every document has tokens. `cls_positions`: the place within its row of the first token of each document; a row's documents are in order, the first at 0. `doc_flags`: each row holds 4 queries and 4 passages in an order drawn from the seed. `positives`: each value is a passage's number, its row times 8 plus its place in the row.
All inputs are finite; a program needn't handle non-finite values.
Results may differ from the reference program's by a relative error of at most 0.017.
Values may be sent and summed in bfloat16 or wider, within the bound.
No kernel may reach another device: no remote copies, remote signals or barrier semaphores. Data moves between devices by JAX's collectives and lax.ppermute only.
A program may use at most 192 MiB of HBM per device.

```python
import jax
import jax.numpy as jnp
from jax import lax

D = 768
HEADS = 12
HEAD = 64
FF = 3072
ROW = 1024
DOCS = 8
ROWS_ALL = 32
TOKENS = 32768
DOCS_ALL = 256


def layout(key):
    per_kind = DOCS // 2
    subkeys = jax.random.split(key, 5)
    orders = jax.vmap(lambda subkey: jax.random.permutation(subkey, DOCS))(jax.random.split(subkeys[0], ROWS_ALL)).astype(jnp.int32)
    query_flags = (orders < per_kind).astype(jnp.int32)
    query_lengths = jax.random.randint(subkeys[1], (ROWS_ALL, per_kind), max(1, ROW // 32), ROW // 16 + 1, dtype=jnp.int32)
    remain = ROW - jnp.sum(query_lengths, axis=1)
    even_share = remain // per_kind
    spread = ROW // (4 * DOCS)
    shifts = jax.random.randint(subkeys[2], (ROWS_ALL, per_kind), -spread, spread + 1, dtype=jnp.int32)
    shifts = shifts.at[:, per_kind - 1].set(0)
    before = jnp.concatenate([jnp.zeros((ROWS_ALL, 1), jnp.int32), shifts[:, :per_kind - 1]], axis=1)
    longer = even_share[:, None] + shifts - before
    longer = longer.at[:, per_kind - 1].add(remain - per_kind * even_share)
    ranked = jnp.concatenate([query_lengths, longer], axis=1)
    lengths = jnp.take_along_axis(ranked, orders, axis=1)
    starts = (jnp.cumsum(lengths, axis=1) - lengths).astype(jnp.int32)
    places = jnp.arange(ROW, dtype=jnp.int32)
    segments = jnp.sum((places[None, None, :] >= starts[:, :, None]).astype(jnp.int32), axis=1) - 1
    inverse = jnp.argsort(orders, axis=1).astype(jnp.int32)
    target_row = jax.random.randint(subkeys[3], (DOCS_ALL,), 0, ROWS_ALL, dtype=jnp.int32)
    target_rank = jax.random.randint(subkeys[4], (DOCS_ALL,), per_kind, DOCS, dtype=jnp.int32)
    chosen = target_row * DOCS + inverse[target_row, target_rank]
    return (segments.reshape(TOKENS).astype(jnp.int32), starts.reshape(DOCS_ALL), query_flags.reshape(DOCS_ALL), chosen.astype(jnp.int32))


def draw_segment_ids(key, part):
    return layout(key)[0]


def draw_cls_positions(key, part):
    return layout(key)[1]


def draw_doc_flags(key, part):
    return layout(key)[2]


def draw_positives(key, part):
    return layout(key)[3]


def steps_of(stream_key, extent, cuts, smallest, largest):
    factor_of, own = 1.0, jax.random.fold_in(stream_key, 6)
    for dim, parts in cuts:
        steps = jnp.exp(jax.random.uniform(jax.random.fold_in(own, dim), (parts,), jnp.float32, smallest / len(cuts), largest / len(cuts)))
        factor_of = factor_of * jnp.repeat(steps, extent[dim] // parts).reshape([-1 if axis == dim else 1 for axis in range(len(extent))])
    return factor_of


def bell_draw(rng, extent, scale, most, cuts=(), kind=jnp.bfloat16):
    drawn = scale * jax.random.normal(rng, extent, jnp.float32)
    if cuts:
        drawn = drawn * steps_of(rng, extent, cuts, -0.22, 0.18)
    return jnp.clip(drawn, -most, most).astype(kind)


def setup_inputs(seed: int = 0) -> dict:
    seeds = jax.random.split(jax.random.key(seed), 22)
    inputs = bell_draw(seeds[0], (TOKENS, D), 1.0, 6.0, ((0, 32),))
    cotangent = bell_draw(seeds[1], (TOKENS, D), 1.0, 6.0, ((0, 32),))
    segment_ids = draw_segment_ids(jax.random.fold_in(seeds[21], 71), 0)
    cls_positions = draw_cls_positions(jax.random.fold_in(seeds[21], 71), 0)
    doc_flags = draw_doc_flags(jax.random.fold_in(seeds[21], 71), 0)
    positives = draw_positives(jax.random.fold_in(seeds[21], 71), 0)
    query_weight = bell_draw(seeds[6], (D, D), D ** -0.5, 0.21875, ((0, 32),))
    query_bias = bell_draw(seeds[7], (D,), 0.3, 1.5, ((0, 32),))
    key_weight = bell_draw(seeds[8], (D, D), D ** -0.5, 0.21875, ((0, 32),))
    value_weight = bell_draw(seeds[9], (D, D), D ** -0.5, 0.21875, ((0, 32),))
    value_bias = bell_draw(seeds[10], (D,), 0.3, 1.5, ((0, 32),))
    out_weight = bell_draw(seeds[11], (D, D), (D // 64) ** -0.5, 1.75, ((0, 32),))
    out_bias = bell_draw(seeds[12], (D,), 0.3, 1.5, ((0, 32),))
    first_gain = jnp.clip(1.0 + 0.1 * jax.random.normal(seeds[13], (D,), jnp.float32), 0.5, 1.5).astype(jnp.bfloat16)
    first_shift = bell_draw(seeds[14], (D,), 0.3, 1.5, ((0, 32),))
    up_weight = bell_draw(seeds[15], (D, FF), D ** -0.5, 0.21875, ((0, 32),))
    up_bias = bell_draw(seeds[16], (FF,), 0.3, 1.5, ((0, 32),))
    down_weight = bell_draw(seeds[17], (FF, D), FF ** -0.5, 0.109375, ((0, 32),))
    down_bias = bell_draw(seeds[18], (D,), 0.3, 1.5, ((0, 32),))
    second_gain = jnp.clip(1.0 + 0.1 * jax.random.normal(seeds[19], (D,), jnp.float32), 0.5, 1.5).astype(jnp.bfloat16)
    second_shift = bell_draw(seeds[20], (D,), 0.3, 1.5, ((0, 32),))
    return {"inputs": inputs, "cotangent": cotangent, "segment_ids": segment_ids, "cls_positions": cls_positions, "doc_flags": doc_flags, "positives": positives, "query_weight": query_weight, "query_bias": query_bias, "key_weight": key_weight, "value_weight": value_weight, "value_bias": value_bias, "out_weight": out_weight, "out_bias": out_bias, "first_gain": first_gain, "first_shift": first_shift, "up_weight": up_weight, "up_bias": up_bias, "down_weight": down_weight, "down_bias": down_bias, "second_gain": second_gain, "second_shift": second_shift}


@jax.custom_vjp
def low(v):
    return lax.optimization_barrier(v.astype(jnp.bfloat16)).astype(jnp.float32)

@jax.custom_vjp
def low_back(v):
    return v

def low_keep(v):
    return (low(v), None)

def low_pass(kept, grad):
    return (grad,)

def back_keep(v):
    return (v, None)

def back_low(kept, grad):
    return (low(grad),)
low.defvjp(low_keep, low_pass)
low_back.defvjp(back_keep, back_low)
EPSILON = 1e-12
HIGHEST = lax.Precision.HIGHEST

def matmul(left, right):
    return jnp.dot(left, right, precision=HIGHEST, preferred_element_type=jnp.float32)

def normalize(values, gain, shift):
    centre = lax.optimization_barrier(jnp.mean(values, axis=-1, keepdims=True))
    centred = values - centre
    spread = lax.optimization_barrier(jnp.mean(centred * centred, axis=-1, keepdims=True))
    return centred * lax.rsqrt(spread + EPSILON) * gain + shift

def row_attention(pieces):
    queries, keys_row, values_row, segments = pieces
    length = queries.shape[0]
    query_heads = queries.reshape(length, HEADS, HEAD)
    key_heads = keys_row.reshape(length, HEADS, HEAD)
    value_heads = values_row.reshape(length, HEADS, HEAD)
    scores = low_back(jnp.einsum('qhd,khd->hqk', query_heads, key_heads, precision=HIGHEST))
    match_mask = segments[:, None] == segments[None, :]
    scores = jnp.where(match_mask[None], scores, -1000000000.0)
    weights = low(jax.nn.softmax(scores, axis=-1))
    result = jnp.einsum('hqk,khd->qhd', weights, value_heads, precision=HIGHEST)
    return result.reshape(length, HEADS * HEAD)

def reference(inputs, cotangent, segment_ids, cls_positions, doc_flags, positives, query_weight, query_bias, key_weight, value_weight, value_bias, out_weight, out_bias, first_gain, first_shift, up_weight, up_bias, down_weight, down_bias, second_gain, second_shift):
    params = tuple((weight.astype(jnp.float32) for weight in (query_weight, query_bias, key_weight, value_weight, value_bias, out_weight, out_bias, first_gain, first_shift, up_weight, up_bias, down_weight, down_bias, second_gain, second_shift)))
    segment_rows = segment_ids.reshape(ROWS_ALL, ROW)

    def layer(source, *weights):
        query_matrix, query_offset, key_matrix, value_matrix, value_offset, out_matrix, out_offset, gain_one, shift_one, up_matrix, up_offset, down_matrix, down_offset, gain_two, shift_two = weights
        queries = low(low_back((matmul(source, query_matrix) + query_offset) * 0.125))
        keys_all = low(low_back(matmul(source, key_matrix)))
        values_all = low(low_back(matmul(source, value_matrix) + value_offset))
        attended = lax.map(jax.checkpoint(row_attention), (queries.reshape(ROWS_ALL, ROW, D), keys_all.reshape(ROWS_ALL, ROW, D), values_all.reshape(ROWS_ALL, ROW, D), segment_rows))
        attended = low(low_back(attended.reshape(TOKENS, D)))
        branch = low_back(matmul(attended, out_matrix) + out_offset)
        first = normalize(source + branch, gain_one, shift_one)
        up_value = low_back(matmul(low(first), up_matrix) + up_offset)
        hidden = low(jax.nn.gelu(up_value, approximate=False))
        down_value = low_back(matmul(hidden, down_matrix) + down_offset)
        return normalize(first + down_value, gain_two, shift_two)
    output_full, pull_layer = jax.vjp(layer, inputs.astype(jnp.float32), *params)
    token_index = (jnp.arange(DOCS_ALL, dtype=jnp.int32) // DOCS * ROW + cls_positions).astype(jnp.int32)
    picker = (token_index[:, None] == jnp.arange(TOKENS, dtype=jnp.int32)[None, :]).astype(jnp.float32)
    embedded = low(matmul(picker, output_full))
    passage = doc_flags == 0
    hit_mask = jnp.arange(DOCS_ALL, dtype=jnp.int32)[None, :] == positives[:, None]
    query_rows = doc_flags.astype(jnp.float32)

    def contrast(vectors):
        raw = low_back(matmul(vectors, vectors.T))
        pair_scores = raw * (2.0 * D ** (-0.5))
        masked = jnp.where(passage[None, :], pair_scores, -1000000000.0)
        log_sums = jax.nn.logsumexp(masked, axis=1)
        picked = lax.optimization_barrier(jnp.sum(jnp.where(hit_mask, pair_scores, 0.0), axis=1))
        return (pair_scores, jnp.sum(query_rows * (log_sums - picked)))
    (pair_scores, loss_total), pull_head = jax.vjp(contrast, embedded)
    embedding_grad, = pull_head((jnp.zeros_like(pair_scores), jnp.ones_like(loss_total)))
    grad_output = cotangent.astype(jnp.float32) + matmul(picker.T, embedding_grad)
    grads = pull_layer(grad_output)
    return (output_full.astype(jnp.bfloat16), embedded.astype(jnp.bfloat16), pair_scores, loss_total / (DOCS_ALL // 2), embedding_grad, grads[0], grads[1], grads[2], grads[3], grads[4], grads[5], grads[6], grads[7], grads[8], grads[9], grads[10], grads[11], grads[12], grads[13], grads[14], grads[15])
```

```python
from functools import partial

import jax
import jax.numpy as jnp
from jax import lax
from jax.experimental import pallas as pl
from jax.experimental.pallas import tpu as pltpu
from jax.sharding import PartitionSpec as P

D = 768
HEADS = 12
HEAD = 64
FF = 3072
ROW = 1024
DOCS = 8
EPSILON = 1e-12
AXES = ("dp", "fsdp")
PAIR = 2 * HEAD
PAIRS = HEADS // 2
QBLOCK = 128
WINDOWS = (384, 640, 1024)
GROUPS = 3
CHUNKS = FF // D
F32 = jnp.float32
BF16 = jnp.bfloat16
VMEM_LIMIT = 56 * 1024 * 1024
HALF = 3 * D // 2
ANY = pl.BlockSpec(memory_space=pl.ANY)


def dot(left, right):
    return jnp.dot(left, right, preferred_element_type=F32)


def dot_tn(left, right):
    return lax.dot_general(left, right, (((0,), (0,)), ((), ())), preferred_element_type=F32)


def dot_nt(left, right):
    return lax.dot_general(left, right, (((1,), (1,)), ((), ())), preferred_element_type=F32)


def stages_of(size):
    bits = size.bit_length() - 1
    return [(low, min(2, bits - low)) for low in range(1, bits, 2)]


def swap(block, mask):
    size = lax.axis_size(AXES)
    return lax.ppermute(block, AXES, [(i, i ^ mask) for i in range(size)])


def place(pieces, own):
    lead, rows, cols = pieces[0].shape
    out = jnp.zeros((lead, len(pieces), rows, cols), pieces[0].dtype)
    for m, piece in enumerate(pieces):
        out = lax.dynamic_update_slice_in_dim(out, piece[:, None], own ^ m, axis=1)
    return out


def gather_chips(block):
    rows, cols = block.shape
    index = lax.axis_index(AXES)
    block = block[None]
    for low, width in reversed(stages_of(lax.axis_size(AXES))):
        pieces = [block] + [swap(block, m << low) for m in range(1, 1 << width)]
        own = (index >> low) & ((1 << width) - 1)
        block = place(pieces, own).reshape(-1, rows, cols)
    return block.reshape(-1, cols)


def gather_rows(block):
    rows, cols = block.shape
    core = lax.axis_index(AXES) & 1
    both = place([block[None], swap(block, 1)[None]], core)
    return gather_chips(both.reshape(2 * rows, cols))


def added(pieces):
    total = pieces[0].astype(F32)
    for piece in pieces[1:]:
        total = total + piece.astype(F32)
    return total


def scatter_steps(mine, other):
    size = lax.axis_size(AXES)
    index = lax.axis_index(AXES)
    rows, cols = 2 * mine.shape[0] // size, mine.shape[1]
    yield [other]
    held = [mine.reshape(-1, rows, cols), swap(other, 1).reshape(-1, rows, cols)]
    for low, width in stages_of(size):
        count = 1 << width
        own = (index >> low) & (count - 1)

        def part(m):
            return [
                lax.dynamic_slice_in_dim(piece.reshape(-1, count, rows, cols), own ^ m, 1, axis=1)[:, 0]
                for piece in held
            ]

        sent = [added(part(m)).astype(BF16) for m in range(1, count)]
        yield sent
        held = part(0) + [swap(piece, m << low) for m, piece in enumerate(sent, 1)]
    total = added(held).reshape(2, rows // 2, cols)
    core = index & 1
    keep = lax.dynamic_index_in_dim(total, core, 0, False)
    give = lax.dynamic_index_in_dim(total, 1 - core, 0, False).astype(BF16)
    got = swap(give, 1).astype(F32)
    yield jnp.where(core == 0, keep, got), jnp.where(core == 0, got, keep)


def project_kernel(half_ref, x_ref, w_ref, offset_ref, factor_ref, *refs):
    out_ref = refs[-1]
    value = dot(x_ref[...], w_ref[...])
    out_ref[...] = ((value + offset_ref[...]) * factor_ref[...]).astype(BF16)


def project(inputs, weights, offset, factor, half, before):
    block = 256
    extra = [] if before is None else [before]
    return pl.pallas_call(
        project_kernel,
        out_shape=jax.ShapeDtypeStruct((ROW, 3 * D), BF16),
        grid_spec=pltpu.PrefetchScalarGridSpec(
            num_scalar_prefetch=1,
            grid=(ROW // block,),
            in_specs=[
                pl.BlockSpec((block, D), lambda i, h: (i, 0)),
                pl.BlockSpec((D, HALF), lambda i, h: (0, 0)),
                pl.BlockSpec((1, HALF), lambda i, h: (0, h[0])),
                pl.BlockSpec((1, HALF), lambda i, h: (0, h[0])),
            ]
            + [ANY] * len(extra),
            out_specs=pl.BlockSpec((block, HALF), lambda i, h: (i, h[0])),
        ),
        input_output_aliases={} if before is None else {5: 0},
        compiler_params=pltpu.CompilerParams(vmem_limit_bytes=VMEM_LIMIT),
        cost_estimate=pl.CostEstimate(flops=1_800_000_000, bytes_accessed=6_000_000, transcendentals=0),
        name="project",
    )(half.reshape(1), inputs, weights, offset, factor, *extra)


def weights_kernel(half_ref, x_ref, q_ref, k_ref, v_ref, grads_ref, out_ref):
    def fill(wide_ref, wide_cols, narrow_cols):
        out_ref[:, wide_cols] = dot_tn(x_ref[...], wide_ref[...]).astype(BF16)
        out_ref[:, narrow_cols] = dot_tn(x_ref[...], k_ref[...]).astype(BF16)
        total = jnp.sum(wide_ref[...].astype(F32), axis=0, keepdims=True)
        table = jnp.concatenate([total, grads_ref[1:16, :], jnp.zeros((112, D), F32)], axis=0)
        out_ref[:, HALF:] = table.T.astype(BF16)

    @pl.when(half_ref[0] == 0)
    def _():
        fill(q_ref, slice(0, D), slice(D, HALF))

    @pl.when(half_ref[0] == 1)
    def _():
        fill(v_ref, slice(D // 2, HALF), slice(0, D // 2))


def weights_back(inputs, dq, dk, dv, grads, half):
    fixed = lambda i, h: (0, 0)
    return pl.pallas_call(
        weights_kernel,
        out_shape=jax.ShapeDtypeStruct((D, HALF + 128), BF16),
        grid_spec=pltpu.PrefetchScalarGridSpec(
            num_scalar_prefetch=1,
            grid=(1,),
            in_specs=[
                pl.BlockSpec((ROW, D), fixed),
                pl.BlockSpec((ROW, D), fixed),
                pl.BlockSpec((ROW, D // 2), lambda i, h: (0, h[0])),
                pl.BlockSpec((ROW, D), fixed),
                pl.BlockSpec((16, D), fixed),
            ],
            out_specs=pl.BlockSpec((D, HALF + 128), fixed),
        ),
        compiler_params=pltpu.CompilerParams(vmem_limit_bytes=VMEM_LIMIT),
        cost_estimate=pl.CostEstimate(flops=1_800_000_000, bytes_accessed=8_000_000, transcendentals=0),
        name="weights_back",
    )(half.reshape(1), inputs, dq, dk, dv, grads)


def inputs_kernel(core_ref, one_ref, q_ref, k_ref, v_ref, mine_ref, other_ref, out_ref):
    def fill(low_ref, high_ref):
        half = D // 2
        total = one_ref[...] + dot_nt(q_ref[...], low_ref[:, :D]) + dot_nt(v_ref[...], high_ref[:, half:HALF])
        total = total + dot_nt(k_ref[:, :half], low_ref[:, D:HALF]) + dot_nt(k_ref[:, half:], high_ref[:, :half])
        out_ref[...] = total

    @pl.when(core_ref[0] == 0)
    def _():
        fill(mine_ref, other_ref)

    @pl.when(core_ref[0] == 1)
    def _():
        fill(other_ref, mine_ref)


def inputs_back(grad_one, dq, dk, dv, mine, other, core):
    block = 256
    rows = pl.BlockSpec((block, D), lambda i, h: (i, 0))
    weights = pl.BlockSpec((D, HALF), lambda i, h: (0, 0))
    return pl.pallas_call(
        inputs_kernel,
        out_shape=jax.ShapeDtypeStruct((ROW, D), F32),
        grid_spec=pltpu.PrefetchScalarGridSpec(
            num_scalar_prefetch=1,
            grid=(ROW // block,),
            in_specs=[rows, rows, rows, rows, weights, weights],
            out_specs=rows,
        ),
        compiler_params=pltpu.CompilerParams(vmem_limit_bytes=VMEM_LIMIT),
        cost_estimate=pl.CostEstimate(flops=3_600_000_000, bytes_accessed=14_000_000, transcendentals=0),
        name="inputs_back",
    )(core.reshape(1), grad_one, dq, dk, dv, mine, other)


def row_bounds(cls_ref, places):
    first = jnp.zeros_like(places)
    end = jnp.full_like(places, ROW)
    for d in range(1, DOCS):
        first = jnp.where(places >= cls_ref[d], cls_ref[d], first)
    for d in range(DOCS - 1, 0, -1):
        end = jnp.where(places < cls_ref[d], cls_ref[d], end)
    return first, end


def scalar_bounds(cls_ref, low, high):
    first, end = jnp.int32(0), jnp.int32(ROW)
    for d in range(1, DOCS):
        first = jnp.where(low >= cls_ref[d], cls_ref[d], first)
    for d in range(DOCS - 1, 0, -1):
        end = jnp.where(high < cls_ref[d], cls_ref[d], end)
    return first, end


def over_windows(cls_ref, begin, step):
    low, high = scalar_bounds(cls_ref, begin, begin + QBLOCK - 1)
    low = (low // 16) * 16
    before = None
    for width in WINDOWS:
        start = pl.multiple_of(jnp.minimum(low, ROW - width), 16)
        fits = high <= start + width
        take = fits if before is None else jnp.logical_and(fits, jnp.logical_not(before))
        before = fits if before is None else jnp.logical_or(fits, before)
        pl.when(take)(partial(step, start, width))


def split_pair(block):
    lane = lax.broadcasted_iota(jnp.int32, block.shape, 1)
    zero = jnp.zeros_like(block)
    return jnp.concatenate(
        [jnp.where(lane < HEAD, block, zero), jnp.where(lane < HEAD, zero, block)], axis=0
    )


def join_pair(both):
    half = both.shape[0] // 2
    lane = lax.broadcasted_iota(jnp.int32, (half, both.shape[1]), 1)
    return jnp.where(lane < HEAD, both[:half], both[half:])


def attend_kernel(cls_ref, q_ref, k_ref, v_ref, out_ref, log_ref):
    begin = pl.program_id(0) * QBLOCK

    def step(start, width):
        places = begin + lax.broadcasted_iota(jnp.int32, (QBLOCK, 1), 0)
        first, end = row_bounds(cls_ref, places)
        keys = start + lax.broadcasted_iota(jnp.int32, (QBLOCK, width), 1)
        mask = jnp.logical_and(keys >= first, keys < end)
        mask = jnp.concatenate([mask, mask], axis=0)
        lane = lax.broadcasted_iota(jnp.int32, (QBLOCK, 128), 1)
        logs = jnp.zeros((QBLOCK, 128), F32)
        for p in range(PAIRS):
            cols = slice(PAIR * p, PAIR * (p + 1))
            queries = split_pair(q_ref[:, cols])
            scores = dot_nt(queries, k_ref[pl.ds(start, width), cols])
            scores = jnp.where(mask, scores, -1000000000.0)
            top = jnp.max(scores, axis=1, keepdims=True)
            weights = jnp.exp(scores - top)
            total = jnp.sum(weights, axis=1, keepdims=True)
            result = dot(weights.astype(BF16), v_ref[pl.ds(start, width), cols]) / total
            out_ref[:, cols] = join_pair(result).astype(BF16)
            log_total = top + jnp.log(total)
            logs = jnp.where(lane == 2 * p, log_total[:QBLOCK], logs)
            logs = jnp.where(lane == 2 * p + 1, log_total[QBLOCK:], logs)
        log_ref[...] = logs.T[:16]

    over_windows(cls_ref, begin, step)


def attend(cls, qkv):
    return pl.pallas_call(
        attend_kernel,
        out_shape=(
            jax.ShapeDtypeStruct((ROW, D), BF16),
            jax.ShapeDtypeStruct((16, ROW), F32),
        ),
        grid_spec=pltpu.PrefetchScalarGridSpec(
            num_scalar_prefetch=1,
            grid=(ROW // QBLOCK,),
            in_specs=[
                pl.BlockSpec((QBLOCK, D), lambda i, c: (i, 0)),
                pl.BlockSpec((ROW, D), lambda i, c: (0, 1)),
                pl.BlockSpec((ROW, D), lambda i, c: (0, 2)),
            ],
            out_specs=[
                pl.BlockSpec((QBLOCK, D), lambda i, c: (i, 0)),
                pl.BlockSpec((16, QBLOCK), lambda i, c: (0, i)),
            ],
        ),
        compiler_params=pltpu.CompilerParams(vmem_limit_bytes=VMEM_LIMIT),
        cost_estimate=pl.CostEstimate(flops=4_000_000_000, bytes_accessed=8_000_000, transcendentals=6_000_000),
        name="attend",
    )(cls, qkv, qkv, qkv)


def attend_back_kernel(base, span, cls_ref, q_ref, k_ref, v_ref, do_ref, log_ref, *refs):
    dq_ref, dk_ref, dv_ref, dk_sum, dv_sum = refs[-5:]
    begin = pl.program_id(0) * QBLOCK

    @pl.when(pl.program_id(0) == 0)
    def _():
        dk_sum[...] = jnp.zeros_like(dk_sum)
        dv_sum[...] = jnp.zeros_like(dv_sum)

    def step(start, width):
        places = begin + lax.broadcasted_iota(jnp.int32, (1, QBLOCK), 1)
        first, end = row_bounds(cls_ref, places)
        keys = start + lax.broadcasted_iota(jnp.int32, (width, QBLOCK), 0)
        mask = jnp.logical_and(keys >= first, keys < end)
        mask = jnp.concatenate([mask, mask], axis=1)
        window = pl.ds(start, width)
        for p in range(span // PAIR):
            cols = slice(PAIR * p, PAIR * (p + 1))
            h = base + 2 * p
            queries = split_pair(q_ref[:, cols])
            grads = split_pair(do_ref[:, cols])
            keys_pair = k_ref[window, cols]
            log_total = jnp.concatenate([log_ref[h : h + 1, :], log_ref[h + 1 : h + 2, :]], axis=1)
            scores = dot_nt(keys_pair, queries)
            weights = jnp.exp(jnp.where(mask, scores - log_total, -1000000000.0))
            dv_sum[window, cols] += dot(weights.astype(BF16), grads)
            grad_weights = dot_nt(v_ref[window, cols], grads)
            inner = jnp.sum(grad_weights * weights, axis=0, keepdims=True)
            grad_scores = (weights * (grad_weights - inner)).astype(BF16)
            dk_sum[window, cols] += dot(grad_scores, queries)
            grad_queries = join_pair(dot_tn(grad_scores, keys_pair))
            dq_ref[:, cols] = (grad_queries.astype(BF16).astype(F32) * 0.125).astype(BF16)

    over_windows(cls_ref, begin, step)

    @pl.when(pl.program_id(0) == pl.num_programs(0) - 1)
    def _():
        dk_ref[...] = dk_sum[...].astype(BF16)
        dv_ref[...] = dv_sum[...].astype(BF16)


def attend_back(cls, qkv, grad_attended, log_total, group, before, after):
    span = D // GROUPS
    extra = list(before) + list(after)
    shape = jax.ShapeDtypeStruct((ROW, D), BF16)
    return pl.pallas_call(
        partial(attend_back_kernel, group * (HEADS // GROUPS), span),
        out_shape=(shape, shape, shape),
        grid_spec=pltpu.PrefetchScalarGridSpec(
            num_scalar_prefetch=1,
            grid=(ROW // QBLOCK,),
            in_specs=[
                pl.BlockSpec((QBLOCK, span), lambda i, c: (i, group)),
                pl.BlockSpec((ROW, span), lambda i, c: (0, GROUPS + group)),
                pl.BlockSpec((ROW, span), lambda i, c: (0, 2 * GROUPS + group)),
                pl.BlockSpec((QBLOCK, span), lambda i, c: (i, group)),
                pl.BlockSpec((16, QBLOCK), lambda i, c: (0, i)),
            ]
            + [ANY] * len(extra),
            out_specs=[
                pl.BlockSpec((QBLOCK, span), lambda i, c: (i, group)),
                pl.BlockSpec((ROW, span), lambda i, c: (0, group)),
                pl.BlockSpec((ROW, span), lambda i, c: (0, group)),
            ],
            scratch_shapes=[pltpu.VMEM((ROW, span), F32), pltpu.VMEM((ROW, span), F32)],
        ),
        input_output_aliases={6 + i: i for i in range(len(before))},
        compiler_params=pltpu.CompilerParams(vmem_limit_bytes=VMEM_LIMIT),
        cost_estimate=pl.CostEstimate(
            flops=12_000_000_000 // GROUPS, bytes_accessed=12_000_000 // GROUPS, transcendentals=6_000_000 // GROUPS
        ),
        name="attend_back",
    )(cls, qkv, qkv, qkv, grad_attended, log_total, *extra)


def normalized(values):
    centre = jnp.mean(values, axis=-1, keepdims=True)
    centred = values - centre
    spread = jnp.mean(centred * centred, axis=-1, keepdims=True)
    inverse = lax.rsqrt(spread + EPSILON)
    return centred * inverse, inverse


def normalized_back(grad, hat, inverse, gain):
    scaled = grad * gain
    mean_scaled = jnp.mean(scaled, axis=-1, keepdims=True)
    mean_hat = jnp.mean(scaled * hat, axis=-1, keepdims=True)
    return inverse * (scaled - mean_scaled - hat * mean_hat)


def first_kernel(att_ref, w_ref, x_ref, vec_ref, hat_ref, inv_ref, low_ref):
    residual = x_ref[...].astype(F32) + dot(att_ref[...], w_ref[...]) + vec_ref[2:3, :]
    hat, inverse = normalized(residual)
    hat_ref[...] = hat
    inv_ref[...] = inverse
    low_ref[...] = (hat * vec_ref[3:4, :] + vec_ref[4:5, :]).astype(BF16)


def first_norm(attended, weights, inputs, vectors):
    block = 256
    rows = lambda i: (i, 0)
    fixed = lambda i: (0, 0)
    return pl.pallas_call(
        first_kernel,
        out_shape=(
            jax.ShapeDtypeStruct((ROW, D), F32),
            jax.ShapeDtypeStruct((ROW, 1), F32),
            jax.ShapeDtypeStruct((ROW, D), BF16),
        ),
        grid=(ROW // block,),
        in_specs=[
            pl.BlockSpec((block, D), rows),
            pl.BlockSpec((D, D), lambda i: (0, 2 * CHUNKS)),
            pl.BlockSpec((block, D), rows),
            pl.BlockSpec((16, D), fixed),
        ],
        out_specs=[
            pl.BlockSpec((block, D), rows),
            pl.BlockSpec((block, 1), rows),
            pl.BlockSpec((block, D), rows),
        ],
        compiler_params=pltpu.CompilerParams(vmem_limit_bytes=VMEM_LIMIT),
        cost_estimate=pl.CostEstimate(flops=1_200_000_000, bytes_accessed=10_000_000, transcendentals=0),
        name="first_norm",
    )(attended, weights, inputs, vectors)


def gelu_parts(v):
    bell = jnp.exp(v * v * -0.5)
    t = 1.0 / (1.0 + (0.3275911 * 0.7071067811865476) * jnp.abs(v))
    poly = t * (0.254829592 + t * (-0.284496736 + t * (1.421413741 + t * (-1.453152027 + t * 1.061405429))))
    tail = 0.5 * poly * bell
    return jnp.where(v >= 0.0, 1.0 - tail, tail), 0.3989422804014327 * bell


def forward_kernel(
    cls_ref, low_ref, hat_ref, up_ref, down_ref, vec_ref, hid_ref, slope_ref, hat2_ref, inv2_ref, out_ref, emb_ref, acc_ref
):
    j = pl.program_id(0)
    block = 256

    @pl.when(j == 0)
    def _():
        acc_ref[...] = hat_ref[...] * vec_ref[3:4, :] + (vec_ref[4:5, :] + vec_ref[5:6, :])

    bias = vec_ref[pl.ds(8 + j, 1), :]
    for r in range(ROW // block):
        rows = slice(block * r, block * (r + 1))
        value = dot(low_ref[rows, :], up_ref[...]) + bias
        phi, density = gelu_parts(value)
        hidden = (value * phi).astype(BF16)
        hid_ref[rows, :] = hidden
        slope_ref[rows, :] = (phi + value * density).astype(BF16)
        acc_ref[rows, :] += dot(hidden, down_ref[...])

    @pl.when(j == CHUNKS - 1)
    def _():
        for r in range(ROW // block):
            rows = slice(block * r, block * (r + 1))
            hat, inverse = normalized(acc_ref[rows, :])
            hat2_ref[rows, :] = hat
            inv2_ref[rows, :] = inverse
            full = hat * vec_ref[6:7, :] + vec_ref[7:8, :]
            out_ref[rows, :] = full.astype(BF16)
            acc_ref[rows, :] = full
        picked = [acc_ref[pl.ds(cls_ref[d], 1), :] for d in range(DOCS)]
        emb_ref[...] = jnp.concatenate(picked, axis=0).astype(BF16)


def feed_forward(cls, low, hat, pack, vectors):
    fixed = lambda j, c: (0, 0)
    return pl.pallas_call(
        forward_kernel,
        out_shape=(
            jax.ShapeDtypeStruct((ROW, FF), BF16),
            jax.ShapeDtypeStruct((ROW, FF), BF16),
            jax.ShapeDtypeStruct((ROW, D), F32),
            jax.ShapeDtypeStruct((ROW, 1), F32),
            jax.ShapeDtypeStruct((ROW, D), BF16),
            jax.ShapeDtypeStruct((DOCS, D), BF16),
        ),
        grid_spec=pltpu.PrefetchScalarGridSpec(
            num_scalar_prefetch=1,
            grid=(CHUNKS,),
            in_specs=[
                pl.BlockSpec((ROW, D), fixed),
                pl.BlockSpec((ROW, D), fixed),
                pl.BlockSpec((D, D), lambda j, c: (0, j)),
                pl.BlockSpec((D, D), lambda j, c: (0, CHUNKS + j)),
                pl.BlockSpec((16, D), fixed),
            ],
            out_specs=[
                pl.BlockSpec((ROW, D), lambda j, c: (0, j)),
                pl.BlockSpec((ROW, D), lambda j, c: (0, j)),
                pl.BlockSpec((ROW, D), fixed),
                pl.BlockSpec((ROW, 1), fixed),
                pl.BlockSpec((ROW, D), fixed),
                pl.BlockSpec((DOCS, D), fixed),
            ],
            scratch_shapes=[pltpu.VMEM((ROW, D), F32)],
        ),
        compiler_params=pltpu.CompilerParams(vmem_limit_bytes=VMEM_LIMIT),
        cost_estimate=pl.CostEstimate(flops=9_700_000_000, bytes_accessed=30_000_000, transcendentals=6_000_000),
        name="feed_forward",
    )(cls, low, hat, pack, pack, vectors)


def chunk_back(core, j, two_low_ref, hid_ref, slope_ref, low_ref, up_ref, down_ref, mine_ref, other_ref, acc_ref, grads_ref, row):
    block = 256
    grad_up = []
    for r in range(ROW // block):
        rows = slice(block * r, block * (r + 1))
        grad_hidden = dot_nt(two_low_ref[rows, :], down_ref[...])
        part = (grad_hidden * slope_ref[rows, :].astype(F32)).astype(BF16)
        grads_ref[pl.ds(row, 1), :] += jnp.sum(part.astype(F32), axis=0, keepdims=True)
        acc_ref[rows, :] += dot_nt(part, up_ref[...])
        grad_up.append(part)
    grad_up = jnp.concatenate(grad_up, axis=0)
    cols = pl.ds(pl.multiple_of(j * D, 128), D)
    down_grad = dot_tn(hid_ref[...], two_low_ref[...]).astype(BF16)
    up_grad = dot_tn(low_ref[...], grad_up).astype(BF16)

    @pl.when(core == 0)
    def _():
        mine_ref[:, cols] = up_grad
        other_ref[:, cols] = down_grad

    @pl.when(core == 1)
    def _():
        mine_ref[:, cols] = down_grad
        other_ref[:, cols] = up_grad


def back_one_kernel(
    cls_ref, core_ref, cot_ref, eg_ref, hat2_ref, inv2_ref, low_ref, hid_ref, slope_ref, up_ref, down_ref, vec_ref,
    mine_ref, other_ref, acc_ref, two_low_ref, grads_ref,
):
    j = pl.program_id(0)
    block = 256

    @pl.when(j == 0)
    def _():
        grads_ref[...] = jnp.zeros_like(grads_ref)
        acc_ref[...] = cot_ref[...].astype(F32)
        for d in range(DOCS):
            acc_ref[pl.ds(cls_ref[d], 1), :] += eg_ref[d : d + 1, :]
        for r in range(ROW // block):
            rows = slice(block * r, block * (r + 1))
            grad, hat = acc_ref[rows, :], hat2_ref[rows, :]
            grads_ref[6:7, :] += jnp.sum(grad * hat, axis=0, keepdims=True)
            grads_ref[7:8, :] += jnp.sum(grad, axis=0, keepdims=True)
            two = normalized_back(grad, hat, inv2_ref[rows, :], vec_ref[6:7, :])
            acc_ref[rows, :] = two
            two_low = two.astype(BF16)
            two_low_ref[rows, :] = two_low
            grads_ref[5:6, :] += jnp.sum(two_low.astype(F32), axis=0, keepdims=True)

    chunk_back(
        core_ref[0], j, two_low_ref, hid_ref, slope_ref, low_ref, up_ref, down_ref, mine_ref, other_ref, acc_ref, grads_ref, 8 + j
    )


def back_one(cls, core, cotangent, embedding_grad, hat2, inv2, low, hidden, slope, pack, vectors):
    fixed = lambda j, c, h: (0, 0)
    whole = lambda rows, cols: pl.BlockSpec((rows, cols), fixed)
    steps = CHUNKS // 2
    return pl.pallas_call(
        back_one_kernel,
        out_shape=(
            jax.ShapeDtypeStruct((D, steps * D), BF16),
            jax.ShapeDtypeStruct((D, steps * D), BF16),
            jax.ShapeDtypeStruct((ROW, D), F32),
            jax.ShapeDtypeStruct((ROW, D), BF16),
            jax.ShapeDtypeStruct((16, D), F32),
        ),
        grid_spec=pltpu.PrefetchScalarGridSpec(
            num_scalar_prefetch=2,
            grid=(steps,),
            in_specs=[
                whole(ROW, D),
                whole(DOCS, D),
                whole(ROW, D),
                whole(ROW, 1),
                whole(ROW, D),
                pl.BlockSpec((ROW, D), lambda j, c, h: (0, j)),
                pl.BlockSpec((ROW, D), lambda j, c, h: (0, j)),
                pl.BlockSpec((D, D), lambda j, c, h: (0, j)),
                pl.BlockSpec((D, D), lambda j, c, h: (0, CHUNKS + j)),
                whole(16, D),
            ],
            out_specs=[
                whole(D, steps * D),
                whole(D, steps * D),
                whole(ROW, D),
                whole(ROW, D),
                whole(16, D),
            ],
        ),
        compiler_params=pltpu.CompilerParams(vmem_limit_bytes=VMEM_LIMIT),
        cost_estimate=pl.CostEstimate(flops=9_700_000_000, bytes_accessed=30_000_000, transcendentals=0),
        name="back_one",
    )(cls, core.reshape(1), cotangent, embedding_grad, hat2, inv2, low, hidden, slope, pack, pack, vectors)


def back_two_kernel(
    core_ref, two_ref, two_low_ref, grads_in_ref, hat_ref, inv_ref, low_ref, hid_ref, slope_ref, up_ref, down_ref,
    out_w_ref, att_ref, vec_ref, mine_ref, other_ref, one_ref, datt_ref, grads_ref,
):
    j = pl.program_id(0)
    block = 256
    steps = CHUNKS // 2

    @pl.when(j == 0)
    def _():
        grads_ref[...] = grads_in_ref[...]
        one_ref[...] = two_ref[...]

    chunk_back(
        core_ref[0], j, two_low_ref, hid_ref, slope_ref, low_ref, up_ref, down_ref, mine_ref, other_ref, one_ref, grads_ref,
        8 + steps + j,
    )

    @pl.when(j == steps - 1)
    def _():
        lows = []
        for r in range(ROW // block):
            rows = slice(block * r, block * (r + 1))
            grad, hat = one_ref[rows, :], hat_ref[rows, :]
            grads_ref[3:4, :] += jnp.sum(grad * hat, axis=0, keepdims=True)
            grads_ref[4:5, :] += jnp.sum(grad, axis=0, keepdims=True)
            one = normalized_back(grad, hat, inv_ref[rows, :], vec_ref[3:4, :])
            one_ref[rows, :] = one
            one_low = one.astype(BF16)
            lows.append(one_low)
            grads_ref[2:3, :] += jnp.sum(one_low.astype(F32), axis=0, keepdims=True)
            datt_ref[rows, :] = dot_nt(one_low, out_w_ref[...]).astype(BF16)
        grad = dot_tn(att_ref[...], jnp.concatenate(lows, axis=0)).astype(BF16)

        @pl.when(core_ref[0] == 0)
        def _():
            mine_ref[:, steps * D :] = grad[:, : D // 2]
            other_ref[:, steps * D :] = grad[:, D // 2 :]

        @pl.when(core_ref[0] == 1)
        def _():
            mine_ref[:, steps * D :] = grad[:, D // 2 :]
            other_ref[:, steps * D :] = grad[:, : D // 2]


def back_two(core, two, two_low, grads, hat, inv, low, hidden, slope, pack, attended, vectors):
    fixed = lambda j, h: (0, 0)
    whole = lambda rows, cols: pl.BlockSpec((rows, cols), fixed)
    steps = CHUNKS // 2
    width = steps * D + D // 2
    return pl.pallas_call(
        back_two_kernel,
        out_shape=(
            jax.ShapeDtypeStruct((D, width), BF16),
            jax.ShapeDtypeStruct((D, width), BF16),
            jax.ShapeDtypeStruct((ROW, D), F32),
            jax.ShapeDtypeStruct((ROW, D), BF16),
            jax.ShapeDtypeStruct((16, D), F32),
        ),
        grid_spec=pltpu.PrefetchScalarGridSpec(
            num_scalar_prefetch=1,
            grid=(steps,),
            in_specs=[
                whole(ROW, D),
                whole(ROW, D),
                whole(16, D),
                whole(ROW, D),
                whole(ROW, 1),
                whole(ROW, D),
                pl.BlockSpec((ROW, D), lambda j, h: (0, steps + j)),
                pl.BlockSpec((ROW, D), lambda j, h: (0, steps + j)),
                pl.BlockSpec((D, D), lambda j, h: (0, steps + j)),
                pl.BlockSpec((D, D), lambda j, h: (0, CHUNKS + steps + j)),
                pl.BlockSpec((D, D), lambda j, h: (0, 2 * CHUNKS)),
                whole(ROW, D),
                whole(16, D),
            ],
            out_specs=[
                whole(D, width),
                whole(D, width),
                whole(ROW, D),
                whole(ROW, D),
                whole(16, D),
            ],
        ),
        compiler_params=pltpu.CompilerParams(vmem_limit_bytes=VMEM_LIMIT),
        cost_estimate=pl.CostEstimate(flops=12_000_000_000, bytes_accessed=35_000_000, transcendentals=0),
        name="back_two",
    )(core.reshape(1), two, two_low, grads, hat, inv, low, hidden, slope, pack, pack, pack, attended, vectors)


def contrast(embeddings, everyone, flags, positives):
    docs_dev, docs_all = embeddings.shape[0], everyone.shape[0]
    begin = lax.axis_index(AXES) * docs_dev
    scale = 2.0 * D ** (-0.5)
    scores = dot_nt(everyone, everyone) * scale
    passage = flags == 0
    masked = jnp.where(passage[None, :], scores, -1000000000.0)
    maxima = jnp.max(masked, axis=1)
    log_sums = maxima + jnp.log(jnp.sum(jnp.exp(masked - maxima[:, None]), axis=1))
    hit_mask = jnp.arange(docs_all, dtype=jnp.int32)[None, :] == positives[:, None]
    picked = jnp.sum(jnp.where(hit_mask, scores, 0.0), axis=1)
    query_rows = flags.astype(F32)
    loss = jnp.sum(query_rows * (log_sums - picked)) / (docs_all // 2)
    chances = jnp.where(passage[None, :], jnp.exp(scores - log_sums[:, None]), 0.0)
    pairs = (query_rows[:, None] * scale * (chances - hit_mask.astype(F32))).astype(BF16)
    own_rows = lax.dynamic_slice_in_dim(pairs, begin, docs_dev, axis=0)
    own_cols = lax.dynamic_slice_in_dim(pairs, begin, docs_dev, axis=1)
    grad = dot(own_rows, everyone) + dot_tn(own_cols, everyone)
    return lax.dynamic_slice_in_dim(scores, begin, docs_dev, axis=0), loss, grad


def body(
    inputs,
    cotangent,
    segment_ids,
    cls_positions,
    doc_flags,
    positives,
    query_weight,
    query_bias,
    key_weight,
    value_weight,
    value_bias,
    out_weight,
    out_bias,
    first_gain,
    first_shift,
    up_weight,
    up_bias,
    down_weight,
    down_bias,
    second_gain,
    second_shift,
):
    rows = query_weight.shape[0]
    size = lax.axis_size(AXES)
    core = lax.axis_index(AXES) & 1

    up_sorted = up_weight.reshape(rows, D, CHUNKS).transpose(0, 2, 1).reshape(rows, FF)
    pack = jnp.concatenate([up_sorted, down_weight.reshape(rows, CHUNKS * D), out_weight], axis=1)
    pack = lax.all_gather(pack, AXES, axis=0, tiled=True)

    small = jnp.stack(
        [query_bias, value_bias, out_bias, first_gain, first_shift, down_bias, second_gain, second_shift], axis=1
    )
    small = jnp.concatenate([small, up_bias.reshape(rows, CHUNKS)], axis=1)
    small = jnp.pad(small, ((0, 0), (0, 4)))
    digits = jnp.concatenate([positives // 128, positives % 128]).astype(BF16)
    digits = jnp.pad(digits[None, :], ((0, rows - 1), (0, 128 - 16 - digits.shape[0])))
    low_half = jnp.concatenate([query_weight, key_weight[:, : D // 2], small, digits], axis=1)
    high_half = jnp.concatenate([key_weight[:, D // 2 :], value_weight, small, digits], axis=1)
    keep = jnp.where(core == 0, low_half, high_half)
    give = jnp.where(core == 0, high_half, low_half)
    both = place([keep[None], swap(give, 1)[None]], core).reshape(2 * rows, -1)
    near = gather_chips(both)
    far = swap(near, 1)

    tail = near[:, HALF:]
    vectors = tail[:, :16].astype(F32).T
    docs_dev = positives.shape[0]
    digits = tail.reshape(size, rows, 128)[:, 0, 16 : 16 + 2 * docs_dev].astype(jnp.int32)
    chosen = (digits[:, :docs_dev] * 128 + digits[:, docs_dev:]).reshape(-1)

    zero = jnp.zeros((D,), F32)
    offset = jnp.concatenate([vectors[0], zero, vectors[1]])[None]
    factor = jnp.concatenate([jnp.full((D,), 0.125, F32), jnp.ones((2 * D,), F32)])[None]
    qkv = project(inputs, near, offset, factor, core, None)
    qkv = project(inputs, far, offset, factor, 1 - core, qkv)

    attended, log_total = attend(cls_positions, qkv)
    hat, inv, low = first_norm(attended, pack, inputs, vectors)
    hidden, slope, hat2, inv2, layer_output, embeddings = feed_forward(cls_positions, low, hat, pack, vectors)

    everyone = gather_rows(embeddings)
    scores, loss, embedding_grad = contrast(embeddings, everyone, doc_flags, chosen)

    mine, other, two, two_low, grads = back_one(
        cls_positions, core, cotangent, embedding_grad, hat2, inv2, low, hidden, slope, pack, vectors
    )
    scatter_one = scatter_steps(mine, other)
    next(scatter_one)
    mine, other, grad_one, grad_attended, grads = back_two(
        core, two, two_low, grads, hat, inv, low, hidden, slope, pack, attended, vectors
    )
    scatter_two = scatter_steps(mine, other)
    next(scatter_two)

    waits = [next(scatter_one), next(scatter_two), next(scatter_one)] if size == 32 else [[], [], []]
    parts = ()
    for g in range(GROUPS):
        parts = attend_back(cls_positions, qkv, grad_attended, log_total, g, parts, waits[g])
    other = weights_back(inputs, *parts, grads, 1 - core)
    mine = weights_back(inputs, *parts, grads, core)
    scatter_late = scatter_steps(mine, other)
    input_grad = inputs_back(grad_one, *parts, near, far, core)

    *_, (up_one, down_one) = scatter_one
    *_, (up_two, down_two) = scatter_two
    *_, (late_low, late_high) = scatter_late
    steps = CHUNKS // 2
    up_grad = jnp.concatenate([up_one, up_two[:, : steps * D]], axis=1)
    down_grad = jnp.concatenate([down_one, down_two[:, : steps * D]], axis=1)
    shard_up = up_grad.reshape(rows, CHUNKS, D).transpose(0, 2, 1).reshape(rows, FF)
    shard_down = down_grad.reshape(rows * CHUNKS, D)
    shard_out = jnp.concatenate([up_two[:, steps * D :], down_two[:, steps * D :]], axis=1)
    vec = late_low[:, HALF:]
    return (
        layer_output,
        embeddings,
        scores,
        loss,
        embedding_grad,
        input_grad,
        late_low[:, :D],
        vec[:, 0],
        jnp.concatenate([late_low[:, D:HALF], late_high[:, : D // 2]], axis=1),
        late_high[:, D // 2 : HALF],
        late_high[:, HALF],
        shard_out,
        vec[:, 2],
        vec[:, 3],
        vec[:, 4],
        shard_up,
        vec[:, 8:12].reshape(-1),
        shard_down,
        vec[:, 5],
        vec[:, 6],
        vec[:, 7],
    )


def solution(mesh):
    split = P(AXES, None)
    vector = P(AXES)
    in_specs = (
        split, split, vector, vector, P(), vector, split, vector, split, split, vector,
        split, vector, vector, vector, split, vector, split, vector, vector, vector,
    )
    out_specs = (
        split, split, split, P(), split, split, split, vector, split, split, vector,
        split, vector, vector, vector, split, vector, split, vector, vector, vector,
    )
    return jax.shard_map(body, mesh=mesh, in_specs=in_specs, out_specs=out_specs, check_vma=False)
```

```python
from functools import partial

import jax
import jax.numpy as jnp
from jax import lax
from jax.experimental import pallas as pl
from jax.experimental.pallas import tpu as pltpu
from jax.sharding import PartitionSpec as P

D = 768
HEADS = 12
HEAD = 64
FF = 3072
ROW = 1024
DOCS = 8
EPSILON = 1e-12
AXES = ("dp", "fsdp")
PAIR = 2 * HEAD
PAIRS = HEADS // 2
QBLOCK = 128
WINDOWS = (256, 384, 512, 1024)
SUB = 1
GROUPS = 2
CHUNKS = FF // D
F32 = jnp.float32
BF16 = jnp.bfloat16
VMEM_LIMIT = 38 * 1024 * 1024
HALF = 3 * D // 2
ANY = pl.BlockSpec(memory_space=pl.ANY)


def dot(left, right):
    return jnp.dot(left, right, preferred_element_type=F32)


def dot_tn(left, right):
    return lax.dot_general(left, right, (((0,), (0,)), ((), ())), preferred_element_type=F32)


def dot_nt(left, right):
    return lax.dot_general(left, right, (((1,), (1,)), ((), ())), preferred_element_type=F32)


def stages_of(size):
    bits = size.bit_length() - 1
    return [(low, min(2, bits - low)) for low in range(1, bits, 2)]


def swap(block, mask):
    size = lax.axis_size(AXES)
    return lax.ppermute(block, AXES, [(i, i ^ mask) for i in range(size)])


def place(pieces, own):
    lead, rows, cols = pieces[0].shape
    out = jnp.zeros((lead, len(pieces), rows, cols), pieces[0].dtype)
    for m, piece in enumerate(pieces):
        out = lax.dynamic_update_slice_in_dim(out, piece[:, None], own ^ m, axis=1)
    return out


def gather_chips(block):
    rows, cols = block.shape
    index = lax.axis_index(AXES)
    block = block[None]
    for low, width in reversed(stages_of(lax.axis_size(AXES))):
        pieces = [block] + [swap(block, m << low) for m in range(1, 1 << width)]
        own = (index >> low) & ((1 << width) - 1)
        block = place(pieces, own).reshape(-1, rows, cols)
    return block.reshape(-1, cols)


def gather_rows(block):
    rows, cols = block.shape
    core = lax.axis_index(AXES) & 1
    both = place([block[None], swap(block, 1)[None]], core)
    return gather_chips(both.reshape(2 * rows, cols))


def added(pieces):
    total = pieces[0].astype(F32)
    for piece in pieces[1:]:
        total = total + piece.astype(F32)
    return total


def after(value, deps):
    return lax.optimization_barrier((value, *deps))[0] if deps else value


class Scatter:
    def __init__(self, mine, other, parts):
        size = lax.axis_size(AXES)
        self.rows = 2 * mine.shape[0] // size
        bits = list(range(size.bit_length() - 2, 0, -1))
        got = swap(other, 1)
        self.parts = []
        for begin, end, order in parts:
            held = [
                piece[:, begin:end].reshape([2] * len(bits) + [self.rows, end - begin]) for piece in (mine, got)
            ]
            self.parts.append([held, list(bits), order(bits)])

    def step(self, deps=()):
        index = lax.axis_index(AXES)
        sums = []
        for part in self.parts:
            held, bits, stages = part
            group = stages.pop(0)
            held[0] = after(held[0], deps)
            others = [b for b in bits if b not in group]

            def cut(piece, m):
                starts = [((index >> b) & 1) ^ ((m >> b) & 1) if b in group else 0 for b in bits] + [0, 0]
                sizes = [1 if b in group else 2 for b in bits] + list(piece.shape[-2:])
                return lax.dynamic_slice(piece, starts, sizes).reshape([2] * len(others) + list(piece.shape[-2:]))

            masks = [0]
            for b in group:
                masks += [m | (1 << b) for m in masks]
            sent = [added([cut(piece, m) for piece in held]).astype(BF16) for m in masks[1:]]
            part[0] = [cut(piece, 0) for piece in held] + [swap(s, m) for s, m in zip(sent, masks[1:])]
            part[1] = others
            sums += sent
        return sums

    def finish(self, deps=()):
        totals = []
        for held, bits, stages in self.parts:
            held[0] = after(held[0], deps)
            totals.append(added(held))
        total = jnp.concatenate(totals, axis=1).reshape(2, self.rows // 2, -1)
        core = lax.axis_index(AXES) & 1
        keep = lax.dynamic_index_in_dim(total, core, 0, False)
        give = lax.dynamic_index_in_dim(total, 1 - core, 0, False).astype(BF16)
        got = swap(give, 1).astype(F32)
        return jnp.where(core == 0, keep, got), jnp.where(core == 0, got, keep)


def down_order(bits):
    pairs = [bits[max(i - 1, 0) : i + 1] for i in range(len(bits) - 1, -1, -2)]
    return [[b] for pair in pairs for b in pair]


def up_order(bits):
    pairs = [bits[max(i - 1, 0) : i + 1] for i in range(len(bits) - 1, -1, -2)]
    return [[b] for pair in pairs for b in reversed(pair)]


def pair_order(bits):
    return [bits[max(i - 1, 0) : i + 1] for i in range(len(bits) - 1, -1, -2)]


def project_kernel(half_ref, x_ref, w_ref, offset_ref, factor_ref, *refs):
    out_ref = refs[-1]
    value = dot(x_ref[...], w_ref[...])
    out_ref[...] = ((value + offset_ref[...]) * factor_ref[...]).astype(BF16)


def project(inputs, weights, offset, factor, half, before):
    block = 256
    extra = [] if before is None else [before]
    return pl.pallas_call(
        project_kernel,
        out_shape=jax.ShapeDtypeStruct((ROW, 3 * D), BF16),
        grid_spec=pltpu.PrefetchScalarGridSpec(
            num_scalar_prefetch=1,
            grid=(ROW // block,),
            in_specs=[
                pl.BlockSpec((block, D), lambda i, h: (i, 0)),
                pl.BlockSpec((D, HALF), lambda i, h: (0, 0)),
                pl.BlockSpec((1, HALF), lambda i, h: (0, h[0])),
                pl.BlockSpec((1, HALF), lambda i, h: (0, h[0])),
            ]
            + [ANY] * len(extra),
            out_specs=pl.BlockSpec((block, HALF), lambda i, h: (i, h[0])),
        ),
        input_output_aliases={} if before is None else {5: 0},
        compiler_params=pltpu.CompilerParams(vmem_limit_bytes=VMEM_LIMIT),
        name="project",
    )(half.reshape(1), inputs, weights, offset, factor, *extra)


def weights_kernel(half_ref, x_ref, q_ref, k_ref, v_ref, grads_ref, *refs):
    out_ref = refs[-1]

    def fill(wide_ref, wide_cols, narrow_cols):
        out_ref[:, wide_cols] = dot_tn(x_ref[...], wide_ref[...]).astype(BF16)
        out_ref[:, narrow_cols] = dot_tn(x_ref[...], k_ref[...]).astype(BF16)
        total = jnp.sum(wide_ref[...].astype(F32), axis=0, keepdims=True)
        table = jnp.concatenate([total, grads_ref[1:16, :], jnp.zeros((112, D), F32)], axis=0)
        out_ref[:, HALF:] = table.T.astype(BF16)

    @pl.when(half_ref[0] == 0)
    def _():
        fill(q_ref, slice(0, D), slice(D, HALF))

    @pl.when(half_ref[0] == 1)
    def _():
        fill(v_ref, slice(D // 2, HALF), slice(0, D // 2))


def weights_back(inputs, dq, dk, dv, grads, half, before):
    fixed = lambda i, h: (0, 0)
    return pl.pallas_call(
        weights_kernel,
        out_shape=jax.ShapeDtypeStruct((D, HALF + 128), BF16),
        grid_spec=pltpu.PrefetchScalarGridSpec(
            num_scalar_prefetch=1,
            grid=(1,),
            in_specs=[
                pl.BlockSpec((ROW, D), fixed),
                pl.BlockSpec((ROW, D), fixed),
                pl.BlockSpec((ROW, D // 2), lambda i, h: (0, h[0])),
                pl.BlockSpec((ROW, D), fixed),
                pl.BlockSpec((16, D), fixed),
            ]
            + [ANY] * len(before),
            out_specs=pl.BlockSpec((D, HALF + 128), fixed),
        ),
        compiler_params=pltpu.CompilerParams(vmem_limit_bytes=VMEM_LIMIT),
        name="weights_back",
    )(half.reshape(1), inputs, dq, dk, dv, grads, *before)


def inputs_kernel(core_ref, one_ref, q_ref, k_ref, v_ref, mine_ref, other_ref, *refs):
    out_ref = refs[-1]

    def fill(low_ref, high_ref):
        half = D // 2
        total = one_ref[...] + dot_nt(q_ref[...], low_ref[:, :D]) + dot_nt(v_ref[...], high_ref[:, half:HALF])
        total = total + dot_nt(k_ref[:, :half], low_ref[:, D:HALF]) + dot_nt(k_ref[:, half:], high_ref[:, :half])
        out_ref[...] = total

    @pl.when(core_ref[0] == 0)
    def _():
        fill(mine_ref, other_ref)

    @pl.when(core_ref[0] == 1)
    def _():
        fill(other_ref, mine_ref)


def inputs_back(grad_one, dq, dk, dv, mine, other, core, before):
    block = 256
    rows = pl.BlockSpec((block, D), lambda i, h: (i, 0))
    weights = pl.BlockSpec((D, HALF), lambda i, h: (0, 0))
    return pl.pallas_call(
        inputs_kernel,
        out_shape=jax.ShapeDtypeStruct((ROW, D), F32),
        grid_spec=pltpu.PrefetchScalarGridSpec(
            num_scalar_prefetch=1,
            grid=(ROW // block,),
            in_specs=[rows, rows, rows, rows, weights, weights] + [ANY] * len(before),
            out_specs=rows,
        ),
        compiler_params=pltpu.CompilerParams(vmem_limit_bytes=VMEM_LIMIT),
        name="inputs_back",
    )(core.reshape(1), grad_one, dq, dk, dv, mine, other, *before)


def row_bounds(cls_ref, places):
    first = jnp.zeros_like(places)
    end = jnp.full_like(places, ROW)
    for d in range(1, DOCS):
        first = jnp.where(places >= cls_ref[d], cls_ref[d], first)
    for d in range(DOCS - 1, 0, -1):
        end = jnp.where(places < cls_ref[d], cls_ref[d], end)
    return first, end


def scalar_bounds(cls_ref, low, high):
    first, end = jnp.int32(0), jnp.int32(ROW)
    for d in range(1, DOCS):
        first = jnp.where(low >= cls_ref[d], cls_ref[d], first)
    for d in range(DOCS - 1, 0, -1):
        end = jnp.where(high < cls_ref[d], cls_ref[d], end)
    return first, end


def over_windows(cls_ref, begin, step):
    low, high = scalar_bounds(cls_ref, begin, begin + QBLOCK - 1)
    low = (low // 16) * 16
    before = None
    for width in WINDOWS:
        start = pl.multiple_of(jnp.minimum(low, ROW - width), 16)
        fits = high <= start + width
        take = fits if before is None else jnp.logical_and(fits, jnp.logical_not(before))
        before = fits if before is None else jnp.logical_or(fits, before)
        pl.when(take)(partial(step, start, width))


def staggered(count, front, middle, finish):
    state = front(0)
    for p in range(count):
        later = front(p + 1) if p + 1 < count else None
        finish(p, middle(p, state))
        state = later


def split_pair(block):
    lane = lax.broadcasted_iota(jnp.int32, block.shape, 1)
    zero = jnp.zeros_like(block)
    return jnp.concatenate(
        [jnp.where(lane < HEAD, block, zero), jnp.where(lane < HEAD, zero, block)], axis=0
    )


def join_pair(both):
    half = both.shape[0] // 2
    lane = lax.broadcasted_iota(jnp.int32, (half, both.shape[1]), 1)
    return jnp.where(lane < HEAD, both[:half], both[half:])


def attend_kernel(cls_ref, q_ref, k_ref, v_ref, out_ref, log_ref):
    @pl.loop(0, SUB)
    def _(s):
        begin = (pl.program_id(0) * SUB + s) * QBLOCK
        rows = pl.ds(pl.multiple_of(s * QBLOCK, QBLOCK), QBLOCK)

        def step(start, width):
            places = begin + lax.broadcasted_iota(jnp.int32, (QBLOCK, 1), 0)
            first, end = row_bounds(cls_ref, places)
            keys = start + lax.broadcasted_iota(jnp.int32, (QBLOCK, width), 1)
            mask = jnp.logical_and(keys >= first, keys < end)
            mask = jnp.concatenate([mask, mask], axis=0)
            lane = lax.broadcasted_iota(jnp.int32, (QBLOCK, 128), 1)
            logs = [jnp.zeros((QBLOCK, 128), F32)]
            window = pl.ds(start, width)

            def front(p):
                cols = slice(PAIR * p, PAIR * (p + 1))
                return dot_nt(split_pair(q_ref[rows, cols]), k_ref[window, cols])

            def middle(p, scores):
                scores = jnp.where(mask, scores, -1000000000.0)
                top = jnp.max(scores, axis=1, keepdims=True)
                weights = jnp.exp(scores - top)
                return top, jnp.sum(weights, axis=1, keepdims=True), weights.astype(BF16)

            def finish(p, state):
                top, total, weights = state
                cols = slice(PAIR * p, PAIR * (p + 1))
                result = dot(weights, v_ref[window, cols]) / total
                out_ref[rows, cols] = join_pair(result).astype(BF16)
                log_total = top + jnp.log(total)
                table = jnp.where(lane == 2 * p, log_total[:QBLOCK], logs[0])
                logs[0] = jnp.where(lane == 2 * p + 1, log_total[QBLOCK:], table)

            staggered(PAIRS, front, middle, finish)
            log_ref[:, rows] = logs[0].T[:16]

        over_windows(cls_ref, begin, step)


def attend(cls, qkv):
    block = SUB * QBLOCK
    return pl.pallas_call(
        attend_kernel,
        out_shape=(
            jax.ShapeDtypeStruct((ROW, D), BF16),
            jax.ShapeDtypeStruct((16, ROW), F32),
        ),
        grid_spec=pltpu.PrefetchScalarGridSpec(
            num_scalar_prefetch=1,
            grid=(ROW // block,),
            in_specs=[
                pl.BlockSpec((block, D), lambda i, c: (i, 0)),
                pl.BlockSpec((ROW, D), lambda i, c: (0, 1)),
                pl.BlockSpec((ROW, D), lambda i, c: (0, 2)),
            ],
            out_specs=[
                pl.BlockSpec((block, D), lambda i, c: (i, 0)),
                pl.BlockSpec((16, block), lambda i, c: (0, i)),
            ],
        ),
        compiler_params=pltpu.CompilerParams(vmem_limit_bytes=VMEM_LIMIT),
        name="attend",
    )(cls, qkv, qkv, qkv)


def attend_back_kernel(base, cls_ref, q_ref, k_ref, v_ref, do_ref, log_ref, *refs):
    dq_ref, dk_ref, dv_ref, dk_sum, dv_sum = refs[-5:]

    @pl.when(pl.program_id(0) == 0)
    def _():
        dk_sum[...] = jnp.zeros_like(dk_sum)
        dv_sum[...] = jnp.zeros_like(dv_sum)

    @pl.loop(0, SUB)
    def _(s):
        begin = (pl.program_id(0) * SUB + s) * QBLOCK
        rows = pl.ds(pl.multiple_of(s * QBLOCK, QBLOCK), QBLOCK)

        def step(start, width):
            places = begin + lax.broadcasted_iota(jnp.int32, (1, QBLOCK), 1)
            first, end = row_bounds(cls_ref, places)
            keys = start + lax.broadcasted_iota(jnp.int32, (width, QBLOCK), 0)
            mask = jnp.logical_and(keys >= first, keys < end)
            mask = jnp.concatenate([mask, mask], axis=1)
            window = pl.ds(start, width)

            def front(p):
                cols = slice(PAIR * p, PAIR * (p + 1))
                queries = split_pair(q_ref[rows, cols])
                grads = split_pair(do_ref[rows, cols])
                return queries, grads, dot_nt(k_ref[window, cols], queries), dot_nt(v_ref[window, cols], grads)

            def middle(p, state):
                queries, grads, scores, grad_weights = state
                h = base + 2 * p
                log_total = jnp.concatenate([log_ref[h : h + 1, rows], log_ref[h + 1 : h + 2, rows]], axis=1)
                weights = jnp.exp(jnp.where(mask, scores - log_total, -1000000000.0))
                inner = jnp.sum(grad_weights * weights, axis=0, keepdims=True)
                grad_scores = (weights * (grad_weights - inner)).astype(BF16)
                return queries, grads, weights.astype(BF16), grad_scores

            def finish(p, state):
                cols = slice(PAIR * p, PAIR * (p + 1))
                queries, grads, weights, grad_scores = state
                dv_sum[window, cols] += dot(weights, grads)
                dk_sum[window, cols] += dot(grad_scores, queries)
                grad_queries = join_pair(dot_tn(grad_scores, k_ref[window, cols]))
                dq_ref[rows, cols] = (grad_queries.astype(BF16).astype(F32) * 0.125).astype(BF16)

            staggered(q_ref.shape[1] // PAIR, front, middle, finish)

        over_windows(cls_ref, begin, step)

    @pl.when(pl.program_id(0) == pl.num_programs(0) - 1)
    def _():
        dk_ref[...] = dk_sum[...].astype(BF16)
        dv_ref[...] = dv_sum[...].astype(BF16)


def attend_back(cls, qkv, grad_attended, log_total, group, earlier, before):
    block = SUB * QBLOCK
    span = D // GROUPS
    shape = jax.ShapeDtypeStruct((ROW, D), BF16)
    extra = list(earlier) + list(before)
    return pl.pallas_call(
        partial(attend_back_kernel, group * (HEADS // GROUPS)),
        out_shape=(shape, shape, shape),
        grid_spec=pltpu.PrefetchScalarGridSpec(
            num_scalar_prefetch=1,
            grid=(ROW // block,),
            in_specs=[
                pl.BlockSpec((block, span), lambda i, c: (i, group)),
                pl.BlockSpec((ROW, span), lambda i, c: (0, GROUPS + group)),
                pl.BlockSpec((ROW, span), lambda i, c: (0, 2 * GROUPS + group)),
                pl.BlockSpec((block, span), lambda i, c: (i, group)),
                pl.BlockSpec((16, block), lambda i, c: (0, i)),
            ]
            + [ANY] * len(extra),
            out_specs=[
                pl.BlockSpec((block, span), lambda i, c: (i, group)),
                pl.BlockSpec((ROW, span), lambda i, c: (0, group)),
                pl.BlockSpec((ROW, span), lambda i, c: (0, group)),
            ],
            scratch_shapes=[pltpu.VMEM((ROW, span), F32), pltpu.VMEM((ROW, span), F32)],
        ),
        input_output_aliases={6 + i: i for i in range(len(earlier))},
        compiler_params=pltpu.CompilerParams(vmem_limit_bytes=VMEM_LIMIT),
        name="attend_back",
    )(cls, qkv, qkv, qkv, grad_attended, log_total, *extra)


def normalized(values):
    centre = jnp.mean(values, axis=-1, keepdims=True)
    centred = values - centre
    spread = jnp.mean(centred * centred, axis=-1, keepdims=True)
    inverse = lax.rsqrt(spread + EPSILON)
    return centred * inverse, inverse


def normalized_back(grad, hat, inverse, gain):
    scaled = grad * gain
    mean_scaled = jnp.mean(scaled, axis=-1, keepdims=True)
    mean_hat = jnp.mean(scaled * hat, axis=-1, keepdims=True)
    return inverse * (scaled - mean_scaled - hat * mean_hat)


def first_kernel(att_ref, w_ref, x_ref, vec_ref, *refs):
    hat_ref, inv_ref, low_ref = refs[-3:]
    residual = x_ref[...].astype(F32) + dot(att_ref[...], w_ref[...]) + vec_ref[2:3, :]
    hat, inverse = normalized(residual)
    hat_ref[...] = hat
    inv_ref[...] = inverse
    low_ref[...] = (hat * vec_ref[3:4, :] + vec_ref[4:5, :]).astype(BF16)


def first_norm(attended, weights, inputs, vectors, before):
    block = 256
    rows = lambda i: (i, 0)
    fixed = lambda i: (0, 0)
    return pl.pallas_call(
        first_kernel,
        out_shape=(
            jax.ShapeDtypeStruct((ROW, D), F32),
            jax.ShapeDtypeStruct((ROW, 1), F32),
            jax.ShapeDtypeStruct((ROW, D), BF16),
        ),
        grid=(ROW // block,),
        in_specs=[
            pl.BlockSpec((block, D), rows),
            pl.BlockSpec((D, D), fixed),
            pl.BlockSpec((block, D), rows),
            pl.BlockSpec((16, D), fixed),
        ]
        + [ANY] * len(before),
        out_specs=[
            pl.BlockSpec((block, D), rows),
            pl.BlockSpec((block, 1), rows),
            pl.BlockSpec((block, D), rows),
        ],
        compiler_params=pltpu.CompilerParams(vmem_limit_bytes=VMEM_LIMIT),
        name="first_norm",
    )(attended, weights, inputs, vectors, *before)


def gelu_parts(v):
    bell = jnp.exp(v * v * -0.5)
    t = 1.0 / (1.0 + (0.3275911 * 0.7071067811865476) * jnp.abs(v))
    poly = t * (0.254829592 + t * (-0.284496736 + t * (1.421413741 + t * (-1.453152027 + t * 1.061405429))))
    tail = 0.5 * poly * bell
    return jnp.where(v >= 0.0, 1.0 - tail, tail), 0.3989422804014327 * bell


def forward_kernel(
    cls_ref, low_ref, hat_ref, up_ref, down_ref, vec_ref, hid_ref, slope_ref, hat2_ref, inv2_ref, out_ref, emb_ref, acc_ref
):
    j = pl.program_id(0)
    block = 256

    @pl.when(j == 0)
    def _():
        acc_ref[...] = hat_ref[...] * vec_ref[3:4, :] + (vec_ref[4:5, :] + vec_ref[5:6, :])

    bias = vec_ref[pl.ds(8 + j, 1), :]

    def front(r):
        return dot(low_ref[block * r : block * (r + 1), :], up_ref[...]) + bias

    def middle(r, value):
        rows = slice(block * r, block * (r + 1))
        phi, density = gelu_parts(value)
        hidden = (value * phi).astype(BF16)
        hid_ref[rows, :] = hidden
        slope_ref[rows, :] = (phi + value * density).astype(BF16)
        return hidden

    def finish(r, hidden):
        acc_ref[block * r : block * (r + 1), :] += dot(hidden, down_ref[...])

    staggered(ROW // block, front, middle, finish)

    @pl.when(j == CHUNKS - 1)
    def _():
        for r in range(ROW // block):
            rows = slice(block * r, block * (r + 1))
            hat, inverse = normalized(acc_ref[rows, :])
            hat2_ref[rows, :] = hat
            inv2_ref[rows, :] = inverse
            full = hat * vec_ref[6:7, :] + vec_ref[7:8, :]
            out_ref[rows, :] = full.astype(BF16)
            acc_ref[rows, :] = full
        picked = [acc_ref[pl.ds(cls_ref[d], 1), :] for d in range(DOCS)]
        emb_ref[...] = jnp.concatenate(picked, axis=0).astype(BF16)


def feed_forward(cls, low, hat, pack, vectors):
    fixed = lambda j, c: (0, 0)
    return pl.pallas_call(
        forward_kernel,
        out_shape=(
            jax.ShapeDtypeStruct((ROW, FF), BF16),
            jax.ShapeDtypeStruct((ROW, FF), BF16),
            jax.ShapeDtypeStruct((ROW, D), F32),
            jax.ShapeDtypeStruct((ROW, 1), F32),
            jax.ShapeDtypeStruct((ROW, D), BF16),
            jax.ShapeDtypeStruct((DOCS, D), BF16),
        ),
        grid_spec=pltpu.PrefetchScalarGridSpec(
            num_scalar_prefetch=1,
            grid=(CHUNKS,),
            in_specs=[
                pl.BlockSpec((ROW, D), fixed),
                pl.BlockSpec((ROW, D), fixed),
                pl.BlockSpec((D, D), lambda j, c: (0, j)),
                pl.BlockSpec((D, D), lambda j, c: (0, CHUNKS + j)),
                pl.BlockSpec((16, D), fixed),
            ],
            out_specs=[
                pl.BlockSpec((ROW, D), lambda j, c: (0, j)),
                pl.BlockSpec((ROW, D), lambda j, c: (0, j)),
                pl.BlockSpec((ROW, D), fixed),
                pl.BlockSpec((ROW, 1), fixed),
                pl.BlockSpec((ROW, D), fixed),
                pl.BlockSpec((DOCS, D), fixed),
            ],
            scratch_shapes=[pltpu.VMEM((ROW, D), F32)],
        ),
        compiler_params=pltpu.CompilerParams(vmem_limit_bytes=VMEM_LIMIT),
        name="feed_forward",
    )(cls, low, hat, pack, pack, vectors)


def chunk_back(core, j, two_low_ref, hid_ref, slope_ref, low_ref, up_ref, down_ref, mine_ref, other_ref, acc_ref, grads_ref, row):
    block = 256
    grad_up = []

    def front(r):
        return dot_nt(two_low_ref[block * r : block * (r + 1), :], down_ref[...])

    def middle(r, grad_hidden):
        part = (grad_hidden * slope_ref[block * r : block * (r + 1), :].astype(F32)).astype(BF16)
        grads_ref[pl.ds(row, 1), :] += jnp.sum(part.astype(F32), axis=0, keepdims=True)
        grad_up.append(part)
        return part

    def finish(r, part):
        acc_ref[block * r : block * (r + 1), :] += dot_nt(part, up_ref[...])

    staggered(ROW // block, front, middle, finish)
    grad_up = jnp.concatenate(grad_up, axis=0)
    cols = pl.ds(pl.multiple_of(j * D, 128), D)
    down_grad = dot_tn(hid_ref[...], two_low_ref[...]).astype(BF16)
    up_grad = dot_tn(low_ref[...], grad_up).astype(BF16)

    @pl.when(core == 0)
    def _():
        mine_ref[:, cols] = up_grad
        other_ref[:, cols] = down_grad

    @pl.when(core == 1)
    def _():
        mine_ref[:, cols] = down_grad
        other_ref[:, cols] = up_grad


def back_one_kernel(
    cls_ref, core_ref, cot_ref, eg_ref, hat2_ref, inv2_ref, low_ref, hid_ref, slope_ref, up_ref, down_ref, vec_ref,
    mine_ref, other_ref, acc_ref, two_low_ref, grads_ref,
):
    j = pl.program_id(0)
    block = 256

    @pl.when(j == 0)
    def _():
        grads_ref[...] = jnp.zeros_like(grads_ref)
        acc_ref[...] = cot_ref[...].astype(F32)
        for d in range(DOCS):
            acc_ref[pl.ds(cls_ref[d], 1), :] += eg_ref[d : d + 1, :]
        for r in range(ROW // block):
            rows = slice(block * r, block * (r + 1))
            grad, hat = acc_ref[rows, :], hat2_ref[rows, :]
            grads_ref[6:7, :] += jnp.sum(grad * hat, axis=0, keepdims=True)
            grads_ref[7:8, :] += jnp.sum(grad, axis=0, keepdims=True)
            two = normalized_back(grad, hat, inv2_ref[rows, :], vec_ref[6:7, :])
            acc_ref[rows, :] = two
            two_low = two.astype(BF16)
            two_low_ref[rows, :] = two_low
            grads_ref[5:6, :] += jnp.sum(two_low.astype(F32), axis=0, keepdims=True)

    chunk_back(
        core_ref[0], j, two_low_ref, hid_ref, slope_ref, low_ref, up_ref, down_ref, mine_ref, other_ref, acc_ref, grads_ref, 8 + j
    )


def back_one(cls, core, cotangent, embedding_grad, hat2, inv2, low, hidden, slope, pack, vectors):
    fixed = lambda j, c, h: (0, 0)
    whole = lambda rows, cols: pl.BlockSpec((rows, cols), fixed)
    steps = CHUNKS // 2
    return pl.pallas_call(
        back_one_kernel,
        out_shape=(
            jax.ShapeDtypeStruct((D, steps * D), BF16),
            jax.ShapeDtypeStruct((D, steps * D), BF16),
            jax.ShapeDtypeStruct((ROW, D), F32),
            jax.ShapeDtypeStruct((ROW, D), BF16),
            jax.ShapeDtypeStruct((16, D), F32),
        ),
        grid_spec=pltpu.PrefetchScalarGridSpec(
            num_scalar_prefetch=2,
            grid=(steps,),
            in_specs=[
                whole(ROW, D),
                whole(DOCS, D),
                whole(ROW, D),
                whole(ROW, 1),
                whole(ROW, D),
                pl.BlockSpec((ROW, D), lambda j, c, h: (0, j)),
                pl.BlockSpec((ROW, D), lambda j, c, h: (0, j)),
                pl.BlockSpec((D, D), lambda j, c, h: (0, j)),
                pl.BlockSpec((D, D), lambda j, c, h: (0, CHUNKS + j)),
                whole(16, D),
            ],
            out_specs=[
                whole(D, steps * D),
                whole(D, steps * D),
                whole(ROW, D),
                whole(ROW, D),
                whole(16, D),
            ],
        ),
        compiler_params=pltpu.CompilerParams(vmem_limit_bytes=VMEM_LIMIT),
        name="back_one",
    )(cls, core.reshape(1), cotangent, embedding_grad, hat2, inv2, low, hidden, slope, pack, pack, vectors)


def back_two_kernel(
    core_ref, two_ref, two_low_ref, grads_in_ref, hat_ref, inv_ref, low_ref, hid_ref, slope_ref, up_ref, down_ref,
    out_w_ref, att_ref, vec_ref, mine_ref, other_ref, one_ref, datt_ref, grads_ref,
):
    j = pl.program_id(0)
    block = 256
    steps = CHUNKS // 2

    @pl.when(j == 0)
    def _():
        grads_ref[...] = grads_in_ref[...]
        one_ref[...] = two_ref[...]

    chunk_back(
        core_ref[0], j, two_low_ref, hid_ref, slope_ref, low_ref, up_ref, down_ref, mine_ref, other_ref, one_ref, grads_ref,
        8 + steps + j,
    )

    @pl.when(j == steps - 1)
    def _():
        lows = []
        for r in range(ROW // block):
            rows = slice(block * r, block * (r + 1))
            grad, hat = one_ref[rows, :], hat_ref[rows, :]
            grads_ref[3:4, :] += jnp.sum(grad * hat, axis=0, keepdims=True)
            grads_ref[4:5, :] += jnp.sum(grad, axis=0, keepdims=True)
            one = normalized_back(grad, hat, inv_ref[rows, :], vec_ref[3:4, :])
            one_ref[rows, :] = one
            one_low = one.astype(BF16)
            lows.append(one_low)
            grads_ref[2:3, :] += jnp.sum(one_low.astype(F32), axis=0, keepdims=True)
            datt_ref[rows, :] = dot_nt(one_low, out_w_ref[...]).astype(BF16)
        grad = dot_tn(att_ref[...], jnp.concatenate(lows, axis=0)).astype(BF16)

        @pl.when(core_ref[0] == 0)
        def _():
            mine_ref[:, steps * D :] = grad[:, : D // 2]
            other_ref[:, steps * D :] = grad[:, D // 2 :]

        @pl.when(core_ref[0] == 1)
        def _():
            mine_ref[:, steps * D :] = grad[:, D // 2 :]
            other_ref[:, steps * D :] = grad[:, : D // 2]


def back_two(core, two, two_low, grads, hat, inv, low, hidden, slope, pack, out_w, attended, vectors):
    fixed = lambda j, h: (0, 0)
    whole = lambda rows, cols: pl.BlockSpec((rows, cols), fixed)
    steps = CHUNKS // 2
    width = steps * D + D // 2
    return pl.pallas_call(
        back_two_kernel,
        out_shape=(
            jax.ShapeDtypeStruct((D, width), BF16),
            jax.ShapeDtypeStruct((D, width), BF16),
            jax.ShapeDtypeStruct((ROW, D), F32),
            jax.ShapeDtypeStruct((ROW, D), BF16),
            jax.ShapeDtypeStruct((16, D), F32),
        ),
        grid_spec=pltpu.PrefetchScalarGridSpec(
            num_scalar_prefetch=1,
            grid=(steps,),
            in_specs=[
                whole(ROW, D),
                whole(ROW, D),
                whole(16, D),
                whole(ROW, D),
                whole(ROW, 1),
                whole(ROW, D),
                pl.BlockSpec((ROW, D), lambda j, h: (0, steps + j)),
                pl.BlockSpec((ROW, D), lambda j, h: (0, steps + j)),
                pl.BlockSpec((D, D), lambda j, h: (0, steps + j)),
                pl.BlockSpec((D, D), lambda j, h: (0, CHUNKS + steps + j)),
                whole(D, D),
                whole(ROW, D),
                whole(16, D),
            ],
            out_specs=[
                whole(D, width),
                whole(D, width),
                whole(ROW, D),
                whole(ROW, D),
                whole(16, D),
            ],
        ),
        compiler_params=pltpu.CompilerParams(vmem_limit_bytes=VMEM_LIMIT),
        name="back_two",
    )(core.reshape(1), two, two_low, grads, hat, inv, low, hidden, slope, pack, pack, out_w, attended, vectors)


def contrast(embeddings, everyone, flags, positives):
    docs_dev, docs_all = embeddings.shape[0], everyone.shape[0]
    begin = lax.axis_index(AXES) * docs_dev
    scale = 2.0 * D ** (-0.5)
    scores = dot_nt(everyone, everyone) * scale
    passage = flags == 0
    masked = jnp.where(passage[None, :], scores, -1000000000.0)
    maxima = jnp.max(masked, axis=1)
    log_sums = maxima + jnp.log(jnp.sum(jnp.exp(masked - maxima[:, None]), axis=1))
    hit_mask = jnp.arange(docs_all, dtype=jnp.int32)[None, :] == positives[:, None]
    picked = jnp.sum(jnp.where(hit_mask, scores, 0.0), axis=1)
    query_rows = flags.astype(F32)
    loss = jnp.sum(query_rows * (log_sums - picked)) / (docs_all // 2)
    chances = jnp.where(passage[None, :], jnp.exp(scores - log_sums[:, None]), 0.0)
    pairs = (query_rows[:, None] * scale * (chances - hit_mask.astype(F32))).astype(BF16)
    own_rows = lax.dynamic_slice_in_dim(pairs, begin, docs_dev, axis=0)
    own_cols = lax.dynamic_slice_in_dim(pairs, begin, docs_dev, axis=1)
    grad = dot(own_rows, everyone) + dot_tn(own_cols, everyone)
    return lax.dynamic_slice_in_dim(scores, begin, docs_dev, axis=0), loss, grad


def body(
    inputs,
    cotangent,
    segment_ids,
    cls_positions,
    doc_flags,
    positives,
    query_weight,
    query_bias,
    key_weight,
    value_weight,
    value_bias,
    out_weight,
    out_bias,
    first_gain,
    first_shift,
    up_weight,
    up_bias,
    down_weight,
    down_bias,
    second_gain,
    second_shift,
):
    rows = query_weight.shape[0]
    size = lax.axis_size(AXES)
    core = lax.axis_index(AXES) & 1

    up_sorted = up_weight.reshape(rows, D, CHUNKS).transpose(0, 2, 1).reshape(rows, FF)
    pack = jnp.concatenate([up_sorted, down_weight.reshape(rows, CHUNKS * D)], axis=1)
    pack = lax.all_gather(pack, AXES, axis=0, tiled=True)

    small = jnp.stack(
        [query_bias, value_bias, out_bias, first_gain, first_shift, down_bias, second_gain, second_shift], axis=1
    )
    small = jnp.concatenate([small, up_bias.reshape(rows, CHUNKS)], axis=1)
    small = jnp.pad(small, ((0, 0), (0, 4)))
    digits = jnp.concatenate([positives // 128, positives % 128]).astype(BF16)
    digits = jnp.pad(digits[None, :], ((0, rows - 1), (0, 128 - 16 - digits.shape[0])))
    half = D // 2
    small = lax.optimization_barrier(jnp.concatenate([small, digits], axis=1))

    def two_ways(left, right):
        return jnp.where(core == 0, left, right), jnp.where(core == 0, right, left)

    keep, give = two_ways(
        jnp.concatenate([query_weight, key_weight[:, :half], out_weight[:, :half]], axis=1),
        jnp.concatenate([key_weight[:, half:], value_weight, out_weight[:, half:]], axis=1),
    )
    keep = jnp.concatenate([keep, small], axis=1)
    give = jnp.concatenate([give, small], axis=1)
    both = place([keep[None], swap(give, 1)[None]], core).reshape(2 * rows, -1)
    near = gather_chips(both)
    far = swap(near, 1)

    tail = near[:, 2 * D :]
    vectors = tail[:, :16].astype(F32).T
    docs_dev = positives.shape[0]
    digits = tail.reshape(size, rows, 128)[:, 0, 16 : 16 + 2 * docs_dev].astype(jnp.int32)
    chosen = (digits[:, :docs_dev] * 128 + digits[:, docs_dev:]).reshape(-1)

    zero = jnp.zeros((D,), F32)
    offset = jnp.concatenate([vectors[0], zero, vectors[1]])[None]
    factor = jnp.concatenate([jnp.full((D,), 0.125, F32), jnp.ones((2 * D,), F32)])[None]
    qkv = project(inputs, near, offset, factor, core, None)
    qkv = project(inputs, far, offset, factor, 1 - core, qkv)

    attended, log_total = attend(cls_positions, qkv)
    out_w = jnp.concatenate(two_ways(near[:, HALF : 2 * D], far[:, HALF : 2 * D]), axis=1)
    hat, inv, low = first_norm(attended, out_w, inputs, vectors, [])
    hidden, slope, hat2, inv2, layer_output, embeddings = feed_forward(cls_positions, low, hat, pack, vectors)

    everyone = gather_rows(embeddings)
    scores, loss, embedding_grad = contrast(embeddings, everyone, doc_flags, chosen)

    mine, other, two, two_low, grads = back_one(
        cls_positions, core, cotangent, embedding_grad, hat2, inv2, low, hidden, slope, pack, vectors
    )
    wide = CHUNKS // 2 * D
    scatter_one = Scatter(mine, other, [(0, wide // 2, down_order), (wide // 2, wide, up_order)])
    mine, other, grad_one, grad_attended, grads = back_two(
        core, two, two_low, grads, hat, inv, low, hidden, slope, pack, out_w, attended, vectors
    )
    sent = scatter_one.step([grads])
    wide = wide + D // 2
    scatter_two = Scatter(mine, other, [(0, 7 * 128, down_order), (7 * 128, wide, up_order)])
    parts = attend_back(cls_positions, qkv, grad_attended, log_total, 0, (), sent)
    sent = scatter_one.step(parts[:1]) + scatter_two.step(parts[:1])
    parts = attend_back(cls_positions, qkv, grad_attended, log_total, 1, parts, sent)
    sent = scatter_one.step(parts[:1]) + scatter_two.step(parts[:1])
    other = weights_back(inputs, *parts, grads, 1 - core, sent)
    mine = weights_back(inputs, *parts, grads, core, [])
    scatter_late = Scatter(mine, other, [(0, HALF + 128, pair_order)])
    sent = scatter_one.step([mine]) + scatter_two.step([mine])
    sent = scatter_late.step(sent)
    input_grad = inputs_back(grad_one, *parts, near, far, core, sent)
    sent = scatter_two.step([input_grad])
    sent = scatter_late.step(sent)
    while scatter_late.parts[0][2]:
        scatter_one.step(), scatter_two.step(), scatter_late.step()
    while scatter_one.parts[0][2]:
        scatter_one.step()
    while scatter_two.parts[0][2]:
        scatter_two.step()
    up_one, down_one = scatter_one.finish(sent)
    up_two, down_two = scatter_two.finish(sent)
    late_low, late_high = scatter_late.finish()
    steps = CHUNKS // 2
    up_grad = jnp.concatenate([up_one, up_two[:, : steps * D]], axis=1)
    down_grad = jnp.concatenate([down_one, down_two[:, : steps * D]], axis=1)
    shard_up = up_grad.reshape(rows, CHUNKS, D).transpose(0, 2, 1).reshape(rows, FF)
    shard_down = down_grad.reshape(rows * CHUNKS, D)
    shard_out = jnp.concatenate([up_two[:, steps * D :], down_two[:, steps * D :]], axis=1)
    vec = late_low[:, HALF:]
    return (
        layer_output,
        embeddings,
        scores,
        loss,
        embedding_grad,
        input_grad,
        late_low[:, :D],
        vec[:, 0],
        jnp.concatenate([late_low[:, D:HALF], late_high[:, : D // 2]], axis=1),
        late_high[:, D // 2 : HALF],
        late_high[:, HALF],
        shard_out,
        vec[:, 2],
        vec[:, 3],
        vec[:, 4],
        shard_up,
        vec[:, 8:12].reshape(-1),
        shard_down,
        vec[:, 5],
        vec[:, 6],
        vec[:, 7],
    )


def solution(mesh):
    split = P(AXES, None)
    vector = P(AXES)
    in_specs = (
        split, split, vector, vector, P(), vector, split, vector, split, split, vector,
        split, vector, vector, vector, split, vector, split, vector, vector, vector,
    )
    out_specs = (
        split, split, split, P(), split, split, split, vector, split, split, vector,
        split, vector, vector, vector, split, vector, split, vector, vector, vector,
    )
    return jax.shard_map(body, mesh=mesh, in_specs=in_specs, out_specs=out_specs, check_vma=False)
```

```python
from functools import partial

import jax
import jax.numpy as jnp
from jax import lax
from jax.experimental import pallas as pl
from jax.experimental.pallas import tpu as pltpu
from jax.sharding import PartitionSpec as P

D = 768
HEADS = 12
HEAD = 64
FF = 3072
ROW = 1024
DOCS = 8
EPSILON = 1e-12
AXES = ("dp", "fsdp")
PAIR = 2 * HEAD
PAIRS = HEADS // 2
QBLOCK = 128
WINDOWS = (256, 384, 512, 1024)
SUB = 1
GROUPS = 3
CHUNKS = FF // D
F32 = jnp.float32
BF16 = jnp.bfloat16
VMEM_LIMIT = 46 * 1024 * 1024
FEED_LIMIT = 46 * 1024 * 1024
HALF = 3 * D // 2
ANY = pl.BlockSpec(memory_space=pl.ANY)


def dot(left, right):
    return jnp.dot(left, right, preferred_element_type=F32)


def dot_tn(left, right):
    return lax.dot_general(left, right, (((0,), (0,)), ((), ())), preferred_element_type=F32)


def dot_nt(left, right):
    return lax.dot_general(left, right, (((1,), (1,)), ((), ())), preferred_element_type=F32)


def stages_of(size):
    bits = size.bit_length() - 1
    return [(low, min(2, bits - low)) for low in range(1, bits, 2)]


def swap(block, mask):
    size = lax.axis_size(AXES)
    return lax.ppermute(block, AXES, [(i, i ^ mask) for i in range(size)])


def place(pieces, own):
    lead, rows, cols = pieces[0].shape
    out = jnp.zeros((lead, len(pieces), rows, cols), pieces[0].dtype)
    for m, piece in enumerate(pieces):
        out = lax.dynamic_update_slice_in_dim(out, piece[:, None], own ^ m, axis=1)
    return out


def gather_chips(block):
    rows, cols = block.shape
    index = lax.axis_index(AXES)
    block = block[None]
    for low, width in reversed(stages_of(lax.axis_size(AXES))):
        pieces = [block] + [swap(block, m << low) for m in range(1, 1 << width)]
        own = (index >> low) & ((1 << width) - 1)
        block = place(pieces, own).reshape(-1, rows, cols)
    return block.reshape(-1, cols)


def gather_rows(block):
    rows, cols = block.shape
    core = lax.axis_index(AXES) & 1
    both = place([block[None], swap(block, 1)[None]], core)
    return gather_chips(both.reshape(2 * rows, cols))


def added(pieces):
    total = pieces[0].astype(F32)
    for piece in pieces[1:]:
        total = total + piece.astype(F32)
    return total


def after(value, deps):
    return lax.optimization_barrier((value, *deps))[0] if deps else value


class Scatter:
    def __init__(self, mine, other, parts):
        size = lax.axis_size(AXES)
        self.rows = 2 * mine.shape[0] // size
        bits = list(range(size.bit_length() - 2, 0, -1))
        got = swap(other, 1)
        self.parts = []
        for begin, end, order in parts:
            held = [piece.reshape([2] * len(bits) + [self.rows, mine.shape[1]]) for piece in (mine, got)]
            self.parts.append([held, list(bits), order(bits), begin, end])

    def step(self, deps=()):
        index = lax.axis_index(AXES)
        sums = []
        for part in self.parts:
            held, bits, stages, begin, end = part
            group = stages.pop(0)
            held[0] = after(held[0], deps)
            others = [b for b in bits if b not in group]

            def cut(piece, m):
                starts = [((index >> b) & 1) ^ ((m >> b) & 1) if b in group else 0 for b in bits]
                starts += [0, 0 if piece.shape[-1] == end - begin else begin]
                tail = [self.rows, end - begin]
                sizes = [1 if b in group else 2 for b in bits] + tail
                return lax.dynamic_slice(piece, starts, sizes).reshape([2] * len(others) + tail)

            masks = [0]
            for b in group:
                masks += [m | (1 << b) for m in masks]
            sent = [added([cut(piece, m) for piece in held]).astype(BF16) for m in masks[1:]]
            part[0] = [cut(piece, 0) for piece in held] + [swap(s, m) for s, m in zip(sent, masks[1:])]
            part[1] = others
            sums += sent
        return sums

    def finish(self, deps=()):
        while self.parts[0][2]:
            self.step()
        totals = []
        for held, *_ in self.parts:
            held[0] = after(held[0], deps)
            totals.append(added(held))
        total = jnp.concatenate(totals, axis=1).reshape(2, self.rows // 2, -1)
        core = lax.axis_index(AXES) & 1
        keep = lax.dynamic_index_in_dim(total, core, 0, False)
        give = lax.dynamic_index_in_dim(total, 1 - core, 0, False).astype(BF16)
        got = swap(give, 1).astype(F32)
        return jnp.where(core == 0, keep, got), jnp.where(core == 0, got, keep), give


def down_order(bits):
    pairs = [bits[max(i - 1, 0) : i + 1] for i in range(len(bits) - 1, -1, -2)]
    return [[b] for pair in pairs for b in pair]


def up_order(bits):
    pairs = [bits[max(i - 1, 0) : i + 1] for i in range(len(bits) - 1, -1, -2)]
    return [[b] for pair in pairs for b in reversed(pair)]


def pair_order(bits):
    return [bits[max(i - 1, 0) : i + 1] for i in range(len(bits) - 1, -1, -2)]


def project_kernel(half_ref, x_ref, w_ref, offset_ref, factor_ref, *refs):
    out_ref = refs[-1]
    value = dot(x_ref[...], w_ref[...])
    out_ref[...] = ((value + offset_ref[...]) * factor_ref[...]).astype(BF16)


def project(inputs, weights, offset, factor, half, before):
    block = 256
    extra = [] if before is None else [before]
    return pl.pallas_call(
        project_kernel,
        out_shape=jax.ShapeDtypeStruct((ROW, 3 * D), BF16),
        grid_spec=pltpu.PrefetchScalarGridSpec(
            num_scalar_prefetch=1,
            grid=(ROW // block,),
            in_specs=[
                pl.BlockSpec((block, D), lambda i, h: (i, 0)),
                pl.BlockSpec((D, HALF), lambda i, h: (0, 0)),
                pl.BlockSpec((1, HALF), lambda i, h: (0, h[0])),
                pl.BlockSpec((1, HALF), lambda i, h: (0, h[0])),
            ]
            + [ANY] * len(extra),
            out_specs=pl.BlockSpec((block, HALF), lambda i, h: (i, h[0])),
        ),
        input_output_aliases={} if before is None else {5: 0},
        compiler_params=pltpu.CompilerParams(vmem_limit_bytes=VMEM_LIMIT),
        name="project",
    )(half.reshape(1), inputs, weights, offset, factor, *extra)


def weights_kernel(half_ref, x_ref, q_ref, k_ref, v_ref, grads_ref, *refs):
    out_ref = refs[-1]

    def fill(wide_ref, wide_cols, narrow_cols):
        out_ref[:, wide_cols] = dot_tn(x_ref[...], wide_ref[...]).astype(BF16)
        out_ref[:, narrow_cols] = dot_tn(x_ref[...], k_ref[...]).astype(BF16)
        total = jnp.sum(wide_ref[...].astype(F32), axis=0, keepdims=True)
        table = jnp.concatenate([total, grads_ref[1:16, :], jnp.zeros((112, D), F32)], axis=0)
        out_ref[:, HALF:] = table.T.astype(BF16)

    @pl.when(half_ref[0] == 0)
    def _():
        fill(q_ref, slice(0, D), slice(D, HALF))

    @pl.when(half_ref[0] == 1)
    def _():
        fill(v_ref, slice(D // 2, HALF), slice(0, D // 2))


def weights_back(inputs, dq, dk, dv, grads, half, before):
    fixed = lambda i, h: (0, 0)
    return pl.pallas_call(
        weights_kernel,
        out_shape=jax.ShapeDtypeStruct((D, HALF + 128), BF16),
        grid_spec=pltpu.PrefetchScalarGridSpec(
            num_scalar_prefetch=1,
            grid=(1,),
            in_specs=[
                pl.BlockSpec((ROW, D), fixed),
                pl.BlockSpec((ROW, D), fixed),
                pl.BlockSpec((ROW, D // 2), lambda i, h: (0, h[0])),
                pl.BlockSpec((ROW, D), fixed),
                pl.BlockSpec((16, D), fixed),
            ]
            + [ANY] * len(before),
            out_specs=pl.BlockSpec((D, HALF + 128), fixed),
        ),
        compiler_params=pltpu.CompilerParams(vmem_limit_bytes=VMEM_LIMIT),
        name="weights_back",
    )(half.reshape(1), inputs, dq, dk, dv, grads, *before)


def inputs_kernel(core_ref, one_ref, q_ref, k_ref, v_ref, mine_ref, other_ref, *refs):
    out_ref = refs[-1]

    def fill(low_ref, high_ref):
        half = D // 2
        total = one_ref[...] + dot_nt(q_ref[...], low_ref[:, :D]) + dot_nt(v_ref[...], high_ref[:, half:HALF])
        total = total + dot_nt(k_ref[:, :half], low_ref[:, D:HALF]) + dot_nt(k_ref[:, half:], high_ref[:, :half])
        out_ref[...] = total

    @pl.when(core_ref[0] == 0)
    def _():
        fill(mine_ref, other_ref)

    @pl.when(core_ref[0] == 1)
    def _():
        fill(other_ref, mine_ref)


def inputs_back(grad_one, dq, dk, dv, mine, other, core, before):
    block = 256
    rows = pl.BlockSpec((block, D), lambda i, h: (i, 0))
    weights = pl.BlockSpec((D, HALF), lambda i, h: (0, 0))
    return pl.pallas_call(
        inputs_kernel,
        out_shape=jax.ShapeDtypeStruct((ROW, D), F32),
        grid_spec=pltpu.PrefetchScalarGridSpec(
            num_scalar_prefetch=1,
            grid=(ROW // block,),
            in_specs=[rows, rows, rows, rows, weights, weights] + [ANY] * len(before),
            out_specs=rows,
        ),
        compiler_params=pltpu.CompilerParams(vmem_limit_bytes=VMEM_LIMIT),
        name="inputs_back",
    )(core.reshape(1), grad_one, dq, dk, dv, mine, other, *before)


def row_bounds(cls_ref, places):
    first = jnp.zeros_like(places)
    end = jnp.full_like(places, ROW)
    for d in range(1, DOCS):
        first = jnp.where(places >= cls_ref[d], cls_ref[d], first)
    for d in range(DOCS - 1, 0, -1):
        end = jnp.where(places < cls_ref[d], cls_ref[d], end)
    return first, end


def scalar_bounds(cls_ref, low, high):
    first, end = jnp.int32(0), jnp.int32(ROW)
    for d in range(1, DOCS):
        first = jnp.where(low >= cls_ref[d], cls_ref[d], first)
    for d in range(DOCS - 1, 0, -1):
        end = jnp.where(high < cls_ref[d], cls_ref[d], end)
    return first, end


def over_windows(cls_ref, begin, step):
    low, high = scalar_bounds(cls_ref, begin, begin + QBLOCK - 1)
    low = (low // 16) * 16
    before = None
    for width in WINDOWS:
        start = pl.multiple_of(jnp.minimum(low, ROW - width), 16)
        fits = high <= start + width
        take = fits if before is None else jnp.logical_and(fits, jnp.logical_not(before))
        before = fits if before is None else jnp.logical_or(fits, before)
        pl.when(take)(partial(step, start, width))


def staggered(count, front, middle, finish):
    state = front(0)
    for p in range(count):
        later = front(p + 1) if p + 1 < count else None
        finish(p, middle(p, state))
        state = later


def split_pair(block):
    lane = lax.broadcasted_iota(jnp.int32, block.shape, 1)
    zero = jnp.zeros_like(block)
    return jnp.concatenate(
        [jnp.where(lane < HEAD, block, zero), jnp.where(lane < HEAD, zero, block)], axis=0
    )


def join_pair(both):
    half = both.shape[0] // 2
    lane = lax.broadcasted_iota(jnp.int32, (half, both.shape[1]), 1)
    return jnp.where(lane < HEAD, both[:half], both[half:])


def attend_kernel(cls_ref, q_ref, k_ref, v_ref, out_ref, log_ref):
    @pl.loop(0, SUB)
    def _(s):
        begin = (pl.program_id(0) * SUB + s) * QBLOCK
        rows = pl.ds(pl.multiple_of(s * QBLOCK, QBLOCK), QBLOCK)

        def step(start, width):
            places = begin + lax.broadcasted_iota(jnp.int32, (QBLOCK, 1), 0)
            first, end = row_bounds(cls_ref, places)
            keys = start + lax.broadcasted_iota(jnp.int32, (QBLOCK, width), 1)
            mask = jnp.logical_and(keys >= first, keys < end)
            mask = jnp.concatenate([mask, mask], axis=0)
            lane = lax.broadcasted_iota(jnp.int32, (QBLOCK, 128), 1)
            logs = [jnp.zeros((QBLOCK, 128), F32)]
            window = pl.ds(start, width)

            def front(p):
                cols = slice(PAIR * p, PAIR * (p + 1))
                return dot_nt(split_pair(q_ref[rows, cols]), k_ref[window, cols])

            def middle(p, scores):
                scores = jnp.where(mask, scores, -1000000000.0)
                top = jnp.max(scores, axis=1, keepdims=True)
                weights = jnp.exp(scores - top)
                return top, jnp.sum(weights, axis=1, keepdims=True), weights.astype(BF16)

            def finish(p, state):
                top, total, weights = state
                cols = slice(PAIR * p, PAIR * (p + 1))
                result = dot(weights, v_ref[window, cols]) / total
                out_ref[rows, cols] = join_pair(result).astype(BF16)
                log_total = top + jnp.log(total)
                table = jnp.where(lane == 2 * p, log_total[:QBLOCK], logs[0])
                logs[0] = jnp.where(lane == 2 * p + 1, log_total[QBLOCK:], table)

            staggered(PAIRS, front, middle, finish)
            log_ref[:, rows] = logs[0].T[:16]

        over_windows(cls_ref, begin, step)


def attend(cls, qkv):
    block = SUB * QBLOCK
    return pl.pallas_call(
        attend_kernel,
        out_shape=(
            jax.ShapeDtypeStruct((ROW, D), BF16),
            jax.ShapeDtypeStruct((16, ROW), F32),
        ),
        grid_spec=pltpu.PrefetchScalarGridSpec(
            num_scalar_prefetch=1,
            grid=(ROW // block,),
            in_specs=[
                pl.BlockSpec((block, D), lambda i, c: (i, 0)),
                pl.BlockSpec((ROW, D), lambda i, c: (0, 1)),
                pl.BlockSpec((ROW, D), lambda i, c: (0, 2)),
            ],
            out_specs=[
                pl.BlockSpec((block, D), lambda i, c: (i, 0)),
                pl.BlockSpec((16, block), lambda i, c: (0, i)),
            ],
        ),
        compiler_params=pltpu.CompilerParams(vmem_limit_bytes=VMEM_LIMIT),
        name="attend",
    )(cls, qkv, qkv, qkv)


def attend_back_kernel(base, cls_ref, q_ref, k_ref, v_ref, do_ref, log_ref, *refs):
    dq_ref, dk_ref, dv_ref, dk_sum, dv_sum = refs[-5:]

    @pl.when(pl.program_id(0) == 0)
    def _():
        dk_sum[...] = jnp.zeros_like(dk_sum)
        dv_sum[...] = jnp.zeros_like(dv_sum)

    @pl.loop(0, SUB)
    def _(s):
        begin = (pl.program_id(0) * SUB + s) * QBLOCK
        rows = pl.ds(pl.multiple_of(s * QBLOCK, QBLOCK), QBLOCK)

        def step(start, width):
            places = begin + lax.broadcasted_iota(jnp.int32, (1, QBLOCK), 1)
            first, end = row_bounds(cls_ref, places)
            keys = start + lax.broadcasted_iota(jnp.int32, (width, QBLOCK), 0)
            mask = jnp.logical_and(keys >= first, keys < end)
            mask = jnp.concatenate([mask, mask], axis=1)
            window = pl.ds(start, width)

            def front(p):
                cols = slice(PAIR * p, PAIR * (p + 1))
                queries = split_pair(q_ref[rows, cols])
                grads = split_pair(do_ref[rows, cols])
                return queries, grads, dot_nt(k_ref[window, cols], queries), dot_nt(v_ref[window, cols], grads)

            def middle(p, state):
                queries, grads, scores, grad_weights = state
                h = base + 2 * p
                log_total = jnp.concatenate([log_ref[h : h + 1, rows], log_ref[h + 1 : h + 2, rows]], axis=1)
                weights = jnp.exp(jnp.where(mask, scores - log_total, -1000000000.0))
                inner = jnp.sum(grad_weights * weights, axis=0, keepdims=True)
                grad_scores = (weights * (grad_weights - inner)).astype(BF16)
                return queries, grads, weights.astype(BF16), grad_scores

            def finish(p, state):
                cols = slice(PAIR * p, PAIR * (p + 1))
                queries, grads, weights, grad_scores = state
                dv_sum[window, cols] += dot(weights, grads)
                dk_sum[window, cols] += dot(grad_scores, queries)
                grad_queries = join_pair(dot_tn(grad_scores, k_ref[window, cols]))
                dq_ref[rows, cols] = (grad_queries.astype(BF16).astype(F32) * 0.125).astype(BF16)

            staggered(q_ref.shape[1] // PAIR, front, middle, finish)

        over_windows(cls_ref, begin, step)

    @pl.when(pl.program_id(0) == pl.num_programs(0) - 1)
    def _():
        dk_ref[...] = dk_sum[...].astype(BF16)
        dv_ref[...] = dv_sum[...].astype(BF16)


def attend_back(cls, qkv, grad_attended, log_total, group, earlier, before):
    block = SUB * QBLOCK
    span = D // GROUPS
    shape = jax.ShapeDtypeStruct((ROW, D), BF16)
    extra = list(earlier) + list(before)
    return pl.pallas_call(
        partial(attend_back_kernel, group * (HEADS // GROUPS)),
        out_shape=(shape, shape, shape),
        grid_spec=pltpu.PrefetchScalarGridSpec(
            num_scalar_prefetch=1,
            grid=(ROW // block,),
            in_specs=[
                pl.BlockSpec((block, span), lambda i, c: (i, group)),
                pl.BlockSpec((ROW, span), lambda i, c: (0, GROUPS + group)),
                pl.BlockSpec((ROW, span), lambda i, c: (0, 2 * GROUPS + group)),
                pl.BlockSpec((block, span), lambda i, c: (i, group)),
                pl.BlockSpec((16, block), lambda i, c: (0, i)),
            ]
            + [ANY] * len(extra),
            out_specs=[
                pl.BlockSpec((block, span), lambda i, c: (i, group)),
                pl.BlockSpec((ROW, span), lambda i, c: (0, group)),
                pl.BlockSpec((ROW, span), lambda i, c: (0, group)),
            ],
            scratch_shapes=[pltpu.VMEM((ROW, span), F32), pltpu.VMEM((ROW, span), F32)],
        ),
        input_output_aliases={6 + i: i for i in range(len(earlier))},
        compiler_params=pltpu.CompilerParams(vmem_limit_bytes=VMEM_LIMIT),
        name="attend_back",
    )(cls, qkv, qkv, qkv, grad_attended, log_total, *extra)


def normalized(values):
    centre = jnp.mean(values, axis=-1, keepdims=True)
    centred = values - centre
    spread = jnp.mean(centred * centred, axis=-1, keepdims=True)
    inverse = lax.rsqrt(spread + EPSILON)
    return centred * inverse, inverse


def normalized_back(grad, hat, inverse, gain):
    scaled = grad * gain
    mean_scaled = jnp.mean(scaled, axis=-1, keepdims=True)
    mean_hat = jnp.mean(scaled * hat, axis=-1, keepdims=True)
    return inverse * (scaled - mean_scaled - hat * mean_hat)


def first_kernel(att_ref, w_ref, x_ref, vec_ref, *refs):
    hat_ref, inv_ref, low_ref = refs[-3:]
    residual = x_ref[...].astype(F32) + dot(att_ref[...], w_ref[...]) + vec_ref[2:3, :]
    hat, inverse = normalized(residual)
    hat_ref[...] = hat.astype(BF16)
    inv_ref[...] = inverse
    low_ref[...] = (hat * vec_ref[3:4, :] + vec_ref[4:5, :]).astype(BF16)


def first_norm(attended, weights, inputs, vectors, before):
    block = 256
    rows = lambda i: (i, 0)
    fixed = lambda i: (0, 0)
    return pl.pallas_call(
        first_kernel,
        out_shape=(
            jax.ShapeDtypeStruct((ROW, D), BF16),
            jax.ShapeDtypeStruct((ROW, 1), F32),
            jax.ShapeDtypeStruct((ROW, D), BF16),
        ),
        grid=(ROW // block,),
        in_specs=[
            pl.BlockSpec((block, D), rows),
            pl.BlockSpec((D, D), fixed),
            pl.BlockSpec((block, D), rows),
            pl.BlockSpec((16, D), fixed),
        ]
        + [ANY] * len(before),
        out_specs=[
            pl.BlockSpec((block, D), rows),
            pl.BlockSpec((block, 1), rows),
            pl.BlockSpec((block, D), rows),
        ],
        compiler_params=pltpu.CompilerParams(vmem_limit_bytes=VMEM_LIMIT),
        name="first_norm",
    )(attended, weights, inputs, vectors, *before)


def gelu_parts(v):
    bell = jnp.exp(v * v * -0.5)
    t = 1.0 / (1.0 + (0.3275911 * 0.7071067811865476) * jnp.abs(v))
    poly = t * (0.254829592 + t * (-0.284496736 + t * (1.421413741 + t * (-1.453152027 + t * 1.061405429))))
    tail = 0.5 * poly * bell
    return jnp.where(v >= 0.0, 1.0 - tail, tail), 0.3989422804014327 * bell


def forward_kernel(
    cls_ref, low_ref, hat_ref, up_ref, down_ref, vec_ref, hid_ref, slope_ref, hat2_ref, inv2_ref, out_ref, emb_ref, acc_ref
):
    j = pl.program_id(0)
    block = 256

    @pl.when(j == 0)
    def _():
        acc_ref[...] = hat_ref[...].astype(F32) * vec_ref[3:4, :] + (vec_ref[4:5, :] + vec_ref[5:6, :])

    bias = vec_ref[pl.ds(8 + j, 1), :]

    def front(r):
        return dot(low_ref[block * r : block * (r + 1), :], up_ref[...]) + bias

    def middle(r, value):
        rows = slice(block * r, block * (r + 1))
        phi, density = gelu_parts(value)
        hidden = (value * phi).astype(BF16)
        hid_ref[rows, :] = hidden
        slope_ref[rows, :] = (phi + value * density).astype(BF16)
        return hidden

    def finish(r, hidden):
        acc_ref[block * r : block * (r + 1), :] += dot(hidden, down_ref[...])

    staggered(ROW // block, front, middle, finish)

    @pl.when(j == CHUNKS - 1)
    def _():
        for r in range(ROW // block):
            rows = slice(block * r, block * (r + 1))
            hat, inverse = normalized(acc_ref[rows, :])
            hat2_ref[rows, :] = hat.astype(BF16)
            inv2_ref[rows, :] = inverse
            full = hat * vec_ref[6:7, :] + vec_ref[7:8, :]
            out_ref[rows, :] = full.astype(BF16)
            acc_ref[rows, :] = full
        picked = [acc_ref[pl.ds(cls_ref[d], 1), :] for d in range(DOCS)]
        emb_ref[...] = jnp.concatenate(picked, axis=0).astype(BF16)


def feed_forward(cls, low, hat, pack, vectors):
    fixed = lambda j, c: (0, 0)
    return pl.pallas_call(
        forward_kernel,
        out_shape=(
            jax.ShapeDtypeStruct((ROW, FF), BF16),
            jax.ShapeDtypeStruct((ROW, FF), BF16),
            jax.ShapeDtypeStruct((ROW, D), BF16),
            jax.ShapeDtypeStruct((ROW, 1), F32),
            jax.ShapeDtypeStruct((ROW, D), BF16),
            jax.ShapeDtypeStruct((DOCS, D), BF16),
        ),
        grid_spec=pltpu.PrefetchScalarGridSpec(
            num_scalar_prefetch=1,
            grid=(CHUNKS,),
            in_specs=[
                pl.BlockSpec((ROW, D), fixed),
                pl.BlockSpec((ROW, D), fixed),
                pl.BlockSpec((D, D), lambda j, c: (0, j)),
                pl.BlockSpec((D, D), lambda j, c: (0, CHUNKS + j)),
                pl.BlockSpec((16, D), fixed),
            ],
            out_specs=[
                pl.BlockSpec((ROW, D), lambda j, c: (0, j)),
                pl.BlockSpec((ROW, D), lambda j, c: (0, j)),
                pl.BlockSpec((ROW, D), fixed),
                pl.BlockSpec((ROW, 1), fixed),
                pl.BlockSpec((ROW, D), fixed),
                pl.BlockSpec((DOCS, D), fixed),
            ],
            scratch_shapes=[pltpu.VMEM((ROW, D), F32)],
        ),
        compiler_params=pltpu.CompilerParams(vmem_limit_bytes=VMEM_LIMIT),
        name="feed_forward",
    )(cls, low, hat, pack, pack, vectors)


def feed_back_kernel(
    cls_ref, core_ref, cot_ref, eg_ref, hat2_ref, inv2_ref, hat_ref, inv_ref, low_ref, hid_ref, slope_ref, up_ref, down_ref,
    vec_ref, mine_ref, other_ref, one_ref, one_low_ref, grads_ref, two_low_ref,
):
    j = pl.program_id(0)
    block = 256
    count = ROW // block
    piece = lambda r: slice(block * r, block * (r + 1))

    @pl.when(j == 0)
    def _():
        grads_ref[...] = jnp.zeros_like(grads_ref)
        one_ref[...] = cot_ref[...].astype(F32)
        for d in range(DOCS):
            one_ref[pl.ds(cls_ref[d], 1), :] += eg_ref[d : d + 1, :]
        for r in range(count):
            rows = piece(r)
            grad, hat = one_ref[rows, :], hat2_ref[rows, :].astype(F32)
            grads_ref[6:7, :] += jnp.sum(grad * hat, axis=0, keepdims=True)
            grads_ref[7:8, :] += jnp.sum(grad, axis=0, keepdims=True)
            two = normalized_back(grad, hat, inv2_ref[rows, :], vec_ref[6:7, :])
            one_ref[rows, :] = two
            two_low = two.astype(BF16)
            two_low_ref[rows, :] = two_low
            grads_ref[5:6, :] += jnp.sum(two_low.astype(F32), axis=0, keepdims=True)

    grad_up = []

    def front(r):
        return dot_nt(two_low_ref[piece(r), :], down_ref[...])

    def middle(r, grad_hidden):
        part = (grad_hidden * slope_ref[piece(r), :].astype(F32)).astype(BF16)
        grads_ref[pl.ds(8 + j, 1), :] += jnp.sum(part.astype(F32), axis=0, keepdims=True)
        grad_up.append(part)
        return part

    def finish(r, part):
        one_ref[piece(r), :] += dot_nt(part, up_ref[...])

    staggered(count, front, middle, finish)
    down_grad = dot_tn(hid_ref[...], two_low_ref[...]).astype(BF16)
    up_grad = dot_tn(low_ref[...], jnp.concatenate(grad_up, axis=0)).astype(BF16)

    @pl.when(core_ref[0] == 0)
    def _():
        mine_ref[...] = up_grad
        other_ref[...] = down_grad

    @pl.when(core_ref[0] == 1)
    def _():
        mine_ref[...] = down_grad
        other_ref[...] = up_grad

    @pl.when(j == CHUNKS - 1)
    def _():
        for r in range(count):
            rows = piece(r)
            grad, hat = one_ref[rows, :], hat_ref[rows, :].astype(F32)
            grads_ref[3:4, :] += jnp.sum(grad * hat, axis=0, keepdims=True)
            grads_ref[4:5, :] += jnp.sum(grad, axis=0, keepdims=True)
            one = normalized_back(grad, hat, inv_ref[rows, :], vec_ref[3:4, :])
            one_ref[rows, :] = one
            one_low = one.astype(BF16)
            one_low_ref[rows, :] = one_low
            grads_ref[2:3, :] += jnp.sum(one_low.astype(F32), axis=0, keepdims=True)


def feed_back(cls, core, cotangent, embedding_grad, hat2, inv2, hat, inv, low, hidden, slope, pack, vectors):
    fixed = lambda j, c, h: (0, 0)
    whole = lambda rows, cols: pl.BlockSpec((rows, cols), fixed)
    chunk = lambda rows, first=0: pl.BlockSpec((rows, D), lambda j, c, h: (0, first + j))
    width = FF + D // 2
    return pl.pallas_call(
        feed_back_kernel,
        out_shape=(
            jax.ShapeDtypeStruct((D, width), BF16),
            jax.ShapeDtypeStruct((D, width), BF16),
            jax.ShapeDtypeStruct((ROW, D), F32),
            jax.ShapeDtypeStruct((ROW, D), BF16),
            jax.ShapeDtypeStruct((16, D), F32),
        ),
        grid_spec=pltpu.PrefetchScalarGridSpec(
            num_scalar_prefetch=2,
            grid=(CHUNKS,),
            in_specs=[
                whole(ROW, D),
                whole(DOCS, D),
                whole(ROW, D),
                whole(ROW, 1),
                whole(ROW, D),
                whole(ROW, 1),
                whole(ROW, D),
                chunk(ROW),
                chunk(ROW),
                chunk(D),
                chunk(D, CHUNKS),
                whole(16, D),
            ],
            out_specs=[chunk(D), chunk(D), whole(ROW, D), whole(ROW, D), whole(16, D)],
            scratch_shapes=[pltpu.VMEM((ROW, D), BF16)],
        ),
        compiler_params=pltpu.CompilerParams(vmem_limit_bytes=FEED_LIMIT),
        name="feed_back",
    )(cls, core.reshape(1), cotangent, embedding_grad, hat2, inv2, hat, inv, low, hidden, slope, pack, pack, vectors)


def out_back_kernel(core_ref, one_low_ref, out_w_ref, att_ref, *refs):
    mine_ref, other_ref, datt_ref = refs[-3:]
    datt_ref[...] = dot_nt(one_low_ref[...], out_w_ref[...]).astype(BF16)
    grad = dot_tn(att_ref[...], one_low_ref[...]).astype(BF16)

    @pl.when(core_ref[0] == 0)
    def _():
        mine_ref[...] = grad[:, : D // 2]
        other_ref[...] = grad[:, D // 2 :]

    @pl.when(core_ref[0] == 1)
    def _():
        mine_ref[...] = grad[:, D // 2 :]
        other_ref[...] = grad[:, : D // 2]


def out_back(core, one_low, out_w, attended, mine, other):
    whole = lambda rows, cols: pl.BlockSpec((rows, cols), lambda i, h: (0, 0))
    last = pl.BlockSpec((D, D // 2), lambda i, h: (0, 2 * CHUNKS))
    return pl.pallas_call(
        out_back_kernel,
        out_shape=(
            jax.ShapeDtypeStruct(mine.shape, BF16),
            jax.ShapeDtypeStruct(other.shape, BF16),
            jax.ShapeDtypeStruct((ROW, D), BF16),
        ),
        grid_spec=pltpu.PrefetchScalarGridSpec(
            num_scalar_prefetch=1,
            grid=(1,),
            in_specs=[whole(ROW, D), whole(D, D), whole(ROW, D), ANY, ANY],
            out_specs=[last, last, whole(ROW, D)],
        ),
        input_output_aliases={4: 0, 5: 1},
        compiler_params=pltpu.CompilerParams(vmem_limit_bytes=VMEM_LIMIT),
        name="out_back",
    )(core.reshape(1), one_low, out_w, attended, mine, other)


def contrast(embeddings, everyone, flags, positives):
    docs_dev, docs_all = embeddings.shape[0], everyone.shape[0]
    begin = lax.axis_index(AXES) * docs_dev
    scale = 2.0 * D ** (-0.5)
    scores = dot_nt(everyone, everyone) * scale
    passage = flags == 0
    masked = jnp.where(passage[None, :], scores, -1000000000.0)
    maxima = jnp.max(masked, axis=1)
    log_sums = maxima + jnp.log(jnp.sum(jnp.exp(masked - maxima[:, None]), axis=1))
    hit_mask = jnp.arange(docs_all, dtype=jnp.int32)[None, :] == positives[:, None]
    picked = jnp.sum(jnp.where(hit_mask, scores, 0.0), axis=1)
    query_rows = flags.astype(F32)
    loss = jnp.sum(query_rows * (log_sums - picked)) / (docs_all // 2)
    chances = jnp.where(passage[None, :], jnp.exp(scores - log_sums[:, None]), 0.0)
    pairs = (query_rows[:, None] * scale * (chances - hit_mask.astype(F32))).astype(BF16)
    own_rows = lax.dynamic_slice_in_dim(pairs, begin, docs_dev, axis=0)
    own_cols = lax.dynamic_slice_in_dim(pairs, begin, docs_dev, axis=1)
    grad = dot(own_rows, everyone) + dot_tn(own_cols, everyone)
    return lax.dynamic_slice_in_dim(scores, begin, docs_dev, axis=0), loss, grad


def body(
    inputs,
    cotangent,
    segment_ids,
    cls_positions,
    doc_flags,
    positives,
    query_weight,
    query_bias,
    key_weight,
    value_weight,
    value_bias,
    out_weight,
    out_bias,
    first_gain,
    first_shift,
    up_weight,
    up_bias,
    down_weight,
    down_bias,
    second_gain,
    second_shift,
):
    rows = query_weight.shape[0]
    size = lax.axis_size(AXES)
    core = lax.axis_index(AXES) & 1

    up_sorted = up_weight.reshape(rows, D, CHUNKS).transpose(0, 2, 1).reshape(rows, FF)
    pack = jnp.concatenate([up_sorted, down_weight.reshape(rows, CHUNKS * D)], axis=1)
    pack = lax.all_gather(pack, AXES, axis=0, tiled=True)

    small = jnp.stack(
        [query_bias, value_bias, out_bias, first_gain, first_shift, down_bias, second_gain, second_shift], axis=1
    )
    small = jnp.concatenate([small, up_bias.reshape(rows, CHUNKS)], axis=1)
    small = jnp.pad(small, ((0, 0), (0, 4)))
    digits = jnp.concatenate([positives // 128, positives % 128]).astype(BF16)
    digits = jnp.pad(digits[None, :], ((0, rows - 1), (0, 128 - 16 - digits.shape[0])))
    half = D // 2
    small = lax.optimization_barrier(jnp.concatenate([small, digits], axis=1))

    def two_ways(left, right):
        return jnp.where(core == 0, left, right), jnp.where(core == 0, right, left)

    keep, give = two_ways(
        jnp.concatenate([query_weight, key_weight[:, :half], out_weight[:, :half]], axis=1),
        jnp.concatenate([key_weight[:, half:], value_weight, out_weight[:, half:]], axis=1),
    )
    keep = jnp.concatenate([keep, small], axis=1)
    give = jnp.concatenate([give, small], axis=1)
    both = place([keep[None], swap(give, 1)[None]], core).reshape(2 * rows, -1)
    near = gather_chips(both)
    far = swap(near, 1)

    tail = near[:, 2 * D :]
    vectors = tail[:, :16].astype(F32).T
    docs_dev = positives.shape[0]
    digits = tail.reshape(size, rows, 128)[:, 0, 16 : 16 + 2 * docs_dev].astype(jnp.int32)
    chosen = (digits[:, :docs_dev] * 128 + digits[:, docs_dev:]).reshape(-1)

    zero = jnp.zeros((D,), F32)
    offset = jnp.concatenate([vectors[0], zero, vectors[1]])[None]
    factor = jnp.concatenate([jnp.full((D,), 0.125, F32), jnp.ones((2 * D,), F32)])[None]
    qkv = project(inputs, near, offset, factor, core, None)
    qkv = project(inputs, far, offset, factor, 1 - core, qkv)

    attended, log_total = attend(cls_positions, qkv)
    out_w = jnp.concatenate(two_ways(near[:, HALF : 2 * D], far[:, HALF : 2 * D]), axis=1)
    hat, inv, low = first_norm(attended, out_w, inputs, vectors, [])
    hidden, slope, hat2, inv2, layer_output, embeddings = feed_forward(cls_positions, low, hat, pack, vectors)

    everyone = gather_rows(embeddings)
    scores, loss, embedding_grad = contrast(embeddings, everyone, doc_flags, chosen)

    mine, other, grad_one, one_low, grads = feed_back(
        cls_positions, core, cotangent, embedding_grad, hat2, inv2, hat, inv, low, hidden, slope, pack, vectors
    )
    mine, other, grad_attended = out_back(core, one_low, out_w, attended, mine, other)
    early = Scatter(mine, other, [(0, 13 * 128, down_order), (13 * 128, 27 * 128, up_order)])
    parts = attend_back(cls_positions, qkv, grad_attended, log_total, 0, (), [])
    sent = early.step(parts[:1])
    for group in range(1, GROUPS):
        parts = attend_back(cls_positions, qkv, grad_attended, log_total, group, parts, sent)
        sent = []
    other = weights_back(inputs, *parts, grads, 1 - core, [])
    mine = weights_back(inputs, *parts, grads, core, [])
    sent = early.step([mine, other])
    late = Scatter(mine, after(other, sent), [(0, HALF + 128, pair_order)])
    sent = late.step(sent)
    input_grad = inputs_back(grad_one, *parts, near, far, core, sent)
    sent = early.step([input_grad])
    sent = late.step(sent)
    sent = early.step(sent)
    early_low, early_high, _ = early.finish()
    late_low, late_high, _ = late.finish()

    shard_up = early_low[:, :FF].reshape(rows, CHUNKS, D).transpose(0, 2, 1).reshape(rows, FF)
    shard_down = early_high[:, :FF].reshape(rows * CHUNKS, D)
    shard_out = jnp.concatenate([early_low[:, FF:], early_high[:, FF:]], axis=1)
    vec = late_low[:, HALF:]
    return (
        layer_output,
        embeddings,
        scores,
        loss,
        embedding_grad,
        input_grad,
        late_low[:, :D],
        vec[:, 0],
        jnp.concatenate([late_low[:, D:HALF], late_high[:, : D // 2]], axis=1),
        late_high[:, D // 2 : HALF],
        late_high[:, HALF],
        shard_out,
        vec[:, 2],
        vec[:, 3],
        vec[:, 4],
        shard_up,
        vec[:, 8:12].reshape(-1),
        shard_down,
        vec[:, 5],
        vec[:, 6],
        vec[:, 7],
    )


def solution(mesh):
    split = P(AXES, None)
    vector = P(AXES)
    in_specs = (
        split, split, vector, vector, P(), vector, split, vector, split, split, vector,
        split, vector, vector, vector, split, vector, split, vector, vector, vector,
    )
    out_specs = (
        split, split, split, P(), split, split, split, vector, split, split, vector,
        split, vector, vector, vector, split, vector, split, vector, vector, vector,
    )
    return jax.shard_map(body, mesh=mesh, in_specs=in_specs, out_specs=out_specs, check_vma=False)
```

```python
from functools import partial

import jax
import jax.numpy as jnp
from jax import lax
from jax.experimental import pallas as pl
from jax.experimental.pallas import tpu as pltpu
from jax.sharding import PartitionSpec as P

D = 768
HEADS = 12
HEAD = 64
FF = 3072
ROW = 1024
DOCS = 8
EPSILON = 1e-12
AXES = ("dp", "fsdp")
PAIR = 2 * HEAD
PAIRS = HEADS // 2
QBLOCK = 128
WINDOWS = (256, 384, 512, 1024)
SUB = 1
GROUPS = ((512, 256), (0, 512))
CHUNKS = FF // D
F32 = jnp.float32
BF16 = jnp.bfloat16
VMEM_LIMIT = 46 * 1024 * 1024
FEED_LIMIT = 46 * 1024 * 1024
HALF = 3 * D // 2
ANY = pl.BlockSpec(memory_space=pl.ANY)


def dot(left, right):
    return jnp.dot(left, right, preferred_element_type=F32)


def dot_tn(left, right):
    return lax.dot_general(left, right, (((0,), (0,)), ((), ())), preferred_element_type=F32)


def dot_nt(left, right):
    return lax.dot_general(left, right, (((1,), (1,)), ((), ())), preferred_element_type=F32)


def stages_of(size):
    bits = size.bit_length() - 1
    return [(low, min(2, bits - low)) for low in range(1, bits, 2)]


def swap(block, mask):
    size = lax.axis_size(AXES)
    return lax.ppermute(block, AXES, [(i, i ^ mask) for i in range(size)])


def place(pieces, own):
    lead, rows, cols = pieces[0].shape
    out = jnp.zeros((lead, len(pieces), rows, cols), pieces[0].dtype)
    for m, piece in enumerate(pieces):
        out = lax.dynamic_update_slice_in_dim(out, piece[:, None], own ^ m, axis=1)
    return out


def gather_chips(block):
    rows, cols = block.shape
    index = lax.axis_index(AXES)
    block = block[None]
    for low, width in reversed(stages_of(lax.axis_size(AXES))):
        pieces = [block] + [swap(block, m << low) for m in range(1, 1 << width)]
        own = (index >> low) & ((1 << width) - 1)
        block = place(pieces, own).reshape(-1, rows, cols)
    return block.reshape(-1, cols)


def gather_halves(block, cut):
    rows, cols = block.shape
    index = lax.axis_index(AXES)
    block = block[None]
    for low, width in reversed(stages_of(lax.axis_size(AXES))[1:]):
        pieces = [block] + [swap(block, m << low) for m in range(1, 1 << width)]
        block = place(pieces, (index >> low) & ((1 << width) - 1)).reshape(-1, rows, cols)
    own_one, own_two = (index >> 1) & 1, (index >> 2) & 1
    left, right = block[:, :, :cut], block[:, :, cut:]
    left = place([left, swap(left, 4)], own_two)
    right = place([right, swap(right, 2)], own_one)
    left, left_far, right, right_far = left[:, :, None], swap(left, 2)[:, :, None], right[:, None], swap(right, 4)[:, None]
    out = jnp.zeros((block.shape[0], 2, 2, rows, cols), block.dtype)
    out = lax.dynamic_update_slice(out, left, (0, 0, own_one, 0, 0))
    out = lax.dynamic_update_slice(out, left_far, (0, 0, 1 - own_one, 0, 0))
    out = lax.dynamic_update_slice(out, right, (0, own_two, 0, 0, cut))
    out = lax.dynamic_update_slice(out, right_far, (0, 1 - own_two, 0, 0, cut))
    return out.reshape(-1, cols)


def gather_rows(block):
    rows, cols = block.shape
    core = lax.axis_index(AXES) & 1
    both = place([block[None], swap(block, 1)[None]], core)
    return gather_chips(both.reshape(2 * rows, cols))


def added(pieces):
    total = pieces[0].astype(F32)
    for piece in pieces[1:]:
        total = total + piece.astype(F32)
    return total


def after(value, deps):
    return lax.optimization_barrier((value, *deps))[0] if deps else value


class Scatter:
    def __init__(self, mine, other, parts):
        size = lax.axis_size(AXES)
        self.rows = 2 * mine.shape[0] // size
        bits = list(range(size.bit_length() - 2, 0, -1))
        got = swap(other, 1)
        self.parts = []
        for begin, end, order in parts:
            held = [
                (piece.reshape([2] * len(bits) + [self.rows, mine.shape[1]]), list(bits), begin)
                for piece in (mine, got)
            ]
            self.parts.append([held, list(bits), order(bits), end - begin])

    def cut(self, part, group, m, deps):
        index = lax.axis_index(AXES)
        held, open_bits, _, width = part
        total = None
        for i, (piece, bits, begin) in enumerate(held):
            piece = after(piece, deps) if i == 0 else piece
            left = [b in open_bits and b not in group for b in bits]
            starts = [0 if free else ((index ^ m) >> b) & 1 for b, free in zip(bits, left)] + [0, begin]
            sizes = [2 if free else 1 for free in left] + [self.rows, width]
            shape = [2] * sum(left) + [self.rows, width]
            piece = lax.dynamic_slice(piece, starts, sizes).reshape(shape).astype(F32)
            total = piece if total is None else total + piece
        return total

    def step(self, deps=()):
        sums = []
        for part in self.parts:
            group = part[2].pop(0)
            masks = [0]
            for b in group:
                masks += [m | (1 << b) for m in masks]
            sent = [self.cut(part, group, m, deps).astype(BF16) for m in masks[1:]]
            part[1] = [b for b in part[1] if b not in group]
            part[0] = part[0] + [(swap(s, m), list(part[1]), 0) for s, m in zip(sent, masks[1:])]
            sums += sent
        return sums

    def last(self, deps=()):
        while self.parts[0][2]:
            self.step()
        totals = [self.cut(part, [], 0, deps) for part in self.parts]
        total = jnp.concatenate(totals, axis=1).reshape(2, self.rows // 2, -1)
        core = lax.axis_index(AXES) & 1
        keep = lax.dynamic_index_in_dim(total, core, 0, False)
        give = lax.dynamic_index_in_dim(total, 1 - core, 0, False).astype(BF16)
        return keep, swap(give, 1), give


def down_order(bits):
    pairs = [bits[max(i - 1, 0) : i + 1] for i in range(len(bits) - 1, -1, -2)]
    return [[b] for pair in pairs for b in pair]


def up_order(bits):
    pairs = [bits[max(i - 1, 0) : i + 1] for i in range(len(bits) - 1, -1, -2)]
    return [[b] for pair in pairs for b in reversed(pair)]


def pair_order(bits):
    return [bits[max(i - 1, 0) : i + 1] for i in range(len(bits) - 1, -1, -2)]


def project_kernel(half_ref, x_ref, w_ref, offset_ref, factor_ref, *refs):
    out_ref = refs[-1]
    value = dot(x_ref[...], w_ref[...])
    out_ref[...] = ((value + offset_ref[...]) * factor_ref[...]).astype(BF16)


def project(inputs, weights, offset, factor, half, before):
    block = 256
    extra = [] if before is None else [before]
    return pl.pallas_call(
        project_kernel,
        out_shape=jax.ShapeDtypeStruct((ROW, 3 * D), BF16),
        grid_spec=pltpu.PrefetchScalarGridSpec(
            num_scalar_prefetch=1,
            grid=(ROW // block,),
            in_specs=[
                pl.BlockSpec((block, D), lambda i, h: (i, 0)),
                pl.BlockSpec((D, HALF), lambda i, h: (0, 0)),
                pl.BlockSpec((1, HALF), lambda i, h: (0, h[0])),
                pl.BlockSpec((1, HALF), lambda i, h: (0, h[0])),
            ]
            + [ANY] * len(extra),
            out_specs=pl.BlockSpec((block, HALF), lambda i, h: (i, h[0])),
        ),
        input_output_aliases={} if before is None else {5: 0},
        compiler_params=pltpu.CompilerParams(vmem_limit_bytes=VMEM_LIMIT),
        name="project",
    )(half.reshape(1), inputs, weights, offset, factor, *extra)


def weights_kernel(core_ref, x_ref, q_ref, k_ref, v_ref, grads_ref, mine_ref, other_ref):
    half = D // 2
    inputs = x_ref[...]

    def table_of(values):
        total = jnp.sum(values.astype(F32), axis=0, keepdims=True)
        return jnp.concatenate([total, grads_ref[1:16, :], jnp.zeros((112, D), F32)], axis=0).T.astype(BF16)

    def fill(low_ref, high_ref):
        low_ref[:, :D] = dot_tn(inputs, q_ref[...]).astype(BF16)
        high_ref[:, half:HALF] = dot_tn(inputs, v_ref[...]).astype(BF16)
        keys = dot_tn(inputs, k_ref[...]).astype(BF16)
        low_ref[:, D:HALF] = keys[:, :half]
        high_ref[:, :half] = keys[:, half:]
        low_ref[:, HALF:] = table_of(q_ref[...])
        high_ref[:, HALF:] = table_of(v_ref[...])

    @pl.when(core_ref[0] == 0)
    def _():
        fill(mine_ref, other_ref)

    @pl.when(core_ref[0] == 1)
    def _():
        fill(other_ref, mine_ref)


def weights_back(inputs, dq, dk, dv, grads, core):
    whole = lambda rows, cols: pl.BlockSpec((rows, cols), lambda i, h: (0, 0))
    shape = jax.ShapeDtypeStruct((D, HALF + 128), BF16)
    return pl.pallas_call(
        weights_kernel,
        out_shape=(shape, shape),
        grid_spec=pltpu.PrefetchScalarGridSpec(
            num_scalar_prefetch=1,
            grid=(1,),
            in_specs=[whole(ROW, D)] * 4 + [whole(16, D)],
            out_specs=[whole(D, HALF + 128)] * 2,
        ),
        compiler_params=pltpu.CompilerParams(vmem_limit_bytes=VMEM_LIMIT),
        name="weights_back",
    )(core.reshape(1), inputs, dq, dk, dv, grads)


def thirds(values, axis):
    terms = []
    for _ in range(3):
        terms.append(values.astype(BF16))
        values = values - terms[-1].astype(F32)
    return jnp.concatenate(terms, axis=axis)


def ones_at(rows, cols, rule):
    shape = (rows, cols)
    row, col = lax.broadcasted_iota(jnp.int32, shape, 0), lax.broadcasted_iota(jnp.int32, shape, 1)
    return rule(row, col).astype(F32).astype(BF16)


def final_kernel(core_ref, early_keep, early_got, late_keep, late_got, *outs):
    up_ref, down_ref, out_ref, q_ref, k_ref, v_ref, *vectors, hidden_ref = outs
    half = D // 2
    rows = q_ref.shape[0]
    group = CHUNKS * 128

    def fill(early_first, early_second, first, second):
        weave = ones_at(group, group, lambda r, c: c == (r % 128) * CHUNKS + r // 128)
        pieces = []
        for g in range(FF // group):
            parts = [early_first[:, D * j + 128 * g : D * j + 128 * (g + 1)].astype(F32) for j in range(CHUNKS)]
            pieces.append(thirds(jnp.concatenate(parts, axis=1), 0))
        woven = dot(jnp.concatenate(pieces, axis=0), weave)
        for g in range(FF // group):
            total = None
            for i in range(3):
                piece = woven[rows * (3 * g + i) : rows * (3 * g + i + 1)]
                total = piece if total is None else total + piece
            up_ref[:, group * g : group * (g + 1)] = total
        for j in range(CHUNKS):
            spread = ones_at(rows * CHUNKS, rows, lambda r, c, j=j: r == c * CHUNKS + j)
            spread = jnp.concatenate([spread] * 3, axis=1)
            piece = dot(spread, thirds(early_second[:, D * j : D * (j + 1)].astype(F32), 0))
            down_ref[...] = piece if j == 0 else down_ref[...] + piece
        out_ref[:, :half] = early_first[:, FF:].astype(F32)
        out_ref[:, half:] = early_second[:, FF:].astype(F32)
        q_ref[...] = first[:, :D].astype(F32)
        k_ref[:, :half] = first[:, D:HALF].astype(F32)
        k_ref[:, half:] = second[:, :half].astype(F32)
        v_ref[...] = second[:, half:HALF].astype(F32)
        same = ones_at(rows, rows, lambda r, c: r == c)
        same = jnp.concatenate([same] * 3, axis=0)
        low = dot_tn(thirds(first[:, HALF:].astype(F32), 0), same)
        high = dot_tn(thirds(second[:, HALF:].astype(F32), 0), same)
        table = [low[0:1], high[0:1]] + [low[i : i + 1] for i in range(2, 8)]
        for ref, row in zip(vectors, table):
            ref[...] = row
        total = None
        for j in range(CHUNKS):
            spread = ones_at(rows, rows * CHUNKS, lambda r, c, j=j: c == r * CHUNKS + j)
            spread = jnp.concatenate([spread] * 3, axis=0)
            piece = dot(thirds(low[8 + j : 9 + j], 1), spread)
            total = piece if total is None else total + piece
        hidden_ref[...] = total

    @pl.when(core_ref[0] == 0)
    def _():
        fill(early_keep, early_got, late_keep, late_got)

    @pl.when(core_ref[0] == 1)
    def _():
        fill(early_got, early_keep, late_got, late_keep)


def final_parts(core, early_keep, early_got, late_keep, late_got):
    rows = late_keep.shape[0]
    shapes = [(rows, FF), (rows * CHUNKS, D)] + [(rows, D)] * 4 + [(1, rows)] * 8 + [(1, rows * CHUNKS)]
    whole = lambda shape: pl.BlockSpec(shape, lambda i, h: (0, 0))
    arrays = (early_keep, early_got, late_keep, late_got)
    return pl.pallas_call(
        final_kernel,
        out_shape=[jax.ShapeDtypeStruct(shape, F32) for shape in shapes],
        grid_spec=pltpu.PrefetchScalarGridSpec(
            num_scalar_prefetch=1,
            grid=(1,),
            in_specs=[whole(array.shape) for array in arrays],
            out_specs=[whole(shape) for shape in shapes],
        ),
        compiler_params=pltpu.CompilerParams(vmem_limit_bytes=VMEM_LIMIT),
        name="final_parts",
    )(core.reshape(1), *arrays)


def inputs_kernel(core_ref, one_ref, q_ref, k_ref, v_ref, mine_ref, other_ref, *refs):
    out_ref = refs[-1]

    def fill(low_ref, high_ref):
        half = D // 2
        total = one_ref[...] + dot_nt(q_ref[...], low_ref[:, :D]) + dot_nt(v_ref[...], high_ref[:, half:HALF])
        total = total + dot_nt(k_ref[:, :half], low_ref[:, D:HALF]) + dot_nt(k_ref[:, half:], high_ref[:, :half])
        out_ref[...] = total

    @pl.when(core_ref[0] == 0)
    def _():
        fill(mine_ref, other_ref)

    @pl.when(core_ref[0] == 1)
    def _():
        fill(other_ref, mine_ref)


def inputs_back(grad_one, dq, dk, dv, mine, other, core, before):
    block = 256
    rows = pl.BlockSpec((block, D), lambda i, h: (i, 0))
    weights = pl.BlockSpec((D, HALF), lambda i, h: (0, 0))
    return pl.pallas_call(
        inputs_kernel,
        out_shape=jax.ShapeDtypeStruct((ROW, D), F32),
        grid_spec=pltpu.PrefetchScalarGridSpec(
            num_scalar_prefetch=1,
            grid=(ROW // block,),
            in_specs=[rows, rows, rows, rows, weights, weights] + [ANY] * len(before),
            out_specs=rows,
        ),
        compiler_params=pltpu.CompilerParams(vmem_limit_bytes=VMEM_LIMIT),
        name="inputs_back",
    )(core.reshape(1), grad_one, dq, dk, dv, mine, other, *before)


def row_bounds(cls_ref, places):
    first = jnp.zeros_like(places)
    end = jnp.full_like(places, ROW)
    for d in range(1, DOCS):
        first = jnp.where(places >= cls_ref[d], cls_ref[d], first)
    for d in range(DOCS - 1, 0, -1):
        end = jnp.where(places < cls_ref[d], cls_ref[d], end)
    return first, end


def scalar_bounds(cls_ref, low, high):
    first, end = jnp.int32(0), jnp.int32(ROW)
    for d in range(1, DOCS):
        first = jnp.where(low >= cls_ref[d], cls_ref[d], first)
    for d in range(DOCS - 1, 0, -1):
        end = jnp.where(high < cls_ref[d], cls_ref[d], end)
    return first, end


def over_windows(cls_ref, begin, step):
    low, high = scalar_bounds(cls_ref, begin, begin + QBLOCK - 1)
    low = (low // 16) * 16
    before = None
    for width in WINDOWS:
        start = pl.multiple_of(jnp.minimum(low, ROW - width), 16)
        fits = high <= start + width
        take = fits if before is None else jnp.logical_and(fits, jnp.logical_not(before))
        before = fits if before is None else jnp.logical_or(fits, before)
        pl.when(take)(partial(step, start, width))


def staggered(count, front, middle, finish):
    state = front(0)
    for p in range(count):
        later = front(p + 1) if p + 1 < count else None
        finish(p, middle(p, state))
        state = later


def split_pair(block):
    lane = lax.broadcasted_iota(jnp.int32, block.shape, 1)
    zero = jnp.zeros_like(block)
    return jnp.concatenate(
        [jnp.where(lane < HEAD, block, zero), jnp.where(lane < HEAD, zero, block)], axis=0
    )


def join_pair(both):
    half = both.shape[0] // 2
    lane = lax.broadcasted_iota(jnp.int32, (half, both.shape[1]), 1)
    return jnp.where(lane < HEAD, both[:half], both[half:])


def attend_kernel(cls_ref, q_ref, k_ref, v_ref, out_ref, log_ref):
    @pl.loop(0, SUB)
    def _(s):
        begin = (pl.program_id(0) * SUB + s) * QBLOCK
        rows = pl.ds(pl.multiple_of(s * QBLOCK, QBLOCK), QBLOCK)

        def step(start, width):
            places = begin + lax.broadcasted_iota(jnp.int32, (QBLOCK, 1), 0)
            first, end = row_bounds(cls_ref, places)
            keys = start + lax.broadcasted_iota(jnp.int32, (QBLOCK, width), 1)
            mask = jnp.logical_and(keys >= first, keys < end)
            mask = jnp.concatenate([mask, mask], axis=0)
            lane = lax.broadcasted_iota(jnp.int32, (QBLOCK, 128), 1)
            logs = [jnp.zeros((QBLOCK, 128), F32)]
            window = pl.ds(start, width)

            def front(p):
                cols = slice(PAIR * p, PAIR * (p + 1))
                return dot_nt(split_pair(q_ref[rows, cols]), k_ref[window, cols])

            def middle(p, scores):
                scores = jnp.where(mask, scores, -1000000000.0)
                top = jnp.max(scores, axis=1, keepdims=True)
                weights = jnp.exp(scores - top)
                return top, jnp.sum(weights, axis=1, keepdims=True), weights.astype(BF16)

            def finish(p, state):
                top, total, weights = state
                cols = slice(PAIR * p, PAIR * (p + 1))
                result = dot(weights, v_ref[window, cols]) / total
                out_ref[rows, cols] = join_pair(result).astype(BF16)
                log_total = top + jnp.log(total)
                table = jnp.where(lane == 2 * p, log_total[:QBLOCK], logs[0])
                logs[0] = jnp.where(lane == 2 * p + 1, log_total[QBLOCK:], table)

            staggered(PAIRS, front, middle, finish)
            log_ref[:, rows] = logs[0].T[:16]

        over_windows(cls_ref, begin, step)


def attend(cls, qkv):
    block = SUB * QBLOCK
    return pl.pallas_call(
        attend_kernel,
        out_shape=(
            jax.ShapeDtypeStruct((ROW, D), BF16),
            jax.ShapeDtypeStruct((16, ROW), F32),
        ),
        grid_spec=pltpu.PrefetchScalarGridSpec(
            num_scalar_prefetch=1,
            grid=(ROW // block,),
            in_specs=[
                pl.BlockSpec((block, D), lambda i, c: (i, 0)),
                pl.BlockSpec((ROW, D), lambda i, c: (0, 1)),
                pl.BlockSpec((ROW, D), lambda i, c: (0, 2)),
            ],
            out_specs=[
                pl.BlockSpec((block, D), lambda i, c: (i, 0)),
                pl.BlockSpec((16, block), lambda i, c: (0, i)),
            ],
        ),
        compiler_params=pltpu.CompilerParams(vmem_limit_bytes=VMEM_LIMIT),
        name="attend",
    )(cls, qkv, qkv, qkv)


def attend_back_kernel(base, cls_ref, q_ref, k_ref, v_ref, do_ref, log_ref, *refs):
    dq_ref, dk_ref, dv_ref, dk_sum, dv_sum = refs[-5:]

    @pl.when(pl.program_id(0) == 0)
    def _():
        dk_sum[...] = jnp.zeros_like(dk_sum)
        dv_sum[...] = jnp.zeros_like(dv_sum)

    @pl.loop(0, SUB)
    def _(s):
        begin = (pl.program_id(0) * SUB + s) * QBLOCK
        rows = pl.ds(pl.multiple_of(s * QBLOCK, QBLOCK), QBLOCK)

        def step(start, width):
            places = begin + lax.broadcasted_iota(jnp.int32, (1, QBLOCK), 1)
            first, end = row_bounds(cls_ref, places)
            keys = start + lax.broadcasted_iota(jnp.int32, (width, QBLOCK), 0)
            mask = jnp.logical_and(keys >= first, keys < end)
            mask = jnp.concatenate([mask, mask], axis=1)
            window = pl.ds(start, width)

            def front(p):
                cols = slice(PAIR * p, PAIR * (p + 1))
                queries = split_pair(q_ref[rows, cols])
                grads = split_pair(do_ref[rows, cols])
                return queries, grads, dot_nt(k_ref[window, cols], queries), dot_nt(v_ref[window, cols], grads)

            def middle(p, state):
                queries, grads, scores, grad_weights = state
                h = base + 2 * p
                log_total = jnp.concatenate([log_ref[h : h + 1, rows], log_ref[h + 1 : h + 2, rows]], axis=1)
                weights = jnp.exp(jnp.where(mask, scores - log_total, -1000000000.0))
                inner = jnp.sum(grad_weights * weights, axis=0, keepdims=True)
                grad_scores = (weights * (grad_weights - inner)).astype(BF16)
                return queries, grads, weights.astype(BF16), grad_scores

            def finish(p, state):
                cols = slice(PAIR * p, PAIR * (p + 1))
                queries, grads, weights, grad_scores = state
                dv_sum[window, cols] += dot(weights, grads)
                dk_sum[window, cols] += dot(grad_scores, queries)
                grad_queries = join_pair(dot_tn(grad_scores, k_ref[window, cols]))
                dq_ref[rows, cols] = (grad_queries.astype(BF16).astype(F32) * 0.125).astype(BF16)

            staggered(dq_ref.shape[1] // PAIR, front, middle, finish)

        over_windows(cls_ref, begin, step)

    @pl.when(pl.program_id(0) == pl.num_programs(0) - 1)
    def _():
        dk_ref[...] = dk_sum[...].astype(BF16)
        dv_ref[...] = dv_sum[...].astype(BF16)


def attend_back(cls, qkv, grad_attended, log_total, group, earlier, before):
    block = SUB * QBLOCK
    begin, span = group
    wide = span if D % span == 0 else D
    across, place = D // wide, begin // wide
    shape = jax.ShapeDtypeStruct((ROW, D), BF16)
    extra = list(earlier) + list(before)
    return pl.pallas_call(
        partial(attend_back_kernel, begin // HEAD),
        out_shape=(shape, shape, shape),
        grid_spec=pltpu.PrefetchScalarGridSpec(
            num_scalar_prefetch=1,
            grid=(ROW // block,),
            in_specs=[
                pl.BlockSpec((block, wide), lambda i, c: (i, place)),
                pl.BlockSpec((ROW, wide), lambda i, c: (0, across + place)),
                pl.BlockSpec((ROW, wide), lambda i, c: (0, 2 * across + place)),
                pl.BlockSpec((block, wide), lambda i, c: (i, place)),
                pl.BlockSpec((16, block), lambda i, c: (0, i)),
            ]
            + [ANY] * len(extra),
            out_specs=[
                pl.BlockSpec((block, span), lambda i, c: (i, begin // span)),
                pl.BlockSpec((ROW, span), lambda i, c: (0, begin // span)),
                pl.BlockSpec((ROW, span), lambda i, c: (0, begin // span)),
            ],
            scratch_shapes=[pltpu.VMEM((ROW, span), F32), pltpu.VMEM((ROW, span), F32)],
        ),
        input_output_aliases={6 + i: i for i in range(len(earlier))},
        compiler_params=pltpu.CompilerParams(vmem_limit_bytes=VMEM_LIMIT),
        name="attend_back",
    )(cls, qkv, qkv, qkv, grad_attended, log_total, *extra)


def normalized(values):
    centre = jnp.mean(values, axis=-1, keepdims=True)
    centred = values - centre
    spread = jnp.mean(centred * centred, axis=-1, keepdims=True)
    inverse = lax.rsqrt(spread + EPSILON)
    return centred * inverse, inverse


def normalized_back(grad, hat, inverse, gain):
    scaled = grad * gain
    mean_scaled = jnp.mean(scaled, axis=-1, keepdims=True)
    mean_hat = jnp.mean(scaled * hat, axis=-1, keepdims=True)
    return inverse * (scaled - mean_scaled - hat * mean_hat)


def first_kernel(att_ref, w_ref, x_ref, vec_ref, *refs):
    hat_ref, inv_ref, low_ref = refs[-3:]
    residual = x_ref[...].astype(F32) + dot(att_ref[...], w_ref[...]) + vec_ref[2:3, :]
    hat, inverse = normalized(residual)
    hat_ref[...] = hat.astype(BF16)
    inv_ref[...] = inverse
    low_ref[...] = (hat * vec_ref[3:4, :] + vec_ref[4:5, :]).astype(BF16)


def first_norm(attended, weights, inputs, vectors, before):
    block = 256
    rows = lambda i: (i, 0)
    fixed = lambda i: (0, 0)
    return pl.pallas_call(
        first_kernel,
        out_shape=(
            jax.ShapeDtypeStruct((ROW, D), BF16),
            jax.ShapeDtypeStruct((ROW, 1), F32),
            jax.ShapeDtypeStruct((ROW, D), BF16),
        ),
        grid=(ROW // block,),
        in_specs=[
            pl.BlockSpec((block, D), rows),
            pl.BlockSpec((D, D), fixed),
            pl.BlockSpec((block, D), rows),
            pl.BlockSpec((16, D), fixed),
        ]
        + [ANY] * len(before),
        out_specs=[
            pl.BlockSpec((block, D), rows),
            pl.BlockSpec((block, 1), rows),
            pl.BlockSpec((block, D), rows),
        ],
        compiler_params=pltpu.CompilerParams(vmem_limit_bytes=VMEM_LIMIT),
        name="first_norm",
    )(attended, weights, inputs, vectors, *before)


def gelu_parts(v):
    bell = jnp.exp2(v * v * -0.7213475204444817)
    t = 1.0 / (1.0 + (0.3275911 * 0.7071067811865476) * jnp.abs(v))
    poly = t * (0.127414796 + t * (-0.142248368 + t * (0.7107068705 + t * (-0.7265760135 + t * 0.5307027145))))
    tail = poly * bell
    return jnp.where(v >= 0.0, 1.0 - tail, tail), 0.3989422804014327 * bell


def forward_kernel(
    cls_ref, low_ref, hat_ref, up_ref, down_ref, vec_ref, hid_ref, slope_ref, hat2_ref, inv2_ref, out_ref, emb_ref, acc_ref
):
    j = pl.program_id(0)
    block = 256

    @pl.when(j == 0)
    def _():
        acc_ref[...] = hat_ref[...].astype(F32) * vec_ref[3:4, :] + (vec_ref[4:5, :] + vec_ref[5:6, :])

    bias = vec_ref[pl.ds(8 + j, 1), :]

    def front(r):
        return dot(low_ref[block * r : block * (r + 1), :], up_ref[...]) + bias

    def middle(r, value):
        rows = slice(block * r, block * (r + 1))
        phi, density = gelu_parts(value)
        hidden = (value * phi).astype(BF16)
        hid_ref[rows, :] = hidden
        slope_ref[rows, :] = (phi + value * density).astype(BF16)
        return hidden

    def finish(r, hidden):
        acc_ref[block * r : block * (r + 1), :] += dot(hidden, down_ref[...])

    staggered(ROW // block, front, middle, finish)

    @pl.when(j == CHUNKS - 1)
    def _():
        for r in range(ROW // block):
            rows = slice(block * r, block * (r + 1))
            hat, inverse = normalized(acc_ref[rows, :])
            hat2_ref[rows, :] = hat.astype(BF16)
            inv2_ref[rows, :] = inverse
            full = hat * vec_ref[6:7, :] + vec_ref[7:8, :]
            out_ref[rows, :] = full.astype(BF16)
            acc_ref[rows, :] = full
        picked = [acc_ref[pl.ds(cls_ref[d], 1), :] for d in range(DOCS)]
        emb_ref[...] = jnp.concatenate(picked, axis=0).astype(BF16)


def feed_forward(cls, low, hat, pack, vectors):
    fixed = lambda j, c: (0, 0)
    return pl.pallas_call(
        forward_kernel,
        out_shape=(
            jax.ShapeDtypeStruct((ROW, FF), BF16),
            jax.ShapeDtypeStruct((ROW, FF), BF16),
            jax.ShapeDtypeStruct((ROW, D), BF16),
            jax.ShapeDtypeStruct((ROW, 1), F32),
            jax.ShapeDtypeStruct((ROW, D), BF16),
            jax.ShapeDtypeStruct((DOCS, D), BF16),
        ),
        grid_spec=pltpu.PrefetchScalarGridSpec(
            num_scalar_prefetch=1,
            grid=(CHUNKS,),
            in_specs=[
                pl.BlockSpec((ROW, D), fixed),
                pl.BlockSpec((ROW, D), fixed),
                pl.BlockSpec((D, D), lambda j, c: (0, j)),
                pl.BlockSpec((D, D), lambda j, c: (0, CHUNKS + j)),
                pl.BlockSpec((16, D), fixed),
            ],
            out_specs=[
                pl.BlockSpec((ROW, D), lambda j, c: (0, j)),
                pl.BlockSpec((ROW, D), lambda j, c: (0, j)),
                pl.BlockSpec((ROW, D), fixed),
                pl.BlockSpec((ROW, 1), fixed),
                pl.BlockSpec((ROW, D), fixed),
                pl.BlockSpec((DOCS, D), fixed),
            ],
            scratch_shapes=[pltpu.VMEM((ROW, D), F32)],
        ),
        compiler_params=pltpu.CompilerParams(vmem_limit_bytes=VMEM_LIMIT),
        name="feed_forward",
    )(cls, low, hat, pack, pack, vectors)


def feed_back_kernel(
    cls_ref, core_ref, cot_ref, eg_ref, hat2_ref, inv2_ref, hat_ref, inv_ref, low_ref, hid_ref, slope_ref, up_ref, down_ref,
    vec_ref, mine_ref, other_ref, one_ref, one_low_ref, grads_ref, two_low_ref,
):
    j = pl.program_id(0)
    block = 256
    count = ROW // block
    piece = lambda r: slice(block * r, block * (r + 1))

    @pl.when(j == 0)
    def _():
        grads_ref[...] = jnp.zeros_like(grads_ref)
        one_ref[...] = cot_ref[...].astype(F32)
        for d in range(DOCS):
            one_ref[pl.ds(cls_ref[d], 1), :] += eg_ref[d : d + 1, :]
        for r in range(count):
            rows = piece(r)
            grad, hat = one_ref[rows, :], hat2_ref[rows, :].astype(F32)
            grads_ref[6:7, :] += jnp.sum(grad * hat, axis=0, keepdims=True)
            grads_ref[7:8, :] += jnp.sum(grad, axis=0, keepdims=True)
            two = normalized_back(grad, hat, inv2_ref[rows, :], vec_ref[6:7, :])
            one_ref[rows, :] = two
            two_low = two.astype(BF16)
            two_low_ref[rows, :] = two_low
            grads_ref[5:6, :] += jnp.sum(two_low.astype(F32), axis=0, keepdims=True)

    grad_up = []

    def front(r):
        return dot_nt(two_low_ref[piece(r), :], down_ref[...])

    def middle(r, grad_hidden):
        part = (grad_hidden * slope_ref[piece(r), :].astype(F32)).astype(BF16)
        grads_ref[pl.ds(8 + j, 1), :] += jnp.sum(part.astype(F32), axis=0, keepdims=True)
        grad_up.append(part)
        return part

    def finish(r, part):
        one_ref[piece(r), :] += dot_nt(part, up_ref[...])

    staggered(count, front, middle, finish)
    down_grad = dot_tn(hid_ref[...], two_low_ref[...]).astype(BF16)
    up_grad = dot_tn(low_ref[...], jnp.concatenate(grad_up, axis=0)).astype(BF16)

    @pl.when(core_ref[0] == 0)
    def _():
        mine_ref[...] = up_grad
        other_ref[...] = down_grad

    @pl.when(core_ref[0] == 1)
    def _():
        mine_ref[...] = down_grad
        other_ref[...] = up_grad

    @pl.when(j == CHUNKS - 1)
    def _():
        for r in range(count):
            rows = piece(r)
            grad, hat = one_ref[rows, :], hat_ref[rows, :].astype(F32)
            grads_ref[3:4, :] += jnp.sum(grad * hat, axis=0, keepdims=True)
            grads_ref[4:5, :] += jnp.sum(grad, axis=0, keepdims=True)
            one = normalized_back(grad, hat, inv_ref[rows, :], vec_ref[3:4, :])
            one_ref[rows, :] = one
            one_low = one.astype(BF16)
            one_low_ref[rows, :] = one_low
            grads_ref[2:3, :] += jnp.sum(one_low.astype(F32), axis=0, keepdims=True)


def feed_back(cls, core, cotangent, embedding_grad, hat2, inv2, hat, inv, low, hidden, slope, pack, vectors):
    fixed = lambda j, c, h: (0, 0)
    whole = lambda rows, cols: pl.BlockSpec((rows, cols), fixed)
    chunk = lambda rows, first=0: pl.BlockSpec((rows, D), lambda j, c, h: (0, first + j))
    width = FF + D // 2
    return pl.pallas_call(
        feed_back_kernel,
        out_shape=(
            jax.ShapeDtypeStruct((D, width), BF16),
            jax.ShapeDtypeStruct((D, width), BF16),
            jax.ShapeDtypeStruct((ROW, D), F32),
            jax.ShapeDtypeStruct((ROW, D), BF16),
            jax.ShapeDtypeStruct((16, D), F32),
        ),
        grid_spec=pltpu.PrefetchScalarGridSpec(
            num_scalar_prefetch=2,
            grid=(CHUNKS,),
            in_specs=[
                whole(ROW, D),
                whole(DOCS, D),
                whole(ROW, D),
                whole(ROW, 1),
                whole(ROW, D),
                whole(ROW, 1),
                whole(ROW, D),
                chunk(ROW),
                chunk(ROW),
                chunk(D),
                chunk(D, CHUNKS),
                whole(16, D),
            ],
            out_specs=[chunk(D), chunk(D), whole(ROW, D), whole(ROW, D), whole(16, D)],
            scratch_shapes=[pltpu.VMEM((ROW, D), BF16)],
        ),
        compiler_params=pltpu.CompilerParams(vmem_limit_bytes=FEED_LIMIT),
        name="feed_back",
    )(cls, core.reshape(1), cotangent, embedding_grad, hat2, inv2, hat, inv, low, hidden, slope, pack, pack, vectors)


def out_back_kernel(core_ref, one_low_ref, out_w_ref, att_ref, *refs):
    mine_ref, other_ref, datt_ref = refs[-3:]
    datt_ref[...] = dot_nt(one_low_ref[...], out_w_ref[...]).astype(BF16)
    grad = dot_tn(att_ref[...], one_low_ref[...]).astype(BF16)

    @pl.when(core_ref[0] == 0)
    def _():
        mine_ref[...] = grad[:, : D // 2]
        other_ref[...] = grad[:, D // 2 :]

    @pl.when(core_ref[0] == 1)
    def _():
        mine_ref[...] = grad[:, D // 2 :]
        other_ref[...] = grad[:, : D // 2]


def out_back(core, one_low, out_w, attended, mine, other):
    whole = lambda rows, cols: pl.BlockSpec((rows, cols), lambda i, h: (0, 0))
    last = pl.BlockSpec((D, D // 2), lambda i, h: (0, 2 * CHUNKS))
    return pl.pallas_call(
        out_back_kernel,
        out_shape=(
            jax.ShapeDtypeStruct(mine.shape, BF16),
            jax.ShapeDtypeStruct(other.shape, BF16),
            jax.ShapeDtypeStruct((ROW, D), BF16),
        ),
        grid_spec=pltpu.PrefetchScalarGridSpec(
            num_scalar_prefetch=1,
            grid=(1,),
            in_specs=[whole(ROW, D), whole(D, D), whole(ROW, D), ANY, ANY],
            out_specs=[last, last, whole(ROW, D)],
        ),
        input_output_aliases={4: 0, 5: 1},
        compiler_params=pltpu.CompilerParams(vmem_limit_bytes=VMEM_LIMIT),
        name="out_back",
    )(core.reshape(1), one_low, out_w, attended, mine, other)


def contrast(embeddings, everyone, flags, positives):
    docs_dev, docs_all = embeddings.shape[0], everyone.shape[0]
    begin = lax.axis_index(AXES) * docs_dev
    scale = 2.0 * D ** (-0.5)
    scores = dot_nt(everyone, everyone) * scale
    passage = flags == 0
    masked = jnp.where(passage[None, :], scores, -1000000000.0)
    maxima = jnp.max(masked, axis=1)
    log_sums = maxima + jnp.log(jnp.sum(jnp.exp(masked - maxima[:, None]), axis=1))
    hit_mask = jnp.arange(docs_all, dtype=jnp.int32)[None, :] == positives[:, None]
    picked = jnp.sum(jnp.where(hit_mask, scores, 0.0), axis=1)
    query_rows = flags.astype(F32)
    loss = jnp.sum(query_rows * (log_sums - picked)) / (docs_all // 2)
    chances = jnp.where(passage[None, :], jnp.exp(scores - log_sums[:, None]), 0.0)
    pairs = (query_rows[:, None] * scale * (chances - hit_mask.astype(F32))).astype(BF16)
    own_rows = lax.dynamic_slice_in_dim(pairs, begin, docs_dev, axis=0)
    own_cols = lax.dynamic_slice_in_dim(pairs, begin, docs_dev, axis=1)
    grad = dot(own_rows, everyone) + dot_tn(own_cols, everyone)
    return lax.dynamic_slice_in_dim(scores, begin, docs_dev, axis=0), loss, grad


def body(
    inputs,
    cotangent,
    segment_ids,
    cls_positions,
    doc_flags,
    positives,
    query_weight,
    query_bias,
    key_weight,
    value_weight,
    value_bias,
    out_weight,
    out_bias,
    first_gain,
    first_shift,
    up_weight,
    up_bias,
    down_weight,
    down_bias,
    second_gain,
    second_shift,
):
    rows = query_weight.shape[0]
    size = lax.axis_size(AXES)
    core = lax.axis_index(AXES) & 1

    up_sorted = up_weight.reshape(rows, D, CHUNKS).transpose(0, 2, 1).reshape(rows, FF)
    pack = jnp.concatenate([up_sorted, down_weight.reshape(rows, CHUNKS * D)], axis=1)
    pack = lax.all_gather(pack, AXES, axis=0, tiled=True)

    small = jnp.stack(
        [query_bias, value_bias, out_bias, first_gain, first_shift, down_bias, second_gain, second_shift], axis=1
    )
    small = jnp.concatenate([small, up_bias.reshape(rows, CHUNKS)], axis=1)
    small = jnp.pad(small, ((0, 0), (0, 4)))
    digits = jnp.concatenate([positives // 128, positives % 128]).astype(BF16)
    digits = jnp.pad(digits[None, :], ((0, rows - 1), (0, 128 - 16 - digits.shape[0])))
    half = D // 2
    small = lax.optimization_barrier(jnp.concatenate([small, digits], axis=1))

    def two_ways(left, right):
        return jnp.where(core == 0, left, right), jnp.where(core == 0, right, left)

    keep, give = two_ways(
        jnp.concatenate([query_weight, key_weight[:, :half], out_weight[:, :half]], axis=1),
        jnp.concatenate([key_weight[:, half:], value_weight, out_weight[:, half:]], axis=1),
    )
    keep = jnp.concatenate([keep, small], axis=1)
    give = jnp.concatenate([give, small], axis=1)
    both = place([keep[None], swap(give, 1)[None]], core).reshape(2 * rows, -1)
    near = gather_halves(both, D)
    far = swap(near, 1)

    tail = near[:, 2 * D :]
    vectors = tail[:, :16].astype(F32).T
    docs_dev = positives.shape[0]
    digits = tail.reshape(size, rows, 128)[:, 0, 16 : 16 + 2 * docs_dev].astype(jnp.int32)
    chosen = (digits[:, :docs_dev] * 128 + digits[:, docs_dev:]).reshape(-1)

    zero = jnp.zeros((D,), F32)
    offset = jnp.concatenate([vectors[0], zero, vectors[1]])[None]
    factor = jnp.concatenate([jnp.full((D,), 0.125, F32), jnp.ones((2 * D,), F32)])[None]
    qkv = project(inputs, near, offset, factor, core, None)
    qkv = project(inputs, far, offset, factor, 1 - core, qkv)

    attended, log_total = attend(cls_positions, qkv)
    out_w = jnp.concatenate(two_ways(near[:, HALF : 2 * D], far[:, HALF : 2 * D]), axis=1)
    hat, inv, low = first_norm(attended, out_w, inputs, vectors, [])
    hidden, slope, hat2, inv2, layer_output, embeddings = feed_forward(cls_positions, low, hat, pack, vectors)

    everyone = gather_rows(embeddings)
    scores, loss, embedding_grad = contrast(embeddings, everyone, doc_flags, chosen)

    mine, other, grad_one, one_low, grads = feed_back(
        cls_positions, core, cotangent, embedding_grad, hat2, inv2, hat, inv, low, hidden, slope, pack, vectors
    )
    mine, other, grad_attended = out_back(core, one_low, out_w, attended, mine, other)
    early = Scatter(mine, other, [(0, 13 * 128, down_order), (13 * 128, 27 * 128, up_order)])
    parts = attend_back(cls_positions, qkv, grad_attended, log_total, GROUPS[0], (), [])
    sent = early.step(parts[:1])
    parts = attend_back(cls_positions, qkv, grad_attended, log_total, GROUPS[1], parts, sent)
    mine, other = weights_back(inputs, *parts, grads, core)
    sent = early.step([mine, other])
    late = Scatter(mine, after(other, sent), [(0, HALF + 128, pair_order)])
    sent = late.step(sent)
    input_grad = inputs_back(grad_one, *parts, near, far, core, sent)
    sent = early.step([input_grad])
    sent = late.step(sent)
    early.step(sent)
    keep, got, give = early.last()
    late_keep, late_got, _ = late.last()
    shard_up, shard_down, shard_out, shard_query, shard_key, shard_value, *small = final_parts(
        core, keep, got, late_keep, late_got
    )
    query_b, value_b, out_b, gain_one, shift_one, down_b, gain_two, shift_two, up_b = [row.reshape(-1) for row in small]
    return (
        layer_output,
        embeddings,
        scores,
        loss,
        embedding_grad,
        input_grad,
        shard_query,
        query_b,
        shard_key,
        shard_value,
        value_b,
        shard_out,
        out_b,
        gain_one,
        shift_one,
        shard_up,
        up_b,
        shard_down,
        down_b,
        gain_two,
        shift_two,
    )


def solution(mesh):
    split = P(AXES, None)
    vector = P(AXES)
    in_specs = (
        split, split, vector, vector, P(), vector, split, vector, split, split, vector,
        split, vector, vector, vector, split, vector, split, vector, vector, vector,
    )
    out_specs = (
        split, split, split, P(), split, split, split, vector, split, split, vector,
        split, vector, vector, vector, split, vector, split, vector, vector, vector,
    )
    return jax.shard_map(body, mesh=mesh, in_specs=in_specs, out_specs=out_specs, check_vma=False)
```

```python
from functools import partial

import jax
import jax.numpy as jnp
from jax import lax
from jax.experimental import pallas as pl
from jax.experimental.pallas import tpu as pltpu
from jax.sharding import PartitionSpec as P

D = 768
HEADS = 12
HEAD = 64
FF = 3072
ROW = 1024
DOCS = 8
EPSILON = 1e-12
AXES = ("dp", "fsdp")
PAIR = 2 * HEAD
PAIRS = HEADS // 2
QBLOCK = 128
WINDOWS = (256, 384, 512, 1024)
SUB = 1
GROUPS = ((0, 768),)
CHUNKS = FF // D
F32 = jnp.float32
BF16 = jnp.bfloat16
VMEM_LIMIT = 46 * 1024 * 1024
FEED_LIMIT = 46 * 1024 * 1024
HALF = 3 * D // 2
ANY = pl.BlockSpec(memory_space=pl.ANY)


def dot(left, right):
    return jnp.dot(left, right, preferred_element_type=F32)


def dot_tn(left, right):
    return lax.dot_general(left, right, (((0,), (0,)), ((), ())), preferred_element_type=F32)


def dot_nt(left, right):
    return lax.dot_general(left, right, (((1,), (1,)), ((), ())), preferred_element_type=F32)


def stages_of(size):
    bits = size.bit_length() - 1
    return [(low, min(2, bits - low)) for low in range(1, bits, 2)]


def swap(block, mask):
    size = lax.axis_size(AXES)
    return lax.ppermute(block, AXES, [(i, i ^ mask) for i in range(size)])


def place(pieces, own):
    lead, rows, cols = pieces[0].shape
    out = jnp.zeros((lead, len(pieces), rows, cols), pieces[0].dtype)
    for m, piece in enumerate(pieces):
        out = lax.dynamic_update_slice_in_dim(out, piece[:, None], own ^ m, axis=1)
    return out


def gather_chips(block):
    rows, cols = block.shape
    index = lax.axis_index(AXES)
    block = block[None]
    for low, width in reversed(stages_of(lax.axis_size(AXES))):
        pieces = [block] + [swap(block, m << low) for m in range(1, 1 << width)]
        own = (index >> low) & ((1 << width) - 1)
        block = place(pieces, own).reshape(-1, rows, cols)
    return block.reshape(-1, cols)


def gather_halves(block, cut):
    rows, cols = block.shape
    index = lax.axis_index(AXES)
    block = block[None]
    for low, width in reversed(stages_of(lax.axis_size(AXES))[1:]):
        pieces = [block] + [swap(block, m << low) for m in range(1, 1 << width)]
        block = place(pieces, (index >> low) & ((1 << width) - 1)).reshape(-1, rows, cols)
    own_one, own_two = (index >> 1) & 1, (index >> 2) & 1
    left, right = block[:, :, :cut], block[:, :, cut:]
    left = place([left, swap(left, 4)], own_two)
    right = place([right, swap(right, 2)], own_one)
    left, left_far, right, right_far = left[:, :, None], swap(left, 2)[:, :, None], right[:, None], swap(right, 4)[:, None]
    out = jnp.zeros((block.shape[0], 2, 2, rows, cols), block.dtype)
    out = lax.dynamic_update_slice(out, left, (0, 0, own_one, 0, 0))
    out = lax.dynamic_update_slice(out, left_far, (0, 0, 1 - own_one, 0, 0))
    out = lax.dynamic_update_slice(out, right, (0, own_two, 0, 0, cut))
    out = lax.dynamic_update_slice(out, right_far, (0, 1 - own_two, 0, 0, cut))
    return out.reshape(-1, cols)


def gather_rows(block):
    rows, cols = block.shape
    core = lax.axis_index(AXES) & 1
    both = place([block[None], swap(block, 1)[None]], core)
    return gather_chips(both.reshape(2 * rows, cols))


def added(pieces):
    total = pieces[0].astype(F32)
    for piece in pieces[1:]:
        total = total + piece.astype(F32)
    return total


def after(value, deps):
    return lax.optimization_barrier((value, *deps))[0] if deps else value


class Scatter:
    def __init__(self, mine, other, parts, extra=None):
        size = lax.axis_size(AXES)
        self.rows = 2 * mine.shape[0] // size
        self.bits = list(range(size.bit_length() - 2, 0, -1))
        self.extra = extra
        got = swap(other, 1)
        self.parts = []
        for begin, end, order in parts:
            run = [end - begin, [self.whole(piece, begin) for piece in (mine, got)]]
            self.parts.append([[run], list(self.bits), order(self.bits)])

    def whole(self, piece, begin):
        return piece.reshape([2] * len(self.bits) + [self.rows, piece.shape[1]]), self.bits, begin

    def cut(self, part, group, m, deps):
        index = lax.axis_index(AXES)
        runs, open_bits, _ = part
        sums = []
        for width, held in runs:
            total = None
            for i, (piece, bits, begin) in enumerate(held):
                piece = after(piece, deps) if i == 0 else piece
                left = [b in open_bits and b not in group for b in bits]
                starts = [0 if free else ((index ^ m) >> b) & 1 for b, free in zip(bits, left)] + [0, begin]
                sizes = [2 if free else 1 for free in left] + [self.rows, width]
                shape = [2] * sum(left) + [self.rows, width]
                piece = lax.dynamic_slice(piece, starts, sizes).reshape(shape).astype(F32)
                total = piece if total is None else total + piece
            sums.append(total)
        return sums[0] if len(sums) == 1 else jnp.concatenate(sums, axis=-1)

    def step(self, deps=()):
        sums = []
        for n, part in enumerate(self.parts):
            if self.extra is not None and n == len(self.parts) - 1:
                mine, other = self.extra
                got = swap(after(other, sums), 1)
                part[0].append([mine.shape[1], [self.whole(piece, 0) for piece in (mine, got)]])
                self.extra = None
            group = part[2].pop(0)
            masks = [0]
            for b in group:
                masks += [m | (1 << b) for m in masks]
            sent = [self.cut(part, group, m, deps).astype(BF16) for m in masks[1:]]
            part[1] = [b for b in part[1] if b not in group]
            for m, piece in zip(masks[1:], sent):
                piece, begin = swap(piece, m), 0
                for run in part[0]:
                    run[1].append((piece, list(part[1]), begin))
                    begin += run[0]
            sums += sent
        return sums

    def last(self, deps=()):
        while self.parts[0][2]:
            self.step()
        totals = [self.cut(part, [], 0, deps) for part in self.parts]
        total = jnp.concatenate(totals, axis=1).reshape(2, self.rows // 2, -1)
        core = lax.axis_index(AXES) & 1
        keep = lax.dynamic_index_in_dim(total, core, 0, False)
        give = lax.dynamic_index_in_dim(total, 1 - core, 0, False).astype(BF16)
        return keep, swap(give, 1), give


def down_order(bits):
    pairs = [bits[max(i - 1, 0) : i + 1] for i in range(len(bits) - 1, -1, -2)]
    return [[b] for pair in pairs for b in pair]


def up_order(bits):
    pairs = [bits[max(i - 1, 0) : i + 1] for i in range(len(bits) - 1, -1, -2)]
    return [[b] for pair in pairs for b in reversed(pair)]


def pair_order(bits):
    return [bits[max(i - 1, 0) : i + 1] for i in range(len(bits) - 1, -1, -2)]


def project_kernel(half_ref, x_ref, w_ref, offset_ref, factor_ref, *refs):
    out_ref = refs[-1]
    value = dot(x_ref[...], w_ref[...])
    out_ref[...] = ((value + offset_ref[...]) * factor_ref[...]).astype(BF16)


def project(inputs, weights, offset, factor, half, before):
    block = 256
    extra = [] if before is None else [before]
    return pl.pallas_call(
        project_kernel,
        out_shape=jax.ShapeDtypeStruct((ROW, 3 * D), BF16),
        grid_spec=pltpu.PrefetchScalarGridSpec(
            num_scalar_prefetch=1,
            grid=(ROW // block,),
            in_specs=[
                pl.BlockSpec((block, D), lambda i, h: (i, 0)),
                pl.BlockSpec((D, HALF), lambda i, h: (0, 0)),
                pl.BlockSpec((1, HALF), lambda i, h: (0, h[0])),
                pl.BlockSpec((1, HALF), lambda i, h: (0, h[0])),
            ]
            + [ANY] * len(extra),
            out_specs=pl.BlockSpec((block, HALF), lambda i, h: (i, h[0])),
        ),
        input_output_aliases={} if before is None else {5: 0},
        compiler_params=pltpu.CompilerParams(vmem_limit_bytes=VMEM_LIMIT),
        name="project",
    )(half.reshape(1), inputs, weights, offset, factor, *extra)


def weights_kernel(core_ref, x_ref, q_ref, k_ref, v_ref, grads_ref, mine_ref, other_ref):
    half = D // 2
    inputs = x_ref[...]

    def table_of(values):
        total = jnp.sum(values.astype(F32), axis=0, keepdims=True)
        return jnp.concatenate([total, grads_ref[1:16, :], jnp.zeros((112, D), F32)], axis=0).T.astype(BF16)

    def fill(low_ref, high_ref):
        low_ref[:, :D] = dot_tn(inputs, q_ref[...]).astype(BF16)
        high_ref[:, half:HALF] = dot_tn(inputs, v_ref[...]).astype(BF16)
        keys = dot_tn(inputs, k_ref[...]).astype(BF16)
        low_ref[:, D:HALF] = keys[:, :half]
        high_ref[:, :half] = keys[:, half:]
        low_ref[:, HALF:] = table_of(q_ref[...])
        high_ref[:, HALF:] = table_of(v_ref[...])

    @pl.when(core_ref[0] == 0)
    def _():
        fill(mine_ref, other_ref)

    @pl.when(core_ref[0] == 1)
    def _():
        fill(other_ref, mine_ref)


def weights_back(inputs, dq, dk, dv, grads, core):
    whole = lambda rows, cols: pl.BlockSpec((rows, cols), lambda i, h: (0, 0))
    shape = jax.ShapeDtypeStruct((D, HALF + 128), BF16)
    return pl.pallas_call(
        weights_kernel,
        out_shape=(shape, shape),
        grid_spec=pltpu.PrefetchScalarGridSpec(
            num_scalar_prefetch=1,
            grid=(1,),
            in_specs=[whole(ROW, D)] * 4 + [whole(16, D)],
            out_specs=[whole(D, HALF + 128)] * 2,
        ),
        compiler_params=pltpu.CompilerParams(vmem_limit_bytes=VMEM_LIMIT),
        name="weights_back",
    )(core.reshape(1), inputs, dq, dk, dv, grads)


def thirds(values, axis):
    terms = []
    for _ in range(3):
        terms.append(values.astype(BF16))
        values = values - terms[-1].astype(F32)
    return jnp.concatenate(terms, axis=axis)


def ones_at(rows, cols, rule):
    shape = (rows, cols)
    row, col = lax.broadcasted_iota(jnp.int32, shape, 0), lax.broadcasted_iota(jnp.int32, shape, 1)
    return rule(row, col).astype(F32).astype(BF16)


def final_kernel(core_ref, early_keep, early_got, late_keep, late_got, *outs):
    up_ref, down_ref, out_ref, q_ref, k_ref, v_ref, *vectors, hidden_ref = outs
    half = D // 2
    rows = q_ref.shape[0]
    group = CHUNKS * 128

    def fill(early_first, early_second, first, second):
        weave = ones_at(group, group, lambda r, c: c == (r % 128) * CHUNKS + r // 128)
        pieces = []
        for g in range(FF // group):
            parts = [early_first[:, D * j + 128 * g : D * j + 128 * (g + 1)].astype(F32) for j in range(CHUNKS)]
            pieces.append(thirds(jnp.concatenate(parts, axis=1), 0))
        woven = dot(jnp.concatenate(pieces, axis=0), weave)
        for g in range(FF // group):
            total = None
            for i in range(3):
                piece = woven[rows * (3 * g + i) : rows * (3 * g + i + 1)]
                total = piece if total is None else total + piece
            up_ref[:, group * g : group * (g + 1)] = total
        for j in range(CHUNKS):
            spread = ones_at(rows * CHUNKS, rows, lambda r, c, j=j: r == c * CHUNKS + j)
            spread = jnp.concatenate([spread] * 3, axis=1)
            piece = dot(spread, thirds(early_second[:, D * j : D * (j + 1)].astype(F32), 0))
            down_ref[...] = piece if j == 0 else down_ref[...] + piece
        out_ref[:, :half] = early_first[:, FF:].astype(F32)
        out_ref[:, half:] = early_second[:, FF:].astype(F32)
        q_ref[...] = first[:, :D].astype(F32)
        k_ref[:, :half] = first[:, D:HALF].astype(F32)
        k_ref[:, half:] = second[:, :half].astype(F32)
        v_ref[...] = second[:, half:HALF].astype(F32)
        same = ones_at(rows, rows, lambda r, c: r == c)
        same = jnp.concatenate([same] * 3, axis=0)
        low = dot_tn(thirds(first[:, HALF:].astype(F32), 0), same)
        high = dot_tn(thirds(second[:, HALF:].astype(F32), 0), same)
        table = [low[0:1], high[0:1]] + [low[i : i + 1] for i in range(2, 8)]
        for ref, row in zip(vectors, table):
            ref[...] = row
        total = None
        for j in range(CHUNKS):
            spread = ones_at(rows, rows * CHUNKS, lambda r, c, j=j: c == r * CHUNKS + j)
            spread = jnp.concatenate([spread] * 3, axis=0)
            piece = dot(thirds(low[8 + j : 9 + j], 1), spread)
            total = piece if total is None else total + piece
        hidden_ref[...] = total

    @pl.when(core_ref[0] == 0)
    def _():
        fill(early_keep, early_got, late_keep, late_got)

    @pl.when(core_ref[0] == 1)
    def _():
        fill(early_got, early_keep, late_got, late_keep)


def final_parts(core, early_keep, early_got, late_keep, late_got):
    rows = late_keep.shape[0]
    shapes = [(rows, FF), (rows * CHUNKS, D)] + [(rows, D)] * 4 + [(1, rows)] * 8 + [(1, rows * CHUNKS)]
    whole = lambda shape: pl.BlockSpec(shape, lambda i, h: (0, 0))
    arrays = (early_keep, early_got, late_keep, late_got)
    return pl.pallas_call(
        final_kernel,
        out_shape=[jax.ShapeDtypeStruct(shape, F32) for shape in shapes],
        grid_spec=pltpu.PrefetchScalarGridSpec(
            num_scalar_prefetch=1,
            grid=(1,),
            in_specs=[whole(array.shape) for array in arrays],
            out_specs=[whole(shape) for shape in shapes],
        ),
        compiler_params=pltpu.CompilerParams(vmem_limit_bytes=VMEM_LIMIT),
        name="final_parts",
    )(core.reshape(1), *arrays)


def inputs_kernel(core_ref, one_ref, q_ref, k_ref, v_ref, mine_ref, other_ref, *refs):
    out_ref = refs[-1]

    def fill(low_ref, high_ref):
        half = D // 2
        total = one_ref[...] + dot_nt(q_ref[...], low_ref[:, :D]) + dot_nt(v_ref[...], high_ref[:, half:HALF])
        total = total + dot_nt(k_ref[:, :half], low_ref[:, D:HALF]) + dot_nt(k_ref[:, half:], high_ref[:, :half])
        out_ref[...] = total

    @pl.when(core_ref[0] == 0)
    def _():
        fill(mine_ref, other_ref)

    @pl.when(core_ref[0] == 1)
    def _():
        fill(other_ref, mine_ref)


def inputs_back(grad_one, dq, dk, dv, mine, other, core, before):
    block = 256
    rows = pl.BlockSpec((block, D), lambda i, h: (i, 0))
    weights = pl.BlockSpec((D, HALF), lambda i, h: (0, 0))
    return pl.pallas_call(
        inputs_kernel,
        out_shape=jax.ShapeDtypeStruct((ROW, D), F32),
        grid_spec=pltpu.PrefetchScalarGridSpec(
            num_scalar_prefetch=1,
            grid=(ROW // block,),
            in_specs=[rows, rows, rows, rows, weights, weights] + [ANY] * len(before),
            out_specs=rows,
        ),
        compiler_params=pltpu.CompilerParams(vmem_limit_bytes=VMEM_LIMIT),
        name="inputs_back",
    )(core.reshape(1), grad_one, dq, dk, dv, mine, other, *before)


def row_bounds(cls_ref, places):
    first = jnp.zeros_like(places)
    end = jnp.full_like(places, ROW)
    for d in range(1, DOCS):
        first = jnp.where(places >= cls_ref[d], cls_ref[d], first)
    for d in range(DOCS - 1, 0, -1):
        end = jnp.where(places < cls_ref[d], cls_ref[d], end)
    return first, end


def scalar_bounds(cls_ref, low, high):
    first, end = jnp.int32(0), jnp.int32(ROW)
    for d in range(1, DOCS):
        first = jnp.where(low >= cls_ref[d], cls_ref[d], first)
    for d in range(DOCS - 1, 0, -1):
        end = jnp.where(high < cls_ref[d], cls_ref[d], end)
    return first, end


def over_windows(cls_ref, begin, step):
    low, high = scalar_bounds(cls_ref, begin, begin + QBLOCK - 1)
    low = (low // 16) * 16
    before = None
    for width in WINDOWS:
        start = pl.multiple_of(jnp.minimum(low, ROW - width), 16)
        fits = high <= start + width
        take = fits if before is None else jnp.logical_and(fits, jnp.logical_not(before))
        before = fits if before is None else jnp.logical_or(fits, before)
        pl.when(take)(partial(step, start, width))


def staggered(count, front, middle, finish):
    state = front(0)
    for p in range(count):
        later = front(p + 1) if p + 1 < count else None
        finish(p, middle(p, state))
        state = later


def split_pair(block):
    lane = lax.broadcasted_iota(jnp.int32, block.shape, 1)
    zero = jnp.zeros_like(block)
    return jnp.concatenate(
        [jnp.where(lane < HEAD, block, zero), jnp.where(lane < HEAD, zero, block)], axis=0
    )


def join_pair(both):
    half = both.shape[0] // 2
    lane = lax.broadcasted_iota(jnp.int32, (half, both.shape[1]), 1)
    return jnp.where(lane < HEAD, both[:half], both[half:])


def attend_kernel(cls_ref, q_ref, k_ref, v_ref, out_ref, log_ref):
    @pl.loop(0, SUB)
    def _(s):
        begin = (pl.program_id(0) * SUB + s) * QBLOCK
        rows = pl.ds(pl.multiple_of(s * QBLOCK, QBLOCK), QBLOCK)

        def step(start, width):
            places = begin + lax.broadcasted_iota(jnp.int32, (QBLOCK, 1), 0)
            first, end = row_bounds(cls_ref, places)
            keys = start + lax.broadcasted_iota(jnp.int32, (QBLOCK, width), 1)
            mask = jnp.logical_and(keys >= first, keys < end)
            mask = jnp.concatenate([mask, mask], axis=0)
            lane = lax.broadcasted_iota(jnp.int32, (QBLOCK, 128), 1)
            logs = [jnp.zeros((QBLOCK, 128), F32)]
            window = pl.ds(start, width)

            def front(p):
                cols = slice(PAIR * p, PAIR * (p + 1))
                return dot_nt(split_pair(q_ref[rows, cols]), k_ref[window, cols])

            def middle(p, scores):
                scores = jnp.where(mask, scores, -1000000000.0)
                top = jnp.max(scores, axis=1, keepdims=True)
                weights = jnp.exp(scores - top)
                return top, jnp.sum(weights, axis=1, keepdims=True), weights.astype(BF16)

            def finish(p, state):
                top, total, weights = state
                cols = slice(PAIR * p, PAIR * (p + 1))
                result = dot(weights, v_ref[window, cols]) / total
                out_ref[rows, cols] = join_pair(result).astype(BF16)
                log_total = top + jnp.log(total)
                table = jnp.where(lane == 2 * p, log_total[:QBLOCK], logs[0])
                logs[0] = jnp.where(lane == 2 * p + 1, log_total[QBLOCK:], table)

            staggered(PAIRS, front, middle, finish)
            log_ref[:, rows] = logs[0].T[:16]

        over_windows(cls_ref, begin, step)


def attend(cls, qkv):
    block = SUB * QBLOCK
    return pl.pallas_call(
        attend_kernel,
        out_shape=(
            jax.ShapeDtypeStruct((ROW, D), BF16),
            jax.ShapeDtypeStruct((16, ROW), F32),
        ),
        grid_spec=pltpu.PrefetchScalarGridSpec(
            num_scalar_prefetch=1,
            grid=(ROW // block,),
            in_specs=[
                pl.BlockSpec((block, D), lambda i, c: (i, 0)),
                pl.BlockSpec((ROW, D), lambda i, c: (0, 1)),
                pl.BlockSpec((ROW, D), lambda i, c: (0, 2)),
            ],
            out_specs=[
                pl.BlockSpec((block, D), lambda i, c: (i, 0)),
                pl.BlockSpec((16, block), lambda i, c: (0, i)),
            ],
        ),
        compiler_params=pltpu.CompilerParams(vmem_limit_bytes=VMEM_LIMIT),
        name="attend",
    )(cls, qkv, qkv, qkv)


def attend_back_kernel(base, cls_ref, q_ref, k_ref, v_ref, do_ref, log_ref, *refs):
    dq_ref, dk_ref, dv_ref, dk_sum, dv_sum = refs[-5:]

    @pl.when(pl.program_id(0) == 0)
    def _():
        dk_sum[...] = jnp.zeros_like(dk_sum)
        dv_sum[...] = jnp.zeros_like(dv_sum)

    @pl.loop(0, SUB)
    def _(s):
        begin = (pl.program_id(0) * SUB + s) * QBLOCK
        rows = pl.ds(pl.multiple_of(s * QBLOCK, QBLOCK), QBLOCK)

        def step(start, width):
            places = begin + lax.broadcasted_iota(jnp.int32, (1, QBLOCK), 1)
            first, end = row_bounds(cls_ref, places)
            keys = start + lax.broadcasted_iota(jnp.int32, (width, QBLOCK), 0)
            mask = jnp.logical_and(keys >= first, keys < end)
            mask = jnp.concatenate([mask, mask], axis=1)
            window = pl.ds(start, width)

            def front(p):
                cols = slice(PAIR * p, PAIR * (p + 1))
                queries = split_pair(q_ref[rows, cols])
                grads = split_pair(do_ref[rows, cols])
                return queries, grads, dot_nt(k_ref[window, cols], queries), dot_nt(v_ref[window, cols], grads)

            def middle(p, state):
                queries, grads, scores, grad_weights = state
                h = base + 2 * p
                log_total = jnp.concatenate([log_ref[h : h + 1, rows], log_ref[h + 1 : h + 2, rows]], axis=1)
                weights = jnp.exp(jnp.where(mask, scores - log_total, -1000000000.0))
                inner = jnp.sum(grad_weights * weights, axis=0, keepdims=True)
                grad_scores = (weights * (grad_weights - inner)).astype(BF16)
                return queries, grads, weights.astype(BF16), grad_scores

            def finish(p, state):
                cols = slice(PAIR * p, PAIR * (p + 1))
                queries, grads, weights, grad_scores = state
                dv_sum[window, cols] += dot(weights, grads)
                dk_sum[window, cols] += dot(grad_scores, queries)
                grad_queries = join_pair(dot_tn(grad_scores, k_ref[window, cols]))
                dq_ref[rows, cols] = (grad_queries.astype(BF16).astype(F32) * 0.125).astype(BF16)

            staggered(dq_ref.shape[1] // PAIR, front, middle, finish)

        over_windows(cls_ref, begin, step)

    @pl.when(pl.program_id(0) == pl.num_programs(0) - 1)
    def _():
        dk_ref[...] = dk_sum[...].astype(BF16)
        dv_ref[...] = dv_sum[...].astype(BF16)


def attend_back(cls, qkv, grad_attended, log_total, group, earlier, before):
    block = SUB * QBLOCK
    begin, span = group
    wide = span if D % span == 0 else D
    across, place = D // wide, begin // wide
    shape = jax.ShapeDtypeStruct((ROW, D), BF16)
    extra = list(earlier) + list(before)
    return pl.pallas_call(
        partial(attend_back_kernel, begin // HEAD),
        out_shape=(shape, shape, shape),
        grid_spec=pltpu.PrefetchScalarGridSpec(
            num_scalar_prefetch=1,
            grid=(ROW // block,),
            in_specs=[
                pl.BlockSpec((block, wide), lambda i, c: (i, place)),
                pl.BlockSpec((ROW, wide), lambda i, c: (0, across + place)),
                pl.BlockSpec((ROW, wide), lambda i, c: (0, 2 * across + place)),
                pl.BlockSpec((block, wide), lambda i, c: (i, place)),
                pl.BlockSpec((16, block), lambda i, c: (0, i)),
            ]
            + [ANY] * len(extra),
            out_specs=[
                pl.BlockSpec((block, span), lambda i, c: (i, begin // span)),
                pl.BlockSpec((ROW, span), lambda i, c: (0, begin // span)),
                pl.BlockSpec((ROW, span), lambda i, c: (0, begin // span)),
            ],
            scratch_shapes=[pltpu.VMEM((ROW, span), F32), pltpu.VMEM((ROW, span), F32)],
        ),
        input_output_aliases={6 + i: i for i in range(len(earlier))},
        compiler_params=pltpu.CompilerParams(vmem_limit_bytes=VMEM_LIMIT),
        name="attend_back",
    )(cls, qkv, qkv, qkv, grad_attended, log_total, *extra)


def normalized(values):
    centre = jnp.mean(values, axis=-1, keepdims=True)
    centred = values - centre
    spread = jnp.mean(centred * centred, axis=-1, keepdims=True)
    inverse = lax.rsqrt(spread + EPSILON)
    return centred * inverse, inverse


def normalized_back(grad, hat, inverse, gain):
    scaled = grad * gain
    mean_scaled = jnp.mean(scaled, axis=-1, keepdims=True)
    mean_hat = jnp.mean(scaled * hat, axis=-1, keepdims=True)
    return inverse * (scaled - mean_scaled - hat * mean_hat)


def first_kernel(att_ref, w_ref, x_ref, vec_ref, *refs):
    hat_ref, inv_ref, low_ref = refs[-3:]
    residual = x_ref[...].astype(F32) + dot(att_ref[...], w_ref[...]) + vec_ref[2:3, :]
    hat, inverse = normalized(residual)
    hat_ref[...] = hat.astype(BF16)
    inv_ref[...] = inverse
    low_ref[...] = (hat * vec_ref[3:4, :] + vec_ref[4:5, :]).astype(BF16)


def first_norm(attended, weights, inputs, vectors, before):
    block = 256
    rows = lambda i: (i, 0)
    fixed = lambda i: (0, 0)
    return pl.pallas_call(
        first_kernel,
        out_shape=(
            jax.ShapeDtypeStruct((ROW, D), BF16),
            jax.ShapeDtypeStruct((ROW, 1), F32),
            jax.ShapeDtypeStruct((ROW, D), BF16),
        ),
        grid=(ROW // block,),
        in_specs=[
            pl.BlockSpec((block, D), rows),
            pl.BlockSpec((D, D), fixed),
            pl.BlockSpec((block, D), rows),
            pl.BlockSpec((16, D), fixed),
        ]
        + [ANY] * len(before),
        out_specs=[
            pl.BlockSpec((block, D), rows),
            pl.BlockSpec((block, 1), rows),
            pl.BlockSpec((block, D), rows),
        ],
        compiler_params=pltpu.CompilerParams(vmem_limit_bytes=VMEM_LIMIT),
        name="first_norm",
    )(attended, weights, inputs, vectors, *before)


def gelu_parts(v):
    bell = jnp.exp2(v * v * -0.7213475204444817)
    t = 1.0 / (1.0 + (0.3275911 * 0.7071067811865476) * jnp.abs(v))
    poly = t * (0.127414796 + t * (-0.142248368 + t * (0.7107068705 + t * (-0.7265760135 + t * 0.5307027145))))
    tail = poly * bell
    return jnp.where(v >= 0.0, 1.0 - tail, tail), 0.3989422804014327 * bell


def forward_kernel(
    cls_ref, low_ref, hat_ref, up_ref, down_ref, vec_ref, hid_ref, slope_ref, hat2_ref, inv2_ref, out_ref, emb_ref, acc_ref
):
    j = pl.program_id(0)
    block = 256

    @pl.when(j == 0)
    def _():
        acc_ref[...] = hat_ref[...].astype(F32) * vec_ref[3:4, :] + (vec_ref[4:5, :] + vec_ref[5:6, :])

    bias = vec_ref[pl.ds(8 + j, 1), :]

    def front(r):
        return dot(low_ref[block * r : block * (r + 1), :], up_ref[...]) + bias

    def middle(r, value):
        rows = slice(block * r, block * (r + 1))
        phi, density = gelu_parts(value)
        hidden = (value * phi).astype(BF16)
        hid_ref[rows, :] = hidden
        slope_ref[rows, :] = (phi + value * density).astype(BF16)
        return hidden

    def finish(r, hidden):
        acc_ref[block * r : block * (r + 1), :] += dot(hidden, down_ref[...])

    staggered(ROW // block, front, middle, finish)

    @pl.when(j == CHUNKS - 1)
    def _():
        for r in range(ROW // block):
            rows = slice(block * r, block * (r + 1))
            hat, inverse = normalized(acc_ref[rows, :])
            hat2_ref[rows, :] = hat.astype(BF16)
            inv2_ref[rows, :] = inverse
            full = hat * vec_ref[6:7, :] + vec_ref[7:8, :]
            out_ref[rows, :] = full.astype(BF16)
            acc_ref[rows, :] = full
        picked = [acc_ref[pl.ds(cls_ref[d], 1), :] for d in range(DOCS)]
        emb_ref[...] = jnp.concatenate(picked, axis=0).astype(BF16)


def feed_forward(cls, low, hat, pack, vectors):
    fixed = lambda j, c: (0, 0)
    return pl.pallas_call(
        forward_kernel,
        out_shape=(
            jax.ShapeDtypeStruct((ROW, FF), BF16),
            jax.ShapeDtypeStruct((ROW, FF), BF16),
            jax.ShapeDtypeStruct((ROW, D), BF16),
            jax.ShapeDtypeStruct((ROW, 1), F32),
            jax.ShapeDtypeStruct((ROW, D), BF16),
            jax.ShapeDtypeStruct((DOCS, D), BF16),
        ),
        grid_spec=pltpu.PrefetchScalarGridSpec(
            num_scalar_prefetch=1,
            grid=(CHUNKS,),
            in_specs=[
                pl.BlockSpec((ROW, D), fixed),
                pl.BlockSpec((ROW, D), fixed),
                pl.BlockSpec((D, D), lambda j, c: (0, j)),
                pl.BlockSpec((D, D), lambda j, c: (0, CHUNKS + j)),
                pl.BlockSpec((16, D), fixed),
            ],
            out_specs=[
                pl.BlockSpec((ROW, D), lambda j, c: (0, j)),
                pl.BlockSpec((ROW, D), lambda j, c: (0, j)),
                pl.BlockSpec((ROW, D), fixed),
                pl.BlockSpec((ROW, 1), fixed),
                pl.BlockSpec((ROW, D), fixed),
                pl.BlockSpec((DOCS, D), fixed),
            ],
            scratch_shapes=[pltpu.VMEM((ROW, D), F32)],
        ),
        compiler_params=pltpu.CompilerParams(vmem_limit_bytes=VMEM_LIMIT),
        name="feed_forward",
    )(cls, low, hat, pack, pack, vectors)


def feed_back_kernel(
    cls_ref, core_ref, cot_ref, eg_ref, hat2_ref, inv2_ref, hat_ref, inv_ref, low_ref, hid_ref, slope_ref, up_ref, down_ref,
    vec_ref, mine_ref, other_ref, one_ref, one_low_ref, grads_ref, two_low_ref,
):
    j = pl.program_id(0)
    block = 256
    count = ROW // block
    piece = lambda r: slice(block * r, block * (r + 1))

    @pl.when(j == 0)
    def _():
        grads_ref[...] = jnp.zeros_like(grads_ref)
        one_ref[...] = cot_ref[...].astype(F32)
        for d in range(DOCS):
            one_ref[pl.ds(cls_ref[d], 1), :] += eg_ref[d : d + 1, :]
        for r in range(count):
            rows = piece(r)
            grad, hat = one_ref[rows, :], hat2_ref[rows, :].astype(F32)
            grads_ref[6:7, :] += jnp.sum(grad * hat, axis=0, keepdims=True)
            grads_ref[7:8, :] += jnp.sum(grad, axis=0, keepdims=True)
            two = normalized_back(grad, hat, inv2_ref[rows, :], vec_ref[6:7, :])
            one_ref[rows, :] = two
            two_low = two.astype(BF16)
            two_low_ref[rows, :] = two_low
            grads_ref[5:6, :] += jnp.sum(two_low.astype(F32), axis=0, keepdims=True)

    grad_up = []

    def front(r):
        return dot_nt(two_low_ref[piece(r), :], down_ref[...])

    def middle(r, grad_hidden):
        part = (grad_hidden * slope_ref[piece(r), :].astype(F32)).astype(BF16)
        grads_ref[pl.ds(8 + j, 1), :] += jnp.sum(part.astype(F32), axis=0, keepdims=True)
        grad_up.append(part)
        return part

    def finish(r, part):
        one_ref[piece(r), :] += dot_nt(part, up_ref[...])

    staggered(count, front, middle, finish)
    down_grad = dot_tn(hid_ref[...], two_low_ref[...]).astype(BF16)
    up_grad = dot_tn(low_ref[...], jnp.concatenate(grad_up, axis=0)).astype(BF16)

    @pl.when(core_ref[0] == 0)
    def _():
        mine_ref[...] = up_grad
        other_ref[...] = down_grad

    @pl.when(core_ref[0] == 1)
    def _():
        mine_ref[...] = down_grad
        other_ref[...] = up_grad

    @pl.when(j == CHUNKS - 1)
    def _():
        for r in range(count):
            rows = piece(r)
            grad, hat = one_ref[rows, :], hat_ref[rows, :].astype(F32)
            grads_ref[3:4, :] += jnp.sum(grad * hat, axis=0, keepdims=True)
            grads_ref[4:5, :] += jnp.sum(grad, axis=0, keepdims=True)
            one = normalized_back(grad, hat, inv_ref[rows, :], vec_ref[3:4, :])
            one_ref[rows, :] = one
            one_low = one.astype(BF16)
            one_low_ref[rows, :] = one_low
            grads_ref[2:3, :] += jnp.sum(one_low.astype(F32), axis=0, keepdims=True)


def feed_back(cls, core, cotangent, embedding_grad, hat2, inv2, hat, inv, low, hidden, slope, pack, vectors):
    fixed = lambda j, c, h: (0, 0)
    whole = lambda rows, cols: pl.BlockSpec((rows, cols), fixed)
    chunk = lambda rows, first=0: pl.BlockSpec((rows, D), lambda j, c, h: (0, first + j))
    return pl.pallas_call(
        feed_back_kernel,
        out_shape=(
            jax.ShapeDtypeStruct((D, FF), BF16),
            jax.ShapeDtypeStruct((D, FF), BF16),
            jax.ShapeDtypeStruct((ROW, D), F32),
            jax.ShapeDtypeStruct((ROW, D), BF16),
            jax.ShapeDtypeStruct((16, D), F32),
        ),
        grid_spec=pltpu.PrefetchScalarGridSpec(
            num_scalar_prefetch=2,
            grid=(CHUNKS,),
            in_specs=[
                whole(ROW, D),
                whole(DOCS, D),
                whole(ROW, D),
                whole(ROW, 1),
                whole(ROW, D),
                whole(ROW, 1),
                whole(ROW, D),
                chunk(ROW),
                chunk(ROW),
                chunk(D),
                chunk(D, CHUNKS),
                whole(16, D),
            ],
            out_specs=[chunk(D), chunk(D), whole(ROW, D), whole(ROW, D), whole(16, D)],
            scratch_shapes=[pltpu.VMEM((ROW, D), BF16)],
        ),
        compiler_params=pltpu.CompilerParams(vmem_limit_bytes=FEED_LIMIT),
        name="feed_back",
    )(cls, core.reshape(1), cotangent, embedding_grad, hat2, inv2, hat, inv, low, hidden, slope, pack, pack, vectors)


def out_back_kernel(core_ref, one_low_ref, out_w_ref, att_ref, *refs):
    mine_ref, other_ref, datt_ref = refs[-3:]
    datt_ref[...] = dot_nt(one_low_ref[...], out_w_ref[...]).astype(BF16)
    grad = dot_tn(att_ref[...], one_low_ref[...]).astype(BF16)

    @pl.when(core_ref[0] == 0)
    def _():
        mine_ref[...] = grad[:, : D // 2]
        other_ref[...] = grad[:, D // 2 :]

    @pl.when(core_ref[0] == 1)
    def _():
        mine_ref[...] = grad[:, D // 2 :]
        other_ref[...] = grad[:, : D // 2]


def out_back(core, one_low, out_w, attended):
    whole = lambda rows, cols: pl.BlockSpec((rows, cols), lambda i, h: (0, 0))
    return pl.pallas_call(
        out_back_kernel,
        out_shape=(
            jax.ShapeDtypeStruct((D, D // 2), BF16),
            jax.ShapeDtypeStruct((D, D // 2), BF16),
            jax.ShapeDtypeStruct((ROW, D), BF16),
        ),
        grid_spec=pltpu.PrefetchScalarGridSpec(
            num_scalar_prefetch=1,
            grid=(1,),
            in_specs=[whole(ROW, D), whole(D, D), whole(ROW, D)],
            out_specs=[whole(D, D // 2), whole(D, D // 2), whole(ROW, D)],
        ),
        compiler_params=pltpu.CompilerParams(vmem_limit_bytes=VMEM_LIMIT),
        name="out_back",
    )(core.reshape(1), one_low, out_w, attended)


def contrast(embeddings, everyone, flags, positives):
    docs_dev, docs_all = embeddings.shape[0], everyone.shape[0]
    begin = lax.axis_index(AXES) * docs_dev
    scale = 2.0 * D ** (-0.5)
    scores = dot_nt(everyone, everyone) * scale
    passage = flags == 0
    masked = jnp.where(passage[None, :], scores, -1000000000.0)
    maxima = jnp.max(masked, axis=1)
    log_sums = maxima + jnp.log(jnp.sum(jnp.exp(masked - maxima[:, None]), axis=1))
    hit_mask = jnp.arange(docs_all, dtype=jnp.int32)[None, :] == positives[:, None]
    picked = jnp.sum(jnp.where(hit_mask, scores, 0.0), axis=1)
    query_rows = flags.astype(F32)
    loss = jnp.sum(query_rows * (log_sums - picked)) / (docs_all // 2)
    chances = jnp.where(passage[None, :], jnp.exp(scores - log_sums[:, None]), 0.0)
    pairs = (query_rows[:, None] * scale * (chances - hit_mask.astype(F32))).astype(BF16)
    own_rows = lax.dynamic_slice_in_dim(pairs, begin, docs_dev, axis=0)
    own_cols = lax.dynamic_slice_in_dim(pairs, begin, docs_dev, axis=1)
    grad = dot(own_rows, everyone) + dot_tn(own_cols, everyone)
    return lax.dynamic_slice_in_dim(scores, begin, docs_dev, axis=0), loss, grad


def body(
    inputs,
    cotangent,
    segment_ids,
    cls_positions,
    doc_flags,
    positives,
    query_weight,
    query_bias,
    key_weight,
    value_weight,
    value_bias,
    out_weight,
    out_bias,
    first_gain,
    first_shift,
    up_weight,
    up_bias,
    down_weight,
    down_bias,
    second_gain,
    second_shift,
):
    rows = query_weight.shape[0]
    size = lax.axis_size(AXES)
    core = lax.axis_index(AXES) & 1

    up_sorted = up_weight.reshape(rows, D, CHUNKS).transpose(0, 2, 1).reshape(rows, FF)
    pack = jnp.concatenate([up_sorted, down_weight.reshape(rows, CHUNKS * D)], axis=1)
    pack = lax.all_gather(pack, AXES, axis=0, tiled=True)

    small = jnp.stack(
        [query_bias, value_bias, out_bias, first_gain, first_shift, down_bias, second_gain, second_shift], axis=1
    )
    small = jnp.concatenate([small, up_bias.reshape(rows, CHUNKS)], axis=1)
    small = jnp.pad(small, ((0, 0), (0, 4)))
    digits = jnp.concatenate([positives // 128, positives % 128]).astype(BF16)
    digits = jnp.pad(digits[None, :], ((0, rows - 1), (0, 128 - 16 - digits.shape[0])))
    half = D // 2
    small = lax.optimization_barrier(jnp.concatenate([small, digits], axis=1))

    def two_ways(left, right):
        return jnp.where(core == 0, left, right), jnp.where(core == 0, right, left)

    keep, give = two_ways(
        jnp.concatenate([query_weight, key_weight[:, :half], out_weight[:, :half]], axis=1),
        jnp.concatenate([key_weight[:, half:], value_weight, out_weight[:, half:]], axis=1),
    )
    keep = jnp.concatenate([keep, small], axis=1)
    give = jnp.concatenate([give, small], axis=1)
    both = place([keep[None], swap(give, 1)[None]], core).reshape(2 * rows, -1)
    near = gather_halves(both, D)
    far = swap(near, 1)

    tail = near[:, 2 * D :]
    vectors = tail[:, :16].astype(F32).T
    docs_dev = positives.shape[0]
    digits = tail.reshape(size, rows, 128)[:, 0, 16 : 16 + 2 * docs_dev].astype(jnp.int32)
    chosen = (digits[:, :docs_dev] * 128 + digits[:, docs_dev:]).reshape(-1)

    zero = jnp.zeros((D,), F32)
    offset = jnp.concatenate([vectors[0], zero, vectors[1]])[None]
    factor = jnp.concatenate([jnp.full((D,), 0.125, F32), jnp.ones((2 * D,), F32)])[None]
    qkv = project(inputs, near, offset, factor, core, None)
    qkv = project(inputs, far, offset, factor, 1 - core, qkv)

    attended, log_total = attend(cls_positions, qkv)
    out_w = jnp.concatenate(two_ways(near[:, HALF : 2 * D], far[:, HALF : 2 * D]), axis=1)
    hat, inv, low = first_norm(attended, out_w, inputs, vectors, [])
    hidden, slope, hat2, inv2, layer_output, embeddings = feed_forward(cls_positions, low, hat, pack, vectors)

    everyone = gather_rows(embeddings)
    scores, loss, embedding_grad = contrast(embeddings, everyone, doc_flags, chosen)

    mine, other, grad_one, one_low, grads = feed_back(
        cls_positions, core, cotangent, embedding_grad, hat2, inv2, hat, inv, low, hidden, slope, pack, vectors
    )
    wide = 14 * 128
    ffn_mine, ffn_other = mine, other
    mine, other, grad_attended = out_back(core, one_low, out_w, attended)
    early = Scatter(ffn_mine, ffn_other, [(0, wide, up_order), (wide, FF, down_order)], (mine, other))
    sent = early.step([grad_attended])
    parts = attend_back(cls_positions, qkv, grad_attended, log_total, GROUPS[0], (), sent)
    mine, other = weights_back(inputs, *parts, grads, core)
    sent = early.step([mine, other])
    late = Scatter(mine, after(other, sent), [(0, HALF + 128, pair_order)])
    sent = late.step(sent)
    input_grad = inputs_back(grad_one, *parts, near, far, core, sent)
    early.step(sent)
    sent = early.step([input_grad])
    sent = late.step(sent)
    keep, got, give = early.last()
    late_keep, late_got, _ = late.last()
    shard_up, shard_down, shard_out, shard_query, shard_key, shard_value, *small = final_parts(
        core, keep, got, late_keep, late_got
    )
    query_b, value_b, out_b, gain_one, shift_one, down_b, gain_two, shift_two, up_b = [row.reshape(-1) for row in small]
    return (
        layer_output,
        embeddings,
        scores,
        loss,
        embedding_grad,
        input_grad,
        shard_query,
        query_b,
        shard_key,
        shard_value,
        value_b,
        shard_out,
        out_b,
        gain_one,
        shift_one,
        shard_up,
        up_b,
        shard_down,
        down_b,
        gain_two,
        shift_two,
    )


def solution(mesh):
    split = P(AXES, None)
    vector = P(AXES)
    in_specs = (
        split, split, vector, vector, P(), vector, split, vector, split, split, vector,
        split, vector, vector, vector, split, vector, split, vector, vector, vector,
    )
    out_specs = (
        split, split, split, P(), split, split, split, vector, split, split, vector,
        split, vector, vector, vector, split, vector, split, vector, vector, vector,
    )
    return jax.shard_map(body, mesh=mesh, in_specs=in_specs, out_specs=out_specs, check_vma=False)
```

```python
from functools import partial

import jax
import jax.numpy as jnp
from jax import lax
from jax.experimental import pallas as pl
from jax.experimental.pallas import tpu as pltpu
from jax.sharding import PartitionSpec as P

D = 768
HEADS = 12
HEAD = 64
FF = 3072
ROW = 1024
DOCS = 8
EPSILON = 1e-12
AXES = ("dp", "fsdp")
PAIR = 2 * HEAD
PAIRS = HEADS // 2
QBLOCK = 128
WINDOWS = (256, 384, 512, 1024)
SUB = 1
GROUPS = ((0, 768),)
CHUNKS = FF // D
F32 = jnp.float32
BF16 = jnp.bfloat16
VMEM_LIMIT = 46 * 1024 * 1024
FEED_LIMIT = 46 * 1024 * 1024
HALF = 3 * D // 2
ANY = pl.BlockSpec(memory_space=pl.ANY)


def dot(left, right):
    return jnp.dot(left, right, preferred_element_type=F32)


def dot_tn(left, right):
    return lax.dot_general(left, right, (((0,), (0,)), ((), ())), preferred_element_type=F32)


def dot_nt(left, right):
    return lax.dot_general(left, right, (((1,), (1,)), ((), ())), preferred_element_type=F32)


def stages_of(size):
    bits = size.bit_length() - 1
    return [(low, min(2, bits - low)) for low in range(1, bits, 2)]


def swap(block, mask):
    size = lax.axis_size(AXES)
    return lax.ppermute(block, AXES, [(i, i ^ mask) for i in range(size)])


def place(pieces, own):
    lead, rows, cols = pieces[0].shape
    out = jnp.zeros((lead, len(pieces), rows, cols), pieces[0].dtype)
    for m, piece in enumerate(pieces):
        out = lax.dynamic_update_slice_in_dim(out, piece[:, None], own ^ m, axis=1)
    return out


def gather_chips(block):
    rows, cols = block.shape
    index = lax.axis_index(AXES)
    block = block[None]
    for low, width in reversed(stages_of(lax.axis_size(AXES))):
        pieces = [block] + [swap(block, m << low) for m in range(1, 1 << width)]
        own = (index >> low) & ((1 << width) - 1)
        block = place(pieces, own).reshape(-1, rows, cols)
    return block.reshape(-1, cols)


def gather_halves(block, cut):
    rows, cols = block.shape
    index = lax.axis_index(AXES)
    left, right = block[None, :, :cut], block[None, :, cut:]

    def outer(piece, bit):
        lead, height, width = piece.shape
        return place([piece, swap(piece, 1 << bit)], (index >> bit) & 1).reshape(lead, 2 * height, width)

    def inner(piece, bit):
        piece = piece.reshape(-1, rows, piece.shape[-1])
        return place([piece, swap(piece, 1 << bit)], (index >> bit) & 1).reshape(-1, rows, piece.shape[-1])

    for low, width in reversed(stages_of(lax.axis_size(AXES))[1:]):
        if width == 1:
            left, right = inner(left, low), inner(right, low)
        else:
            left, right = inner(left, low), inner(right, low + 1)
            left = outer(left.reshape(-1, 2 * rows, cut), low + 1).reshape(-1, rows, cut)
            right = inner(right, low)
    own_one, own_two = (index >> 1) & 1, (index >> 2) & 1
    left = place([left, swap(left, 4)], own_two)
    right = place([right, swap(right, 2)], own_one)
    left, left_far, right, right_far = left[:, :, None], swap(left, 2)[:, :, None], right[:, None], swap(right, 4)[:, None]
    out = jnp.zeros((left.shape[0], 2, 2, rows, cols), block.dtype)
    out = lax.dynamic_update_slice(out, left, (0, 0, own_one, 0, 0))
    out = lax.dynamic_update_slice(out, left_far, (0, 0, 1 - own_one, 0, 0))
    out = lax.dynamic_update_slice(out, right, (0, own_two, 0, 0, cut))
    out = lax.dynamic_update_slice(out, right_far, (0, 1 - own_two, 0, 0, cut))
    return out.reshape(-1, cols)


def gather_rows(block):
    rows, cols = block.shape
    core = lax.axis_index(AXES) & 1
    both = place([block[None], swap(block, 1)[None]], core)
    return gather_chips(both.reshape(2 * rows, cols))


def added(pieces):
    total = pieces[0].astype(F32)
    for piece in pieces[1:]:
        total = total + piece.astype(F32)
    return total


def after(value, deps):
    return lax.optimization_barrier((value, *deps))[0] if deps else value


class Scatter:
    def __init__(self, mine, other, parts, extra=None):
        size = lax.axis_size(AXES)
        self.rows = 2 * mine.shape[0] // size
        self.bits = list(range(size.bit_length() - 2, 0, -1))
        self.extra = extra
        got = swap(other, 1)
        self.parts = []
        for begin, end, order in parts:
            run = [end - begin, [self.whole(piece, begin) for piece in (mine, got)]]
            self.parts.append([[run], list(self.bits), order(self.bits)])

    def whole(self, piece, begin):
        return piece.reshape([2] * len(self.bits) + [self.rows, piece.shape[1]]), self.bits, begin

    def cut(self, part, group, m, deps):
        index = lax.axis_index(AXES)
        runs, open_bits, _ = part
        sums = []
        for width, held in runs:
            total = None
            for i, (piece, bits, begin) in enumerate(held):
                piece = after(piece, deps) if i == 0 else piece
                left = [b in open_bits and b not in group for b in bits]
                starts = [0 if free else ((index ^ m) >> b) & 1 for b, free in zip(bits, left)] + [0, begin]
                sizes = [2 if free else 1 for free in left] + [self.rows, width]
                shape = [2] * sum(left) + [self.rows, width]
                piece = lax.dynamic_slice(piece, starts, sizes).reshape(shape).astype(F32)
                total = piece if total is None else total + piece
            sums.append(total)
        return sums[0] if len(sums) == 1 else jnp.concatenate(sums, axis=-1)

    def step(self, deps=()):
        sums = []
        for n, part in enumerate(self.parts):
            if self.extra is not None and n == len(self.parts) - 1:
                mine, other = self.extra
                got = swap(after(other, sums), 1)
                part[0].append([mine.shape[1], [self.whole(piece, 0) for piece in (mine, got)]])
                self.extra = None
            group = part[2].pop(0)
            masks = [0]
            for b in group:
                masks += [m | (1 << b) for m in masks]
            sent = [self.cut(part, group, m, deps).astype(BF16) for m in masks[1:]]
            part[1] = [b for b in part[1] if b not in group]
            for m, piece in zip(masks[1:], sent):
                piece, begin = swap(piece, m), 0
                for run in part[0]:
                    run[1].append((piece, list(part[1]), begin))
                    begin += run[0]
            sums += sent
        return sums

    def last(self, deps=()):
        while self.parts[0][2]:
            self.step()
        totals = [self.cut(part, [], 0, deps) for part in self.parts]
        total = jnp.concatenate(totals, axis=1).reshape(2, self.rows // 2, -1)
        core = lax.axis_index(AXES) & 1
        keep = lax.dynamic_index_in_dim(total, core, 0, False)
        give = lax.dynamic_index_in_dim(total, 1 - core, 0, False).astype(BF16)
        return keep, swap(give, 1), give


def down_order(bits):
    pairs = [bits[max(i - 1, 0) : i + 1] for i in range(len(bits) - 1, -1, -2)]
    return [[b] for pair in pairs for b in pair]


def up_order(bits):
    pairs = [bits[max(i - 1, 0) : i + 1] for i in range(len(bits) - 1, -1, -2)]
    return [[b] for pair in pairs for b in reversed(pair)]


def pair_order(bits):
    return [bits[max(i - 1, 0) : i + 1] for i in range(len(bits) - 1, -1, -2)]


def project_kernel(half_ref, x_ref, w_ref, offset_ref, factor_ref, *refs):
    out_ref = refs[-1]
    value = dot(x_ref[...], w_ref[...])
    out_ref[...] = ((value + offset_ref[...]) * factor_ref[...]).astype(BF16)


def project(inputs, weights, offset, factor, half, before):
    block = 256
    extra = [] if before is None else [before]
    return pl.pallas_call(
        project_kernel,
        out_shape=jax.ShapeDtypeStruct((ROW, 3 * D), BF16),
        grid_spec=pltpu.PrefetchScalarGridSpec(
            num_scalar_prefetch=1,
            grid=(ROW // block,),
            in_specs=[
                pl.BlockSpec((block, D), lambda i, h: (i, 0)),
                pl.BlockSpec((D, HALF), lambda i, h: (0, 0)),
                pl.BlockSpec((1, HALF), lambda i, h: (0, h[0])),
                pl.BlockSpec((1, HALF), lambda i, h: (0, h[0])),
            ]
            + [ANY] * len(extra),
            out_specs=pl.BlockSpec((block, HALF), lambda i, h: (i, h[0])),
        ),
        input_output_aliases={} if before is None else {5: 0},
        compiler_params=pltpu.CompilerParams(vmem_limit_bytes=VMEM_LIMIT),
        name="project",
    )(half.reshape(1), inputs, weights, offset, factor, *extra)


def weights_kernel(core_ref, x_ref, q_ref, k_ref, v_ref, grads_ref, mine_ref, other_ref):
    half = D // 2
    inputs = x_ref[...]

    def table_of(values):
        total = jnp.sum(values.astype(F32), axis=0, keepdims=True)
        return jnp.concatenate([total, grads_ref[1:16, :], jnp.zeros((112, D), F32)], axis=0).T.astype(BF16)

    def fill(low_ref, high_ref):
        low_ref[:, :D] = dot_tn(inputs, q_ref[...]).astype(BF16)
        high_ref[:, half:HALF] = dot_tn(inputs, v_ref[...]).astype(BF16)
        keys = dot_tn(inputs, k_ref[...]).astype(BF16)
        low_ref[:, D:HALF] = keys[:, :half]
        high_ref[:, :half] = keys[:, half:]
        low_ref[:, HALF:] = table_of(q_ref[...])
        high_ref[:, HALF:] = table_of(v_ref[...])

    @pl.when(core_ref[0] == 0)
    def _():
        fill(mine_ref, other_ref)

    @pl.when(core_ref[0] == 1)
    def _():
        fill(other_ref, mine_ref)


def weights_back(inputs, dq, dk, dv, grads, core):
    whole = lambda rows, cols: pl.BlockSpec((rows, cols), lambda i, h: (0, 0))
    shape = jax.ShapeDtypeStruct((D, HALF + 128), BF16)
    return pl.pallas_call(
        weights_kernel,
        out_shape=(shape, shape),
        grid_spec=pltpu.PrefetchScalarGridSpec(
            num_scalar_prefetch=1,
            grid=(1,),
            in_specs=[whole(ROW, D)] * 4 + [whole(16, D)],
            out_specs=[whole(D, HALF + 128)] * 2,
        ),
        compiler_params=pltpu.CompilerParams(vmem_limit_bytes=VMEM_LIMIT),
        name="weights_back",
    )(core.reshape(1), inputs, dq, dk, dv, grads)


def thirds(values, axis):
    terms = []
    for _ in range(3):
        terms.append(values.astype(BF16))
        values = values - terms[-1].astype(F32)
    return jnp.concatenate(terms, axis=axis)


def ones_at(rows, cols, rule):
    shape = (rows, cols)
    row, col = lax.broadcasted_iota(jnp.int32, shape, 0), lax.broadcasted_iota(jnp.int32, shape, 1)
    return rule(row, col).astype(F32).astype(BF16)


def final_kernel(core_ref, early_keep, early_got, late_keep, late_got, *outs):
    up_ref, down_ref, out_ref, q_ref, k_ref, v_ref, *vectors, hidden_ref = outs
    half = D // 2
    rows = q_ref.shape[0]
    group = CHUNKS * 128

    def fill(early_first, early_second, first, second):
        weave = ones_at(group, group, lambda r, c: c == (r % 128) * CHUNKS + r // 128)
        pieces = []
        for g in range(FF // group):
            parts = [early_first[:, D * j + 128 * g : D * j + 128 * (g + 1)].astype(F32) for j in range(CHUNKS)]
            pieces.append(thirds(jnp.concatenate(parts, axis=1), 0))
        woven = dot(jnp.concatenate(pieces, axis=0), weave)
        for g in range(FF // group):
            total = None
            for i in range(3):
                piece = woven[rows * (3 * g + i) : rows * (3 * g + i + 1)]
                total = piece if total is None else total + piece
            up_ref[:, group * g : group * (g + 1)] = total
        for j in range(CHUNKS):
            spread = ones_at(rows * CHUNKS, rows, lambda r, c, j=j: r == c * CHUNKS + j)
            spread = jnp.concatenate([spread] * 3, axis=1)
            piece = dot(spread, thirds(early_second[:, D * j : D * (j + 1)].astype(F32), 0))
            down_ref[...] = piece if j == 0 else down_ref[...] + piece
        out_ref[:, :half] = early_first[:, FF:].astype(F32)
        out_ref[:, half:] = early_second[:, FF:].astype(F32)
        q_ref[...] = first[:, :D].astype(F32)
        k_ref[:, :half] = first[:, D:HALF].astype(F32)
        k_ref[:, half:] = second[:, :half].astype(F32)
        v_ref[...] = second[:, half:HALF].astype(F32)
        same = ones_at(rows, rows, lambda r, c: r == c)
        same = jnp.concatenate([same] * 3, axis=0)
        low = dot_tn(thirds(first[:, HALF:].astype(F32), 0), same)
        high = dot_tn(thirds(second[:, HALF:].astype(F32), 0), same)
        table = [low[0:1], high[0:1]] + [low[i : i + 1] for i in range(2, 8)]
        for ref, row in zip(vectors, table):
            ref[...] = row
        total = None
        for j in range(CHUNKS):
            spread = ones_at(rows, rows * CHUNKS, lambda r, c, j=j: c == r * CHUNKS + j)
            spread = jnp.concatenate([spread] * 3, axis=0)
            piece = dot(thirds(low[8 + j : 9 + j], 1), spread)
            total = piece if total is None else total + piece
        hidden_ref[...] = total

    @pl.when(core_ref[0] == 0)
    def _():
        fill(early_keep, early_got, late_keep, late_got)

    @pl.when(core_ref[0] == 1)
    def _():
        fill(early_got, early_keep, late_got, late_keep)


def final_parts(core, early_keep, early_got, late_keep, late_got):
    rows = late_keep.shape[0]
    shapes = [(rows, FF), (rows * CHUNKS, D)] + [(rows, D)] * 4 + [(1, rows)] * 8 + [(1, rows * CHUNKS)]
    whole = lambda shape: pl.BlockSpec(shape, lambda i, h: (0, 0))
    arrays = (early_keep, early_got, late_keep, late_got)
    return pl.pallas_call(
        final_kernel,
        out_shape=[jax.ShapeDtypeStruct(shape, F32) for shape in shapes],
        grid_spec=pltpu.PrefetchScalarGridSpec(
            num_scalar_prefetch=1,
            grid=(1,),
            in_specs=[whole(array.shape) for array in arrays],
            out_specs=[whole(shape) for shape in shapes],
        ),
        compiler_params=pltpu.CompilerParams(vmem_limit_bytes=VMEM_LIMIT),
        name="final_parts",
    )(core.reshape(1), *arrays)


def inputs_kernel(core_ref, one_ref, q_ref, k_ref, v_ref, mine_ref, other_ref, *refs):
    out_ref = refs[-1]

    def fill(low_ref, high_ref):
        half = D // 2
        total = one_ref[...] + dot_nt(q_ref[...], low_ref[:, :D]) + dot_nt(v_ref[...], high_ref[:, half:HALF])
        total = total + dot_nt(k_ref[:, :half], low_ref[:, D:HALF]) + dot_nt(k_ref[:, half:], high_ref[:, :half])
        out_ref[...] = total

    @pl.when(core_ref[0] == 0)
    def _():
        fill(mine_ref, other_ref)

    @pl.when(core_ref[0] == 1)
    def _():
        fill(other_ref, mine_ref)


def inputs_back(grad_one, dq, dk, dv, mine, other, core, before):
    block = 256
    rows = pl.BlockSpec((block, D), lambda i, h: (i, 0))
    weights = pl.BlockSpec((D, HALF), lambda i, h: (0, 0))
    return pl.pallas_call(
        inputs_kernel,
        out_shape=jax.ShapeDtypeStruct((ROW, D), F32),
        grid_spec=pltpu.PrefetchScalarGridSpec(
            num_scalar_prefetch=1,
            grid=(ROW // block,),
            in_specs=[rows, rows, rows, rows, weights, weights] + [ANY] * len(before),
            out_specs=rows,
        ),
        compiler_params=pltpu.CompilerParams(vmem_limit_bytes=VMEM_LIMIT),
        name="inputs_back",
    )(core.reshape(1), grad_one, dq, dk, dv, mine, other, *before)


def row_bounds(cls_ref, places):
    first = jnp.zeros_like(places)
    end = jnp.full_like(places, ROW)
    for d in range(1, DOCS):
        first = jnp.where(places >= cls_ref[d], cls_ref[d], first)
    for d in range(DOCS - 1, 0, -1):
        end = jnp.where(places < cls_ref[d], cls_ref[d], end)
    return first, end


def scalar_bounds(cls_ref, low, high):
    first, end = jnp.int32(0), jnp.int32(ROW)
    for d in range(1, DOCS):
        first = jnp.where(low >= cls_ref[d], cls_ref[d], first)
    for d in range(DOCS - 1, 0, -1):
        end = jnp.where(high < cls_ref[d], cls_ref[d], end)
    return first, end


def over_windows(cls_ref, begin, step):
    low, high = scalar_bounds(cls_ref, begin, begin + QBLOCK - 1)
    low = (low // 16) * 16
    before = None
    for width in WINDOWS:
        start = pl.multiple_of(jnp.minimum(low, ROW - width), 16)
        fits = high <= start + width
        take = fits if before is None else jnp.logical_and(fits, jnp.logical_not(before))
        before = fits if before is None else jnp.logical_or(fits, before)
        pl.when(take)(partial(step, start, width))


def staggered(count, front, middle, finish):
    state = front(0)
    for p in range(count):
        later = front(p + 1) if p + 1 < count else None
        finish(p, middle(p, state))
        state = later


def split_pair(block):
    lane = lax.broadcasted_iota(jnp.int32, block.shape, 1)
    zero = jnp.zeros_like(block)
    return jnp.concatenate(
        [jnp.where(lane < HEAD, block, zero), jnp.where(lane < HEAD, zero, block)], axis=0
    )


def join_pair(both):
    half = both.shape[0] // 2
    lane = lax.broadcasted_iota(jnp.int32, (half, both.shape[1]), 1)
    return jnp.where(lane < HEAD, both[:half], both[half:])


def attend_kernel(cls_ref, q_ref, k_ref, v_ref, out_ref, log_ref):
    @pl.loop(0, SUB)
    def _(s):
        begin = (pl.program_id(0) * SUB + s) * QBLOCK
        rows = pl.ds(pl.multiple_of(s * QBLOCK, QBLOCK), QBLOCK)

        def step(start, width):
            places = begin + lax.broadcasted_iota(jnp.int32, (QBLOCK, 1), 0)
            first, end = row_bounds(cls_ref, places)
            keys = start + lax.broadcasted_iota(jnp.int32, (QBLOCK, width), 1)
            mask = jnp.logical_and(keys >= first, keys < end)
            mask = jnp.concatenate([mask, mask], axis=0)
            lane = lax.broadcasted_iota(jnp.int32, (QBLOCK, 128), 1)
            logs = [jnp.zeros((QBLOCK, 128), F32)]
            window = pl.ds(start, width)

            def front(p):
                cols = slice(PAIR * p, PAIR * (p + 1))
                return dot_nt(split_pair(q_ref[rows, cols]), k_ref[window, cols])

            def middle(p, scores):
                scores = jnp.where(mask, scores, -1000000000.0)
                top = jnp.max(scores, axis=1, keepdims=True)
                weights = jnp.exp(scores - top)
                return top, jnp.sum(weights, axis=1, keepdims=True), weights.astype(BF16)

            def finish(p, state):
                top, total, weights = state
                cols = slice(PAIR * p, PAIR * (p + 1))
                result = dot(weights, v_ref[window, cols]) / total
                out_ref[rows, cols] = join_pair(result).astype(BF16)
                log_total = top + jnp.log(total)
                table = jnp.where(lane == 2 * p, log_total[:QBLOCK], logs[0])
                logs[0] = jnp.where(lane == 2 * p + 1, log_total[QBLOCK:], table)

            staggered(PAIRS, front, middle, finish)
            log_ref[:, rows] = logs[0].T[:16]

        over_windows(cls_ref, begin, step)


def attend(cls, qkv):
    block = SUB * QBLOCK
    return pl.pallas_call(
        attend_kernel,
        out_shape=(
            jax.ShapeDtypeStruct((ROW, D), BF16),
            jax.ShapeDtypeStruct((16, ROW), F32),
        ),
        grid_spec=pltpu.PrefetchScalarGridSpec(
            num_scalar_prefetch=1,
            grid=(ROW // block,),
            in_specs=[
                pl.BlockSpec((block, D), lambda i, c: (i, 0)),
                pl.BlockSpec((ROW, D), lambda i, c: (0, 1)),
                pl.BlockSpec((ROW, D), lambda i, c: (0, 2)),
            ],
            out_specs=[
                pl.BlockSpec((block, D), lambda i, c: (i, 0)),
                pl.BlockSpec((16, block), lambda i, c: (0, i)),
            ],
        ),
        compiler_params=pltpu.CompilerParams(vmem_limit_bytes=VMEM_LIMIT),
        name="attend",
    )(cls, qkv, qkv, qkv)


def attend_back_kernel(base, cls_ref, q_ref, k_ref, v_ref, do_ref, log_ref, *refs):
    dq_ref, dk_ref, dv_ref, dk_sum, dv_sum = refs[-5:]

    @pl.when(pl.program_id(0) == 0)
    def _():
        dk_sum[...] = jnp.zeros_like(dk_sum)
        dv_sum[...] = jnp.zeros_like(dv_sum)

    @pl.loop(0, SUB)
    def _(s):
        begin = (pl.program_id(0) * SUB + s) * QBLOCK
        rows = pl.ds(pl.multiple_of(s * QBLOCK, QBLOCK), QBLOCK)

        def step(start, width):
            places = begin + lax.broadcasted_iota(jnp.int32, (1, QBLOCK), 1)
            first, end = row_bounds(cls_ref, places)
            keys = start + lax.broadcasted_iota(jnp.int32, (width, QBLOCK), 0)
            mask = jnp.logical_and(keys >= first, keys < end)
            mask = jnp.concatenate([mask, mask], axis=1)
            window = pl.ds(start, width)

            def front(p):
                cols = slice(PAIR * p, PAIR * (p + 1))
                queries = split_pair(q_ref[rows, cols])
                grads = split_pair(do_ref[rows, cols])
                return queries, grads, dot_nt(k_ref[window, cols], queries), dot_nt(v_ref[window, cols], grads)

            def middle(p, state):
                queries, grads, scores, grad_weights = state
                h = base + 2 * p
                log_total = jnp.concatenate([log_ref[h : h + 1, rows], log_ref[h + 1 : h + 2, rows]], axis=1)
                weights = jnp.exp(jnp.where(mask, scores - log_total, -1000000000.0))
                inner = jnp.sum(grad_weights * weights, axis=0, keepdims=True)
                grad_scores = (weights * (grad_weights - inner)).astype(BF16)
                return queries, grads, weights.astype(BF16), grad_scores

            def finish(p, state):
                cols = slice(PAIR * p, PAIR * (p + 1))
                queries, grads, weights, grad_scores = state
                dv_sum[window, cols] += dot(weights, grads)
                dk_sum[window, cols] += dot(grad_scores, queries)
                grad_queries = join_pair(dot_tn(grad_scores, k_ref[window, cols]))
                dq_ref[rows, cols] = (grad_queries.astype(BF16).astype(F32) * 0.125).astype(BF16)

            staggered(dq_ref.shape[1] // PAIR, front, middle, finish)

        over_windows(cls_ref, begin, step)

    @pl.when(pl.program_id(0) == pl.num_programs(0) - 1)
    def _():
        dk_ref[...] = dk_sum[...].astype(BF16)
        dv_ref[...] = dv_sum[...].astype(BF16)


def attend_back(cls, qkv, grad_attended, log_total, group, earlier, before):
    block = SUB * QBLOCK
    begin, span = group
    wide = span if D % span == 0 else D
    across, place = D // wide, begin // wide
    shape = jax.ShapeDtypeStruct((ROW, D), BF16)
    extra = list(earlier) + list(before)
    return pl.pallas_call(
        partial(attend_back_kernel, begin // HEAD),
        out_shape=(shape, shape, shape),
        grid_spec=pltpu.PrefetchScalarGridSpec(
            num_scalar_prefetch=1,
            grid=(ROW // block,),
            in_specs=[
                pl.BlockSpec((block, wide), lambda i, c: (i, place)),
                pl.BlockSpec((ROW, wide), lambda i, c: (0, across + place)),
                pl.BlockSpec((ROW, wide), lambda i, c: (0, 2 * across + place)),
                pl.BlockSpec((block, wide), lambda i, c: (i, place)),
                pl.BlockSpec((16, block), lambda i, c: (0, i)),
            ]
            + [ANY] * len(extra),
            out_specs=[
                pl.BlockSpec((block, span), lambda i, c: (i, begin // span)),
                pl.BlockSpec((ROW, span), lambda i, c: (0, begin // span)),
                pl.BlockSpec((ROW, span), lambda i, c: (0, begin // span)),
            ],
            scratch_shapes=[pltpu.VMEM((ROW, span), F32), pltpu.VMEM((ROW, span), F32)],
        ),
        input_output_aliases={6 + i: i for i in range(len(earlier))},
        compiler_params=pltpu.CompilerParams(vmem_limit_bytes=VMEM_LIMIT),
        name="attend_back",
    )(cls, qkv, qkv, qkv, grad_attended, log_total, *extra)


def normalized(values):
    centre = jnp.mean(values, axis=-1, keepdims=True)
    centred = values - centre
    spread = jnp.mean(centred * centred, axis=-1, keepdims=True)
    inverse = lax.rsqrt(spread + EPSILON)
    return centred * inverse, inverse


def normalized_back(grad, hat, inverse, gain):
    scaled = grad * gain
    mean_scaled = jnp.mean(scaled, axis=-1, keepdims=True)
    mean_hat = jnp.mean(scaled * hat, axis=-1, keepdims=True)
    return inverse * (scaled - mean_scaled - hat * mean_hat)


def first_kernel(att_ref, w_ref, x_ref, vec_ref, *refs):
    hat_ref, inv_ref, low_ref = refs[-3:]
    residual = x_ref[...].astype(F32) + dot(att_ref[...], w_ref[...]) + vec_ref[2:3, :]
    hat, inverse = normalized(residual)
    hat_ref[...] = hat.astype(BF16)
    inv_ref[...] = inverse
    low_ref[...] = (hat * vec_ref[3:4, :] + vec_ref[4:5, :]).astype(BF16)


def first_norm(attended, weights, inputs, vectors, before):
    block = 256
    rows = lambda i: (i, 0)
    fixed = lambda i: (0, 0)
    return pl.pallas_call(
        first_kernel,
        out_shape=(
            jax.ShapeDtypeStruct((ROW, D), BF16),
            jax.ShapeDtypeStruct((ROW, 1), F32),
            jax.ShapeDtypeStruct((ROW, D), BF16),
        ),
        grid=(ROW // block,),
        in_specs=[
            pl.BlockSpec((block, D), rows),
            pl.BlockSpec((D, D), fixed),
            pl.BlockSpec((block, D), rows),
            pl.BlockSpec((16, D), fixed),
        ]
        + [ANY] * len(before),
        out_specs=[
            pl.BlockSpec((block, D), rows),
            pl.BlockSpec((block, 1), rows),
            pl.BlockSpec((block, D), rows),
        ],
        compiler_params=pltpu.CompilerParams(vmem_limit_bytes=VMEM_LIMIT),
        name="first_norm",
    )(attended, weights, inputs, vectors, *before)


def gelu_parts(v):
    bell = jnp.exp2(v * v * -0.7213475204444817)
    t = 1.0 / (1.0 + (0.3275911 * 0.7071067811865476) * jnp.abs(v))
    poly = t * (0.127414796 + t * (-0.142248368 + t * (0.7107068705 + t * (-0.7265760135 + t * 0.5307027145))))
    tail = poly * bell
    return jnp.where(v >= 0.0, 1.0 - tail, tail), 0.3989422804014327 * bell


def forward_kernel(
    cls_ref, low_ref, hat_ref, up_ref, down_ref, vec_ref, hid_ref, slope_ref, hat2_ref, inv2_ref, out_ref, emb_ref, acc_ref
):
    j = pl.program_id(0)
    block = 256

    @pl.when(j == 0)
    def _():
        acc_ref[...] = hat_ref[...].astype(F32) * vec_ref[3:4, :] + (vec_ref[4:5, :] + vec_ref[5:6, :])

    bias = vec_ref[pl.ds(8 + j, 1), :]

    def front(r):
        return dot(low_ref[block * r : block * (r + 1), :], up_ref[...]) + bias

    def middle(r, value):
        rows = slice(block * r, block * (r + 1))
        phi, density = gelu_parts(value)
        hidden = (value * phi).astype(BF16)
        hid_ref[rows, :] = hidden
        slope_ref[rows, :] = (phi + value * density).astype(BF16)
        return hidden

    def finish(r, hidden):
        acc_ref[block * r : block * (r + 1), :] += dot(hidden, down_ref[...])

    staggered(ROW // block, front, middle, finish)

    @pl.when(j == CHUNKS - 1)
    def _():
        for r in range(ROW // block):
            rows = slice(block * r, block * (r + 1))
            hat, inverse = normalized(acc_ref[rows, :])
            hat2_ref[rows, :] = hat.astype(BF16)
            inv2_ref[rows, :] = inverse
            full = hat * vec_ref[6:7, :] + vec_ref[7:8, :]
            out_ref[rows, :] = full.astype(BF16)
            acc_ref[rows, :] = full
        picked = [acc_ref[pl.ds(cls_ref[d], 1), :] for d in range(DOCS)]
        emb_ref[...] = jnp.concatenate(picked, axis=0).astype(BF16)


def feed_forward(cls, low, hat, pack, vectors):
    fixed = lambda j, c: (0, 0)
    return pl.pallas_call(
        forward_kernel,
        out_shape=(
            jax.ShapeDtypeStruct((ROW, FF), BF16),
            jax.ShapeDtypeStruct((ROW, FF), BF16),
            jax.ShapeDtypeStruct((ROW, D), BF16),
            jax.ShapeDtypeStruct((ROW, 1), F32),
            jax.ShapeDtypeStruct((ROW, D), BF16),
            jax.ShapeDtypeStruct((DOCS, D), BF16),
        ),
        grid_spec=pltpu.PrefetchScalarGridSpec(
            num_scalar_prefetch=1,
            grid=(CHUNKS,),
            in_specs=[
                pl.BlockSpec((ROW, D), fixed),
                pl.BlockSpec((ROW, D), fixed),
                pl.BlockSpec((D, D), lambda j, c: (0, j)),
                pl.BlockSpec((D, D), lambda j, c: (0, CHUNKS + j)),
                pl.BlockSpec((16, D), fixed),
            ],
            out_specs=[
                pl.BlockSpec((ROW, D), lambda j, c: (0, j)),
                pl.BlockSpec((ROW, D), lambda j, c: (0, j)),
                pl.BlockSpec((ROW, D), fixed),
                pl.BlockSpec((ROW, 1), fixed),
                pl.BlockSpec((ROW, D), fixed),
                pl.BlockSpec((DOCS, D), fixed),
            ],
            scratch_shapes=[pltpu.VMEM((ROW, D), F32)],
        ),
        compiler_params=pltpu.CompilerParams(vmem_limit_bytes=VMEM_LIMIT),
        name="feed_forward",
    )(cls, low, hat, pack, pack, vectors)


def feed_back_kernel(
    cls_ref, core_ref, cot_ref, eg_ref, hat2_ref, inv2_ref, hat_ref, inv_ref, low_ref, hid_ref, slope_ref, up_ref, down_ref,
    vec_ref, mine_ref, other_ref, one_ref, one_low_ref, grads_ref, two_low_ref,
):
    j = pl.program_id(0)
    block = 256
    count = ROW // block
    piece = lambda r: slice(block * r, block * (r + 1))

    @pl.when(j == 0)
    def _():
        grads_ref[...] = jnp.zeros_like(grads_ref)
        one_ref[...] = cot_ref[...].astype(F32)
        for d in range(DOCS):
            one_ref[pl.ds(cls_ref[d], 1), :] += eg_ref[d : d + 1, :]
        for r in range(count):
            rows = piece(r)
            grad, hat = one_ref[rows, :], hat2_ref[rows, :].astype(F32)
            grads_ref[6:7, :] += jnp.sum(grad * hat, axis=0, keepdims=True)
            grads_ref[7:8, :] += jnp.sum(grad, axis=0, keepdims=True)
            two = normalized_back(grad, hat, inv2_ref[rows, :], vec_ref[6:7, :])
            one_ref[rows, :] = two
            two_low = two.astype(BF16)
            two_low_ref[rows, :] = two_low
            grads_ref[5:6, :] += jnp.sum(two_low.astype(F32), axis=0, keepdims=True)

    grad_up = []

    def front(r):
        return dot_nt(two_low_ref[piece(r), :], down_ref[...])

    def middle(r, grad_hidden):
        part = (grad_hidden * slope_ref[piece(r), :].astype(F32)).astype(BF16)
        grads_ref[pl.ds(8 + j, 1), :] += jnp.sum(part.astype(F32), axis=0, keepdims=True)
        grad_up.append(part)
        return part

    def finish(r, part):
        one_ref[piece(r), :] += dot_nt(part, up_ref[...])

    staggered(count, front, middle, finish)
    down_grad = dot_tn(hid_ref[...], two_low_ref[...]).astype(BF16)
    up_grad = dot_tn(low_ref[...], jnp.concatenate(grad_up, axis=0)).astype(BF16)

    @pl.when(core_ref[0] == 0)
    def _():
        mine_ref[...] = up_grad
        other_ref[...] = down_grad

    @pl.when(core_ref[0] == 1)
    def _():
        mine_ref[...] = down_grad
        other_ref[...] = up_grad

    @pl.when(j == CHUNKS - 1)
    def _():
        for r in range(count):
            rows = piece(r)
            grad, hat = one_ref[rows, :], hat_ref[rows, :].astype(F32)
            grads_ref[3:4, :] += jnp.sum(grad * hat, axis=0, keepdims=True)
            grads_ref[4:5, :] += jnp.sum(grad, axis=0, keepdims=True)
            one = normalized_back(grad, hat, inv_ref[rows, :], vec_ref[3:4, :])
            one_ref[rows, :] = one
            one_low = one.astype(BF16)
            one_low_ref[rows, :] = one_low
            grads_ref[2:3, :] += jnp.sum(one_low.astype(F32), axis=0, keepdims=True)


def feed_back(cls, core, cotangent, embedding_grad, hat2, inv2, hat, inv, low, hidden, slope, pack, vectors):
    fixed = lambda j, c, h: (0, 0)
    whole = lambda rows, cols: pl.BlockSpec((rows, cols), fixed)
    chunk = lambda rows, first=0: pl.BlockSpec((rows, D), lambda j, c, h: (0, first + j))
    return pl.pallas_call(
        feed_back_kernel,
        out_shape=(
            jax.ShapeDtypeStruct((D, FF), BF16),
            jax.ShapeDtypeStruct((D, FF), BF16),
            jax.ShapeDtypeStruct((ROW, D), F32),
            jax.ShapeDtypeStruct((ROW, D), BF16),
            jax.ShapeDtypeStruct((16, D), F32),
        ),
        grid_spec=pltpu.PrefetchScalarGridSpec(
            num_scalar_prefetch=2,
            grid=(CHUNKS,),
            in_specs=[
                whole(ROW, D),
                whole(DOCS, D),
                whole(ROW, D),
                whole(ROW, 1),
                whole(ROW, D),
                whole(ROW, 1),
                whole(ROW, D),
                chunk(ROW),
                chunk(ROW),
                chunk(D),
                chunk(D, CHUNKS),
                whole(16, D),
            ],
            out_specs=[chunk(D), chunk(D), whole(ROW, D), whole(ROW, D), whole(16, D)],
            scratch_shapes=[pltpu.VMEM((ROW, D), BF16)],
        ),
        compiler_params=pltpu.CompilerParams(vmem_limit_bytes=FEED_LIMIT),
        name="feed_back",
    )(cls, core.reshape(1), cotangent, embedding_grad, hat2, inv2, hat, inv, low, hidden, slope, pack, pack, vectors)


def out_back_kernel(core_ref, one_low_ref, out_w_ref, att_ref, *refs):
    mine_ref, other_ref, datt_ref = refs[-3:]
    datt_ref[...] = dot_nt(one_low_ref[...], out_w_ref[...]).astype(BF16)
    grad = dot_tn(att_ref[...], one_low_ref[...]).astype(BF16)

    @pl.when(core_ref[0] == 0)
    def _():
        mine_ref[...] = grad[:, : D // 2]
        other_ref[...] = grad[:, D // 2 :]

    @pl.when(core_ref[0] == 1)
    def _():
        mine_ref[...] = grad[:, D // 2 :]
        other_ref[...] = grad[:, : D // 2]


def out_back(core, one_low, out_w, attended):
    whole = lambda rows, cols: pl.BlockSpec((rows, cols), lambda i, h: (0, 0))
    return pl.pallas_call(
        out_back_kernel,
        out_shape=(
            jax.ShapeDtypeStruct((D, D // 2), BF16),
            jax.ShapeDtypeStruct((D, D // 2), BF16),
            jax.ShapeDtypeStruct((ROW, D), BF16),
        ),
        grid_spec=pltpu.PrefetchScalarGridSpec(
            num_scalar_prefetch=1,
            grid=(1,),
            in_specs=[whole(ROW, D), whole(D, D), whole(ROW, D)],
            out_specs=[whole(D, D // 2), whole(D, D // 2), whole(ROW, D)],
        ),
        compiler_params=pltpu.CompilerParams(vmem_limit_bytes=VMEM_LIMIT),
        name="out_back",
    )(core.reshape(1), one_low, out_w, attended)


def contrast(embeddings, everyone, flags, positives):
    docs_dev, docs_all = embeddings.shape[0], everyone.shape[0]
    begin = lax.axis_index(AXES) * docs_dev
    scale = 2.0 * D ** (-0.5)
    scores = dot_nt(everyone, everyone) * scale
    passage = flags == 0
    masked = jnp.where(passage[None, :], scores, -1000000000.0)
    maxima = jnp.max(masked, axis=1)
    log_sums = maxima + jnp.log(jnp.sum(jnp.exp(masked - maxima[:, None]), axis=1))
    hit_mask = jnp.arange(docs_all, dtype=jnp.int32)[None, :] == positives[:, None]
    picked = jnp.sum(jnp.where(hit_mask, scores, 0.0), axis=1)
    query_rows = flags.astype(F32)
    loss = jnp.sum(query_rows * (log_sums - picked)) / (docs_all // 2)
    chances = jnp.where(passage[None, :], jnp.exp(scores - log_sums[:, None]), 0.0)
    pairs = (query_rows[:, None] * scale * (chances - hit_mask.astype(F32))).astype(BF16)
    own_rows = lax.dynamic_slice_in_dim(pairs, begin, docs_dev, axis=0)
    own_cols = lax.dynamic_slice_in_dim(pairs, begin, docs_dev, axis=1)
    grad = dot(own_rows, everyone) + dot_tn(own_cols, everyone)
    return lax.dynamic_slice_in_dim(scores, begin, docs_dev, axis=0), loss, grad


def body(
    inputs,
    cotangent,
    segment_ids,
    cls_positions,
    doc_flags,
    positives,
    query_weight,
    query_bias,
    key_weight,
    value_weight,
    value_bias,
    out_weight,
    out_bias,
    first_gain,
    first_shift,
    up_weight,
    up_bias,
    down_weight,
    down_bias,
    second_gain,
    second_shift,
):
    rows = query_weight.shape[0]
    size = lax.axis_size(AXES)
    core = lax.axis_index(AXES) & 1

    up_sorted = up_weight.reshape(rows, D, CHUNKS).transpose(0, 2, 1).reshape(rows, FF)
    pack = jnp.concatenate([up_sorted, down_weight.reshape(rows, CHUNKS * D)], axis=1)
    pack = lax.all_gather(pack, AXES, axis=0, tiled=True)

    small = jnp.stack(
        [query_bias, value_bias, out_bias, first_gain, first_shift, down_bias, second_gain, second_shift], axis=1
    )
    small = jnp.concatenate([small, up_bias.reshape(rows, CHUNKS)], axis=1)
    small = jnp.pad(small, ((0, 0), (0, 4)))
    digits = jnp.concatenate([positives // 128, positives % 128]).astype(BF16)
    digits = jnp.pad(digits[None, :], ((0, rows - 1), (0, 128 - 16 - digits.shape[0])))
    half = D // 2
    small = lax.optimization_barrier(jnp.concatenate([small, digits], axis=1))

    def two_ways(left, right):
        return jnp.where(core == 0, left, right), jnp.where(core == 0, right, left)

    keep, give = two_ways(
        jnp.concatenate([query_weight, key_weight[:, :half], out_weight[:, :half]], axis=1),
        jnp.concatenate([key_weight[:, half:], value_weight, out_weight[:, half:]], axis=1),
    )
    keep = jnp.concatenate([keep, small], axis=1)
    give = jnp.concatenate([give, small], axis=1)
    both = place([keep[None], swap(give, 1)[None]], core).reshape(2 * rows, -1)
    near = gather_halves(both, D)
    far = swap(near, 1)

    tail = near[:, 2 * D :]
    vectors = tail[:, :16].astype(F32).T
    docs_dev = positives.shape[0]
    digits = tail.reshape(size, rows, 128)[:, 0, 16 : 16 + 2 * docs_dev].astype(jnp.int32)
    chosen = (digits[:, :docs_dev] * 128 + digits[:, docs_dev:]).reshape(-1)

    zero = jnp.zeros((D,), F32)
    offset = jnp.concatenate([vectors[0], zero, vectors[1]])[None]
    factor = jnp.concatenate([jnp.full((D,), 0.125, F32), jnp.ones((2 * D,), F32)])[None]
    qkv = project(inputs, near, offset, factor, core, None)
    qkv = project(inputs, far, offset, factor, 1 - core, qkv)

    attended, log_total = attend(cls_positions, qkv)
    out_w = jnp.concatenate(two_ways(near[:, HALF : 2 * D], far[:, HALF : 2 * D]), axis=1)
    hat, inv, low = first_norm(attended, out_w, inputs, vectors, [])
    hidden, slope, hat2, inv2, layer_output, embeddings = feed_forward(cls_positions, low, hat, pack, vectors)

    everyone = gather_rows(embeddings)
    scores, loss, embedding_grad = contrast(embeddings, everyone, doc_flags, chosen)

    mine, other, grad_one, one_low, grads = feed_back(
        cls_positions, core, cotangent, embedding_grad, hat2, inv2, hat, inv, low, hidden, slope, pack, vectors
    )
    wide = 14 * 128
    ffn_mine, ffn_other = mine, other
    mine, other, grad_attended = out_back(core, one_low, out_w, attended)
    early = Scatter(ffn_mine, ffn_other, [(0, wide, up_order), (wide, FF, down_order)], (mine, other))
    sent = early.step([grad_attended])
    parts = attend_back(cls_positions, qkv, grad_attended, log_total, GROUPS[0], (), sent)
    mine, other = weights_back(inputs, *parts, grads, core)
    sent = early.step([mine, other])
    late = Scatter(mine, after(other, sent), [(0, HALF + 128, pair_order)])
    sent = late.step(sent)
    input_grad = inputs_back(grad_one, *parts, near, far, core, sent)
    early.step(sent)
    sent = early.step([input_grad])
    sent = late.step(sent)
    keep, got, give = early.last()
    late_keep, late_got, _ = late.last()
    shard_up, shard_down, shard_out, shard_query, shard_key, shard_value, *small = final_parts(
        core, keep, got, late_keep, late_got
    )
    query_b, value_b, out_b, gain_one, shift_one, down_b, gain_two, shift_two, up_b = [row.reshape(-1) for row in small]
    return (
        layer_output,
        embeddings,
        scores,
        loss,
        embedding_grad,
        input_grad,
        shard_query,
        query_b,
        shard_key,
        shard_value,
        value_b,
        shard_out,
        out_b,
        gain_one,
        shift_one,
        shard_up,
        up_b,
        shard_down,
        down_b,
        gain_two,
        shift_two,
    )


def solution(mesh):
    split = P(AXES, None)
    vector = P(AXES)
    in_specs = (
        split, split, vector, vector, P(), vector, split, vector, split, split, vector,
        split, vector, vector, vector, split, vector, split, vector, vector, vector,
    )
    out_specs = (
        split, split, split, P(), split, split, split, vector, split, split, vector,
        split, vector, vector, vector, split, vector, split, vector, vector, vector,
    )
    return jax.shard_map(body, mesh=mesh, in_specs=in_specs, out_specs=out_specs, check_vma=False)
```
